32 devices in a mesh: var: 4 (over y, core), patch: 8 (over z, x).
Axes of the slice: x: 2, y: 2, z: 4, core: 2. Of those that a mesh axis runs over, the one named last changes fastest.
Arguments:
- pixels: bfloat16 [2, 4, 8, 128, 192], P(None, None, 'patch', None, 'var'), may hold values from -6 to 6
- targets: bfloat16 [2, 4, 8, 128, 192], P(None, 'var', 'patch'), may hold values from -6 to 6
- masks: int32 [2, 4, 8, 128, 4], P(None, 'var', 'patch'), may hold values from 0 to 1
- lengths: int32 [2, 4, 8], P(None, 'var', 'patch'), may hold values from 32 to 128, as said below
- groups: int32 [2, 4, 8], P(None, 'var', 'patch'), may hold values from 0 to 4
- latitudes: int32 [2, 4, 8, 128], P(None, 'var', 'patch'), may hold values from 0 to 63
- step_count: int32 [1], replicated, may hold values from 1 to 20
- square_master: float32 [8, 1024, 1024], P(None, 'var', 'patch')
- square_first: float32 [8, 1024, 1024], P(None, 'var', 'patch'), may hold values from -1.5258789e-05 to 1.5258789e-05
- square_second: float32 [8, 1024, 1024], P(None, 'var', 'patch'), as said below
- dense_master: float32 [2, 1024, 4096], P(None, 'var', 'patch'), may hold values from -0.1875 to 0.1875
- dense_first: float32 [2, 1024, 4096], P(None, 'var', 'patch'), may hold values from -1.5258789e-05 to 1.5258789e-05
- dense_second: float32 [2, 1024, 4096], P(None, 'var', 'patch'), as said below
- head_master: float32 [1024, 192], P('var', 'patch'), may hold values from -0.1875 to 0.1875
- head_first: float32 [1024, 192], P('var', 'patch'), may hold values from -1.5258789e-05 to 1.5258789e-05
- head_second: float32 [1024, 192], P('var', 'patch'), as said below
- table_master: float32 [376, 1024], P('var', 'patch')
- table_first: float32 [376, 1024], P('var', 'patch'), may hold values from -1.5258789e-05 to 1.5258789e-05
- table_second: float32 [376, 1024], P('var', 'patch'), as said below
Outputs:
- loss: float32 [], replicated
- grad_norm: float32 [], replicated
- square_new: float32 [8, 1024, 1024], P(None, 'var', 'patch')
- square_first_new: float32 [8, 1024, 1024], P(None, 'var', 'patch')
- square_second_new: float32 [8, 1024, 1024], P(None, 'var', 'patch')
- square_copy: bfloat16 [8, 1024, 1024], P(None, 'var', 'patch')
- dense_new: float32 [2, 1024, 4096], P(None, 'var', 'patch')
- dense_first_new: float32 [2, 1024, 4096], P(None, 'var', 'patch')
- dense_second_new: float32 [2, 1024, 4096], P(None, 'var', 'patch')
- dense_copy: bfloat16 [2, 1024, 4096], P(None, 'var', 'patch')
- head_new: float32 [1024, 192], P('var', 'patch')
- head_first_new: float32 [1024, 192], P('var', 'patch')
- head_second_new: float32 [1024, 192], P('var', 'patch')
- head_copy: bfloat16 [1024, 192], P('var', 'patch')
- table_new: float32 [376, 1024], P('var', 'patch')
- table_first_new: float32 [376, 1024], P('var', 'patch')
- table_second_new: float32 [376, 1024], P('var', 'patch')
- table_copy: bfloat16 [376, 1024], P('var', 'patch')
The draws below stay inside these ranges and needn't reach their ends.
Inputs may be any that keep to these rules, and one draw needn't show every extreme that they name: `lengths`: each item's number of used patch slots; some item has 128. `square_second`: positive. `dense_second`: positive. `head_second`: positive. `table_second`: positive.
All inputs are finite; a program needn't handle non-finite values.
Results may differ from the reference program's by a relative error of at most 0.011.
Values may be sent and summed in bfloat16 or wider, within the bound.
No kernel may reach another device: no remote copies, remote signals or barrier semaphores. Data moves between devices by JAX's collectives and lax.ppermute only.
A program may use at most 384 MiB of HBM per device.

```python
import math
import jax
import jax.numpy as jnp
from jax import lax

D = 1024
HEADS = 16
FF = 4096
V = 48
PATCH_PIXELS = 4
SOURCES = 5
LATS = 64
MB = 2
CAP = 128
HO = 192
TABLE_ROWS = 376
NPARAM = 17358848
N_VAR = 4
N_PATCH = 8


def draw_masks(key, part):
    item = jnp.arange(N_VAR)[:, None] * N_PATCH + jnp.arange(N_PATCH)[None, :]
    share = 25 + 50 * item // max(1, N_VAR * N_PATCH - 1)
    rolls = jax.random.randint(key, (MB, N_VAR, N_PATCH, CAP, PATCH_PIXELS), 0, 100)
    return (rolls < share[None, :, :, None, None]).astype(jnp.int32)


def draw_lengths(key, part):
    lowest = max(1, CAP // 4)
    rolls = jax.random.randint(key, (MB, N_VAR, N_PATCH), lowest, CAP + 1)
    rolls = rolls.at[:, 0, 0].set(CAP)
    return rolls.at[:, 1, 0].set(lowest)


def draw_square_master(key, part):
    base = jax.random.normal(key, (8, D, D), jnp.float32) * D ** (-0.5)
    factor = jnp.where(jnp.arange(8) == 7, 0.5 * CAP ** 0.5, 1.0).astype(jnp.float32)
    return base * factor[:, None, None]


def draw_table_master(key, part):
    first_key = jax.random.fold_in(key, 11)
    second_key = jax.random.fold_in(key, 12)
    base = jax.random.normal(first_key, (TABLE_ROWS, D), jnp.float32)
    gains = 1.0 + 0.1 * jax.random.uniform(second_key, (TABLE_ROWS, D), jnp.float32, -1.0, 1.0)
    index = jnp.arange(TABLE_ROWS)[:, None]
    edge = 5 * V + CAP + SOURCES
    return jnp.where(index < edge, 0.5 * base, jnp.where(index == edge, 2.0 * base, gains))


def second_moment(key, shape):
    lower = math.log(0.0001 / NPARAM)
    upper = math.log(0.0004 / NPARAM)
    return jnp.exp(jax.random.uniform(key, shape, jnp.float32, lower, upper))


def draw_square_second(key, part):
    return second_moment(key, (8, D, D))


def draw_dense_second(key, part):
    return second_moment(key, (2, D, FF))


def draw_head_second(key, part):
    return second_moment(key, (D, HO))


def draw_table_second(key, part):
    return second_moment(key, (TABLE_ROWS, D))


def touch_ends(array, own_key, least, largest):
    longest = array.shape.index(max(array.shape))
    spots = []
    for shift in (0, 1):
        where = [jax.random.randint(jax.random.fold_in(own_key, axis), (), 0, length) for axis, length in enumerate(array.shape)]
        where[longest] = (where[longest] + shift) % array.shape[longest]
        spots.append(tuple(where))
    return array.at[spots[0]].set(least).at[spots[1]].set(largest)


def steps_of(own_key, shape, cuts, least, largest):
    loudness = 1.0
    for position, shards_of in cuts:
        draws = jax.random.uniform(jax.random.fold_in(jax.random.fold_in(own_key, 6), position), (shards_of,), jnp.float32, least / len(cuts), largest / len(cuts))
        loudness = loudness * jnp.repeat(jnp.exp(draws), shape[position] // shards_of).reshape((-1,) + (1,) * (len(shape) - 1 - position))
    return loudness


def scatter_about(own_key, extent, deviation, most, pieces=(), held_as=jnp.bfloat16):
    array = jax.random.normal(own_key, extent, jnp.float32) * deviation
    if len(pieces) > 0:
        array = steps_of(own_key, extent, pieces, -0.22, 0.18) * array
    return jnp.clip(array, min=-most, max=most).astype(held_as)


def setup_inputs(seed: int = 0) -> dict:
    key_of = jax.random.split(jax.random.key(seed), 20)
    pixels = scatter_about(key_of[0], (MB, N_VAR, N_PATCH, CAP, HO), 1.0, 6.0, ((2, 8), (4, 4)))
    targets = scatter_about(key_of[1], (MB, N_VAR, N_PATCH, CAP, HO), 1.0, 6.0, ((1, 4), (2, 8)))
    masks = draw_masks(jax.random.fold_in(key_of[19], 71), 0)
    lengths = draw_lengths(jax.random.fold_in(key_of[19], 71), 0)
    groups = touch_ends(jax.random.randint(key_of[4], (MB, N_VAR, N_PATCH), 0, SOURCES), jax.random.fold_in(key_of[4], 1), 0, SOURCES - 1).astype(jnp.int32)
    latitudes = touch_ends(jax.random.randint(key_of[5], (MB, N_VAR, N_PATCH, CAP), 0, LATS), jax.random.fold_in(key_of[5], 1), 0, LATS - 1).astype(jnp.int32)
    step_count = jax.random.randint(key_of[6], (1,), 1, 21).astype(jnp.int32)
    square_master = draw_square_master(jax.random.fold_in(key_of[19], 71), 0)
    square_first = scatter_about(key_of[8], (8, D, D), (10000 * NPARAM) ** -0.5, 1.52587890625e-05, ((1, 4), (2, 8)), jnp.float32)
    square_second = draw_square_second(jax.random.fold_in(key_of[19], 71), 0)
    dense_master = scatter_about(key_of[10], (2, D, FF), D ** -0.5, 0.1875, ((1, 4), (2, 8)), jnp.float32)
    dense_first = scatter_about(key_of[11], (2, D, FF), (10000 * NPARAM) ** -0.5, 1.52587890625e-05, ((1, 4), (2, 8)), jnp.float32)
    dense_second = draw_dense_second(jax.random.fold_in(key_of[19], 71), 0)
    head_master = scatter_about(key_of[13], (D, HO), D ** -0.5, 0.1875, ((0, 4), (1, 8)), jnp.float32)
    head_first = scatter_about(key_of[14], (D, HO), (10000 * NPARAM) ** -0.5, 1.52587890625e-05, ((0, 4), (1, 8)), jnp.float32)
    head_second = draw_head_second(jax.random.fold_in(key_of[19], 71), 0)
    table_master = draw_table_master(jax.random.fold_in(key_of[19], 71), 0)
    table_first = scatter_about(key_of[17], (TABLE_ROWS, D), (10000 * NPARAM) ** -0.5, 1.52587890625e-05, ((0, 4), (1, 8)), jnp.float32)
    table_second = draw_table_second(jax.random.fold_in(key_of[19], 71), 0)
    return dict(pixels=pixels, targets=targets, masks=masks, lengths=lengths, groups=groups, latitudes=latitudes, step_count=step_count, square_master=square_master, square_first=square_first, square_second=square_second, dense_master=dense_master, dense_first=dense_first, dense_second=dense_second, head_master=head_master, head_first=head_first, head_second=head_second, table_master=table_master, table_first=table_first, table_second=table_second)


HIGH = lax.Precision.HIGHEST
CLIP_AT = 0.01
LEARN_RATE = 0.01
TABLE_RATE = 0.3
WEIGHT_DECAY = 0.1
FIRST_DECAY = 0.5
SECOND_DECAY = 0.5
EPSILON = 1e-08
NORM_EPSILON = 1e-05

@jax.custom_vjp
def low(v):
    return lax.optimization_barrier(v.astype(jnp.bfloat16)).astype(jnp.float32)

@jax.custom_vjp
def low_back(v):
    return v

def low_keep(v):
    return (low(v), None)

def low_pass(kept, grad):
    return (grad,)

def back_keep(v):
    return (v, None)

def back_low(kept, grad):
    return (low(grad),)
low.defvjp(low_keep, low_pass)
low_back.defvjp(back_keep, back_low)

def latitude_table():
    levels = jnp.arange(2 * LATS).astype(jnp.float32)
    cosine = jnp.cos(((levels + 0.5) / (2 * LATS) - 0.5) * math.pi)
    scaled = cosine / jnp.mean(cosine)
    index = 2 * jnp.arange(LATS)[:, None] + jnp.arange(PATCH_PIXELS)[None, :] // 2
    return scaled[index]

def layer_norm(value, gain):
    center = value - lax.optimization_barrier(jnp.mean(value, axis=-1, keepdims=True))
    spread = lax.optimization_barrier(jnp.mean(center * center, axis=-1, keepdims=True))
    return center * lax.rsqrt(spread + NORM_EPSILON) * gain

def item_loss(weights, kproj, pix, tgt, wpix, length, source):
    square, dense, outhead, variable_table = weights
    cap = pix.shape[0]
    size = D // HEADS
    scale = size ** (-0.5)
    base = 5 * V + cap
    patch_token_rows = variable_table[:PATCH_PIXELS * V].reshape(V, PATCH_PIXELS, D)
    variable_rows = variable_table[PATCH_PIXELS * V:5 * V]
    pos_rows = variable_table[5 * V:base]
    src_rows = variable_table[base:base + SOURCES]
    gain_one = variable_table[base + SOURCES + 1]
    gain_two = variable_table[base + SOURCES + 2]
    emb = jnp.einsum('cvk,vkd->cvd', pix.reshape(cap, V, PATCH_PIXELS), patch_token_rows, precision=HIGH)
    tok = low(low_back(emb + variable_rows[None] + pos_rows[:, None]))
    vscore = low_back(jnp.einsum('cvd,dh->cvh', tok, kproj, precision=HIGH))
    vprob = low(jax.nn.softmax(vscore, axis=1))
    vproj = low(low_back(jnp.einsum('cvd,de->cve', tok, square[2], precision=HIGH)))
    gathered = low(low_back(jnp.einsum('cvh,cvhe->che', vprob, vproj.reshape(cap, V, HEADS, size), precision=HIGH).reshape(cap, D)))
    onehot = (source == jnp.arange(SOURCES)).astype(jnp.float32)
    start = low_back(jnp.dot(gathered, square[3], precision=HIGH)) + jnp.dot(onehot, src_rows, precision=HIGH)[None, :]
    normed_one = low(layer_norm(start, gain_one))
    wqkv = jnp.concatenate([square[4], square[5], square[6]], axis=1)
    qkv = low(low_back(jnp.dot(normed_one, wqkv, precision=HIGH)))
    queries = qkv[:, :D].reshape(cap, HEADS, size)
    keys = qkv[:, D:2 * D].reshape(cap, HEADS, size)
    values = qkv[:, 2 * D:].reshape(cap, HEADS, size)
    scores = low_back(jnp.einsum('qhe,khe->hqk', queries, keys, precision=HIGH) * scale)
    keymask = jnp.arange(cap) < length
    scores = jnp.where(keymask[None, None, :], scores, -1e+30)
    probs = low(jax.nn.softmax(scores, axis=-1))
    attended = low(low_back(jnp.einsum('hqk,khe->qhe', probs, values, precision=HIGH).reshape(cap, D)))
    middle = start + low_back(jnp.dot(attended, square[7], precision=HIGH))
    normed_two = low(layer_norm(middle, gain_two))
    hidden = low_back(jnp.dot(normed_two, dense[0], precision=HIGH))
    active = low(jax.nn.gelu(hidden, approximate=False))
    final = middle + low_back(jnp.einsum('cf,df->cd', active, dense[1], precision=HIGH))
    predict = low_back(jnp.dot(low(final), outhead, precision=HIGH))
    diff = predict - tgt
    return jnp.sum(jnp.tile(wpix, (1, V)) * diff * diff)

def adam_update(master, first, second, grad, factor, steps, rate):
    clipped = grad * factor
    new_first = FIRST_DECAY * first + (1.0 - FIRST_DECAY) * clipped
    new_second = SECOND_DECAY * second + (1.0 - SECOND_DECAY) * clipped * clipped
    first_hat = new_first / (1.0 - jnp.power(FIRST_DECAY, steps))
    second_hat = new_second / (1.0 - jnp.power(SECOND_DECAY, steps))
    new_master = master - rate * (first_hat / (jnp.sqrt(second_hat) + EPSILON) + WEIGHT_DECAY * master)
    return (new_master, new_first, new_second, new_master.astype(jnp.bfloat16))

def reference(pixels, targets, masks, lengths, groups, latitudes, step_count, square_master, square_first, square_second, dense_master, dense_first, dense_second, head_master, head_first, head_second, table_master, table_first, table_second):
    items = MB * N_VAR * N_PATCH
    cap = CAP
    size = D // HEADS
    pix = pixels.astype(jnp.float32).reshape(items, cap, V * PATCH_PIXELS)
    tgt = targets.astype(jnp.float32).reshape(items, cap, V * PATCH_PIXELS)
    lens = lengths.reshape(items)
    source = groups.reshape(items)
    lat = latitudes.reshape(items, cap)
    slots = jnp.arange(cap)
    valid = masks.reshape(items, cap, PATCH_PIXELS).astype(jnp.float32) * (slots[None, :] < lens[:, None]).astype(jnp.float32)[..., None]
    wpix = latitude_table()[lat] * valid
    count = jnp.sum(valid)

    def total_loss(square, dense, outhead, variable_table):
        weights = (low(square), low(dense), low(outhead), low(variable_table))
        query = weights[3][5 * V + cap + SOURCES]
        qvec = low(jnp.dot(query, weights[0][0], precision=HIGH))
        kproj = low(jnp.einsum('dhe,he->dh', weights[0][1].reshape(D, HEADS, size), qvec.reshape(HEADS, size), precision=HIGH) * size ** (-0.5))

        def one_item(carry, data):
            return (carry + item_loss(weights, kproj, *data), None)
        total, _ = lax.scan(jax.checkpoint(one_item), jnp.zeros((), jnp.float32), (pix, tgt, wpix, lens, source))
        return total / count
    loss, back = jax.vjp(total_loss, square_master, dense_master, head_master, table_master)
    grads = back(jnp.ones((), jnp.float32))
    norm = jnp.sqrt(sum((jnp.sum(g * g) for g in grads)))
    factor = jnp.minimum(1.0, CLIP_AT / norm)
    steps = step_count[0].astype(jnp.float32)
    sq = adam_update(square_master, square_first, square_second, grads[0], factor, steps, LEARN_RATE)
    de = adam_update(dense_master, dense_first, dense_second, grads[1], factor, steps, LEARN_RATE)
    hd = adam_update(head_master, head_first, head_second, grads[2], factor, steps, LEARN_RATE)
    tb = adam_update(table_master, table_first, table_second, grads[3], factor, steps, TABLE_RATE)
    return (loss, norm, sq[0], sq[1], sq[2], sq[3], de[0], de[1], de[2], de[3], hd[0], hd[1], hd[2], hd[3], tb[0], tb[1], tb[2], tb[3])
```

```python
import math

import jax
import jax.numpy as jnp
from jax import lax
from jax.sharding import Mesh
from jax.sharding import PartitionSpec as P

HEADS = 16
V = 48
PATCH_PIXELS = 4
SOURCES = 5
LATS = 64
PAD = 8

HIGH = lax.Precision.HIGHEST
CLIP_AT = 0.01
LEARN_RATE = 0.01
TABLE_RATE = 0.3
WEIGHT_DECAY = 0.1
FIRST_DECAY = 0.5
SECOND_DECAY = 0.5
EPSILON = 1e-08
NORM_EPSILON = 1e-05
AXES = ("y", "c", "z", "x")
BF = jnp.bfloat16
F32 = jnp.float32


class Grid:
    def __init__(self, mesh):
        nv, npatch = mesh.shape["var"], mesh.shape["patch"]
        self.sizes = {"y": nv // 2, "c": 2, "z": npatch // 2, "x": 2}
        self.mesh = Mesh(mesh.devices.reshape(tuple(self.sizes.values())), AXES)
        self.nv, self.np = nv, npatch
        self.fast = self.sizes["y"] == 2

    def flat(self, move):
        s = [self.sizes[a] for a in AXES]
        pairs = []
        for y in range(s[0]):
            for c in range(s[1]):
                for z in range(s[2]):
                    for x in range(s[3]):
                        ty, tc, tz, tx = move(y, c, z, x)
                        src = ((y * s[1] + c) * s[2] + z) * s[3] + x
                        dst = ((ty * s[1] + tc) * s[2] + tz) * s[3] + tx
                        pairs.append((src, dst))
        return pairs

    def permute(self, value, move):
        return lax.ppermute(value, AXES, self.flat(move))

    def swap(self, value, axis, bit=1):
        return lax.ppermute(value, axis, [(i, i ^ bit) for i in range(self.sizes[axis])])

    def total(self, value, axes=AXES):
        for axis in axes:
            bit = 1
            while bit < self.sizes[axis]:
                value = jax.tree.map(lambda v: v + self.swap(v, axis, bit), value)
                bit *= 2
        return value

    def spread(self, value, axes):
        count = math.prod(self.sizes[a] for a in axes)
        held = jnp.zeros((count,) + value.shape, value.dtype)
        held = lax.dynamic_update_index_in_dim(held, value, lax.axis_index(axes), 0)
        return self.total(held, axes)

    def along(self, first):
        def move(y, c, z, x):
            if (c == 0) == first:
                return (y ^ 1, c, z, x)
            return (y, c, z, x ^ 1)

        return move

    def flips(self, core, a, b):
        return jnp.where(core == 0, a, b), jnp.where(core == 0, b, a)

    def gather(self, piece):
        rows, w = piece.shape
        if not self.fast:
            return lax.all_gather(piece, AXES).reshape(self.nv, self.np, rows, w)
        nz = self.sizes["z"]
        y, c, z, x = (lax.axis_index(a) for a in AXES)
        line = jnp.zeros((nz, rows, w), piece.dtype)
        line = lax.dynamic_update_index_in_dim(line, piece, z, 0)
        for k in range(1, nz):
            got = lax.ppermute(piece, "z", [(i, (i + k) % nz) for i in range(nz)])
            line = lax.dynamic_update_index_in_dim(line, got, (z - k) % nz, 0)
        near = self.permute(line, self.along(False))
        far = [self.permute(v, self.along(True)) for v in (line, near)]
        mine = [[line, near], far]
        out = jnp.zeros((2, 2, nz, 2, rows, w), piece.dtype)
        for a in range(2):
            for b in range(2):
                fy, fx = self.flips(c, a, b)
                out = lax.dynamic_update_slice(
                    out, mine[a][b][None, None, :, None], (y ^ fy, c, 0, x ^ fx, 0, 0)
                )
                got = self.swap(mine[a][b], "c")
                fy, fx = self.flips(1 - c, a, b)
                out = lax.dynamic_update_slice(
                    out, got[None, None, :, None], (y ^ fy, 1 - c, 0, x ^ fx, 0, 0)
                )
        return out.reshape(self.nv, self.np, rows, w)

    def scatter(self, parts):
        nv, npatch, rows, w = parts.shape
        if not self.fast:
            flat = parts.reshape(nv * npatch * rows, w)
            return lax.psum_scatter(flat, AXES, scatter_dimension=0, tiled=True).astype(F32)
        nz = self.sizes["z"]
        y, c, z, x = (lax.axis_index(a) for a in AXES)
        cut = parts.reshape(2, 2, nz, 2, rows, w)

        def pick(core, a, b):
            fy, fx = self.flips(core, a, b)
            got = lax.dynamic_slice(
                cut, (y ^ fy, core, 0, x ^ fx, 0, 0), (1, 1, nz, 1, rows, w)
            )
            return got.reshape(nz, rows, w)

        def add(left, right):
            return (left.astype(F32) + right.astype(F32)).astype(BF)

        half = [
            [add(pick(c, a, b), self.swap(pick(1 - c, a, b), "c")) for b in range(2)]
            for a in range(2)
        ]
        quarter = [add(half[0][b], self.permute(half[1][b], self.along(True))) for b in range(2)]
        line = add(quarter[0], self.permute(quarter[1], self.along(False)))
        total = lax.dynamic_index_in_dim(line, z, 0, False).astype(F32)
        for k in range(1, nz):
            out = lax.dynamic_index_in_dim(line, (z + k) % nz, 0, False)
            got = lax.ppermute(out, "z", [(i, (i + k) % nz) for i in range(nz)])
            total = total + got.astype(F32)
        return total


def whole(chunks):
    nv, npatch, rows, w = chunks.shape
    return jnp.transpose(chunks, (0, 2, 1, 3)).reshape(nv * rows, npatch * w)


def chunked(value, nv, npatch):
    r, c = value.shape
    return jnp.transpose(value.reshape(nv, r // nv, npatch, c // npatch), (0, 2, 1, 3))


def latitude_table():
    levels = jnp.arange(2 * LATS).astype(F32)
    cosine = jnp.cos(((levels + 0.5) / (2 * LATS) - 0.5) * math.pi)
    scaled = cosine / jnp.mean(cosine)
    index = 2 * jnp.arange(LATS)[:, None] + jnp.arange(PATCH_PIXELS)[None, :] // 2
    return scaled[index]


def layer_norm(value, gain):
    center = value - jnp.mean(value, axis=-1, keepdims=True)
    spread = jnp.mean(center * center, axis=-1, keepdims=True)
    return center * lax.rsqrt(spread + NORM_EPSILON) * gain


def exact_gelu(value):
    return jax.nn.gelu(value, approximate=False)


def adam_update(master, first, second, grad, factor, steps, rate):
    clipped = grad * factor
    new_first = FIRST_DECAY * first + (1.0 - FIRST_DECAY) * clipped
    new_second = SECOND_DECAY * second + (1.0 - SECOND_DECAY) * clipped * clipped
    first_hat = new_first / (1.0 - jnp.power(FIRST_DECAY, steps))
    second_hat = new_second / (1.0 - jnp.power(SECOND_DECAY, steps))
    new_master = master - rate * (
        first_hat / (jnp.sqrt(second_hat) + EPSILON) + WEIGHT_DECAY * master
    )
    return (new_master, new_first, new_second, new_master.astype(BF))


def dot(a, b, dims, batch=((), ()), precision=None):
    return lax.dot_general(
        a, b, (dims, batch), precision=precision, preferred_element_type=F32
    )


NN = ((1,), (0,))
NT = ((1,), (1,))
TN = ((0,), (0,))


def body(
    grid,
    pixels,
    targets,
    masks,
    lengths,
    groups,
    latitudes,
    step_count,
    square_master,
    square_first,
    square_second,
    dense_master,
    dense_first,
    dense_second,
    head_master,
    head_first,
    head_second,
    table_master,
    table_first,
    table_second,
):
    nv, npatch = grid.nv, grid.np
    micro, items, _, cap, own_pixels = pixels.shape
    rows = micro * cap
    width = square_master.shape[1] * nv
    size = width // HEADS
    scale = size ** (-0.5)
    band, strip = square_master.shape[1:]
    ff_strip = dense_master.shape[2]
    ho = head_master.shape[1] * npatch
    base = 5 * V + cap
    table_band = table_master.shape[0]
    table_pad = -table_band % PAD
    my_band = lax.axis_index(("y", "c"))
    my_strip = lax.axis_index(("z", "x"))

    square_low = square_master.astype(BF)
    dense_low = dense_master.astype(BF)
    head_low = head_master.astype(BF)
    table_low = table_master.astype(BF)
    first = jnp.concatenate(
        [
            jnp.pad(table_low, ((0, table_pad), (0, 0))),
            square_low[2],
            square_low[3],
        ],
        axis=0,
    )
    first = grid.gather(first)
    table = whole(first[:, :, :table_band])
    start = table_band + table_pad
    wv = whole(first[:, :, start : start + band])
    wa = whole(first[:, :, start + band : start + 2 * band])
    second = grid.gather(square_low[4:8].reshape(4 * band, strip))
    wqkv = jnp.concatenate(
        [whole(second[:, :, k * band : (k + 1) * band]) for k in range(3)], axis=1
    )
    wo = whole(second[:, :, 3 * band :])
    w1 = whole(grid.gather(dense_low[0]))
    w2 = whole(grid.gather(dense_low[1]))
    head = whole(grid.gather(head_low))

    slots = jnp.arange(cap)
    lat_table = latitude_table()
    valid = masks[:, 0, 0].astype(F32) * (slots[None] < lengths[:, 0, 0][:, None]).astype(F32)[..., None]
    lat_onehot = (latitudes[:, 0, 0][..., None] == jnp.arange(LATS)).astype(F32)
    wpix = jnp.einsum("mcl,lk->mck", lat_onehot, lat_table, precision=HIGH) * valid
    weighted = jnp.tile(wpix.reshape(rows, PATCH_PIXELS), (1, V))
    count = grid.total(jnp.sum(valid))

    parts = pixels[:, :, 0]
    mine = lax.all_to_all(parts, ("y", "c"), split_axis=1, concat_axis=3, tiled=True)[:, 0]
    pix = jnp.transpose(mine.reshape(rows, V, PATCH_PIXELS), (0, 2, 1)).astype(F32)

    query = table[base + SOURCES]
    query_own = lax.dynamic_slice_in_dim(query, my_band * band, band)
    qv = dot(query_own[None], square_low[0], NN)[0]
    qv_own = grid.total(qv, ("y", "c")).astype(BF)
    col_head = (my_strip * strip + jnp.arange(strip)) // size
    head_mask = (col_head[:, None] == jnp.arange(HEADS)[None]).astype(F32)
    u_part = dot(square_low[1].astype(F32) * qv_own.astype(F32)[None], head_mask, NN, precision=HIGH)
    u_band = (grid.total(u_part, ("z", "x")) * scale).astype(BF)
    u = grid.spread(u_band, ("y", "c")).reshape(width, HEADS)
    rows_t = jnp.concatenate(
        [
            jnp.transpose(table[: PATCH_PIXELS * V].reshape(V, PATCH_PIXELS, width), (1, 0, 2)).reshape(-1, width),
            table[PATCH_PIXELS * V : base],
        ],
        axis=0,
    )
    tv = dot(rows_t, wv, NN)
    tu = dot(rows_t, u, NN)
    nk = PATCH_PIXELS * V
    n5 = nk + V
    scores = (
        jnp.einsum("ckv,kvh->chv", pix, tu[:nk].reshape(PATCH_PIXELS, V, HEADS), precision=HIGH)
        + tu[nk:n5].T[None]
        + jnp.tile(tu[n5:], (micro, 1))[:, :, None]
    )
    pa = jax.nn.softmax(scores, axis=-1)
    pal = pa.astype(BF).astype(F32)
    mass = jnp.sum(pal, axis=-1)
    fold = jnp.concatenate(
        [(pal[:, :, None] * pix[:, None]).reshape(rows, HEADS, nk), pal], axis=2
    )
    tv_heads = tv.reshape(-1, HEADS, size)
    pos_v = jnp.tile(tv_heads[n5:], (micro, 1, 1))
    agg = (
        jnp.einsum("chn,nhe->che", fold, tv_heads[:n5], precision=HIGH)
        + mass[:, :, None] * pos_v
    )
    gathered = agg.reshape(rows, width).astype(BF)

    gain_one = table[base + SOURCES + 1].astype(F32)
    gain_two = table[base + SOURCES + 2].astype(F32)
    onehot = (groups[:, 0, 0][:, None] == jnp.arange(SOURCES)).astype(F32)
    src = jnp.dot(onehot, table[base : base + SOURCES].astype(F32), precision=HIGH)
    x0 = dot(gathered, wa, NN) + jnp.repeat(src, cap, axis=0)
    h1 = layer_norm(x0, gain_one).astype(BF)
    qkv = dot(h1, wqkv, NN).astype(BF)
    q, k, vv = (
        qkv[:, i * width : (i + 1) * width].reshape(micro, cap, HEADS, size) for i in range(3)
    )
    keymask = slots[None] < lengths[:, 0, 0][:, None]
    raw = jnp.einsum("mqhe,mkhe->mhqk", q, k, preferred_element_type=F32) * scale
    probs = jax.nn.softmax(jnp.where(keymask[:, None, None], raw, -1e30), axis=-1)
    probs_low = probs.astype(BF)
    o = jnp.einsum("mhqk,mkhe->mqhe", probs_low, vv, preferred_element_type=F32)
    o = o.reshape(rows, width).astype(BF)
    x1 = x0 + dot(o, wo, NN)
    h2 = layer_norm(x1, gain_two).astype(BF)
    f = dot(h2, w1, NN)
    act = exact_gelu(f).astype(BF)
    x2 = x1 + dot(act, w2, NT)
    x2_low = x2.astype(BF)
    pred = dot(x2_low, head, NN)
    diff = pred - targets[:, 0, 0].astype(F32).reshape(rows, ho)
    loss_local = jnp.sum(weighted * diff * diff)
    dpred = (2.0 * weighted * diff / count).astype(BF)

    d_head = dot(x2_low, dpred, TN)
    dx2 = dot(dpred, head, NT)
    dx2_low = dx2.astype(BF)
    d_down = dot(dx2_low, act, TN)
    dact = dot(dx2_low, w2, NN)
    _, gelu_back = jax.vjp(exact_gelu, f)
    df = gelu_back(dact)[0].astype(BF)
    d_up = dot(h2, df, TN)
    dh2 = dot(df, w1, NT)
    _, norm_back = jax.vjp(layer_norm, x1, gain_two)
    dx1n, d_gain_two = norm_back(dh2)
    dx1 = dx2 + dx1n
    dx1_low = dx1.astype(BF)
    d_wo = dot(o, dx1_low, TN)
    do = dot(dx1_low, wo, NT).astype(BF).reshape(micro, cap, HEADS, size)
    dprobs = jnp.einsum("mqhe,mkhe->mhqk", do, vv, preferred_element_type=F32)
    dvv = jnp.einsum("mhqk,mqhe->mkhe", probs_low, do, preferred_element_type=F32)
    ds = (probs * (dprobs - jnp.sum(probs * dprobs, axis=-1, keepdims=True))).astype(BF)
    dq = jnp.einsum("mhqk,mkhe->mqhe", ds, k, preferred_element_type=F32) * scale
    dk = jnp.einsum("mhqk,mqhe->mkhe", ds, q, preferred_element_type=F32) * scale
    dqkv = jnp.concatenate([t.reshape(rows, width) for t in (dq, dk, dvv)], axis=1).astype(BF)
    d_wqkv = dot(h1, dqkv, TN)
    dh1 = dot(dqkv, wqkv, NT)
    _, norm_back = jax.vjp(layer_norm, x0, gain_one)
    dx0n, d_gain_one = norm_back(dh1)
    dx0 = dx1 + dx0n
    d_src = jnp.dot(onehot.T, jnp.sum(dx0.reshape(micro, cap, width), axis=1), precision=HIGH)
    dx0_low = dx0.astype(BF)
    d_wa = dot(gathered, dx0_low, TN)
    dagg = dot(dx0_low, wa, NT).astype(BF).astype(F32).reshape(rows, HEADS, size)

    dfold = jnp.einsum("che,nhe->chn", dagg, tv_heads[:n5], precision=HIGH)
    dpal = (
        jnp.sum(dfold[:, :, :nk].reshape(rows, HEADS, PATCH_PIXELS, V) * pix[:, None], axis=2)
        + dfold[:, :, nk:]
        + jnp.sum(dagg * pos_v, axis=-1)[:, :, None]
    )
    dsv = (pa * (dpal - jnp.sum(pa * dpal, axis=-1, keepdims=True))).astype(BF).astype(F32)
    g_rows = jnp.einsum("chn,che->nhe", fold, dagg, precision=HIGH).reshape(n5, width)
    g_pos = jnp.sum((mass[:, :, None] * dagg).reshape(micro, cap, width), axis=0)
    s_rows = jnp.concatenate(
        [
            jnp.einsum("ckv,chv->kvh", pix, dsv, precision=HIGH).reshape(nk, HEADS),
            jnp.sum(dsv, axis=0).T,
            jnp.sum(jnp.sum(dsv, axis=-1).reshape(micro, cap, HEADS), axis=0),
        ],
        axis=0,
    )
    g_table = jnp.concatenate(
        [
            jnp.transpose(g_rows[:nk].reshape(PATCH_PIXELS, V, width), (1, 0, 2)).reshape(nk, width),
            g_rows[nk:],
            g_pos,
            d_src,
            jnp.zeros((1, width), F32),
            d_gain_one[None],
            d_gain_two[None],
        ],
        axis=0,
    )
    s_table = jnp.concatenate(
        [
            jnp.transpose(s_rows[:nk].reshape(PATCH_PIXELS, V, HEADS), (1, 0, 2)).reshape(nk, HEADS),
            s_rows[nk:],
        ],
        axis=0,
    )

    def to_owner(value):
        return grid.scatter(chunked(value.astype(BF), nv, npatch))

    down_sum = to_owner(d_down)
    up_sum = to_owner(d_up)
    s_sum = grid.total(s_table)
    low_part = jnp.concatenate(
        [
            jnp.pad(chunked(g_table.astype(BF), nv, npatch), ((0, 0), (0, 0), (0, table_pad), (0, 0))),
            chunked(d_wa.astype(BF), nv, npatch),
        ],
        axis=2,
    )
    low_sum = grid.scatter(low_part)
    g_own = low_sum[:table_band]
    wa_sum = low_sum[table_band + table_pad :]
    attn_sum = grid.scatter(
        jnp.concatenate(
            [chunked(d_wqkv[:, i * width : (i + 1) * width].astype(BF), nv, npatch) for i in range(3)]
            + [chunked(d_wo.astype(BF), nv, npatch)],
            axis=2,
        )
    )
    head_sum = to_owner(d_head)

    g_low = g_own.astype(BF)
    g_column = grid.spread(g_low, ("y", "c")).reshape(nv * table_band, strip)[:base]
    g_line = jnp.transpose(grid.spread(g_low, ("z", "x")), (1, 0, 2)).reshape(table_band, width)
    table_own_band = lax.dynamic_slice_in_dim(table, my_band * band, band, 1)
    value_sum = dot(table_own_band[:base], g_column, TN)
    du_own = dot(table_own_band[:base].astype(F32), s_sum, TN, precision=HIGH)
    du_cols = dot(du_own, head_mask, NT, precision=HIGH)
    key_sum = du_cols * qv_own.astype(F32)[None] * scale
    dqv = grid.total(jnp.sum(square_low[1].astype(F32) * du_cols, axis=0) * scale, ("y", "c"))
    query_sum = query_own.astype(F32)[:, None] * dqv[None]
    dquery = jnp.sum(square_low[0].astype(F32) * dqv[None], axis=1)
    dquery = lax.dynamic_update_slice_in_dim(jnp.zeros((width,), F32), dquery, my_band * band, 0)
    dquery = grid.total(dquery)
    table_row = my_band * table_band + jnp.arange(table_band)
    s_pad = jnp.pad(s_sum, ((0, nv * table_band - base), (0, 0)))
    s_own = lax.dynamic_slice_in_dim(s_pad, my_band * table_band, table_band, 0)
    wv_rows = lax.dynamic_slice_in_dim(wv, my_strip * strip, strip, 0)
    u_rows = lax.dynamic_slice_in_dim(u, my_strip * strip, strip, 0)
    d_rows = dot(g_line, wv_rows, NT) + dot(s_own, u_rows.astype(F32), NT, precision=HIGH)
    dq_own = lax.dynamic_slice_in_dim(dquery, my_strip * strip, strip, 0)
    table_sum = jnp.where((table_row < base)[:, None], d_rows, g_own)
    table_sum = jnp.where((table_row == base + SOURCES)[:, None], dq_own[None], table_sum)
    square_sum = jnp.concatenate(
        [query_sum[None], key_sum[None], value_sum[None], wa_sum[None], attn_sum.reshape(4, band, strip)],
        axis=0,
    )
    dense_sum = jnp.stack([up_sum, down_sum])
    shards = (square_sum, dense_sum, head_sum, table_sum)
    sumsq = sum(jnp.sum(s * s) for s in shards)
    both = grid.total(jnp.stack([loss_local, sumsq]))
    loss = both[0] / count
    norm = jnp.sqrt(both[1])
    factor = jnp.minimum(1.0, CLIP_AT / norm)
    steps = step_count[0].astype(F32)
    sq = adam_update(square_master, square_first, square_second, shards[0], factor, steps, LEARN_RATE)
    de = adam_update(dense_master, dense_first, dense_second, shards[1], factor, steps, LEARN_RATE)
    hd = adam_update(head_master, head_first, head_second, shards[2], factor, steps, LEARN_RATE)
    tb = adam_update(table_master, table_first, table_second, shards[3], factor, steps, TABLE_RATE)
    return (loss, norm, *sq, *de, *hd, *tb)


def solution(mesh):
    grid = Grid(mesh)
    var, patch = ("y", "c"), ("z", "x")
    item = P(None, var, patch)
    weight = P(None, var, patch)
    flat = P(var, patch)
    in_specs = (
        P(None, None, patch, None, var),
        item,
        item,
        item,
        item,
        item,
        P(),
        *(weight,) * 6,
        *(flat,) * 6,
    )
    out_specs = (P(), P(), *(weight,) * 8, *(flat,) * 8)

    def step(*args):
        return body(grid, *args)

    return jax.shard_map(step, mesh=grid.mesh, in_specs=in_specs, out_specs=out_specs, check_vma=False)
```

```python
import math

import jax
import jax.numpy as jnp
import numpy as np
from jax import lax
from jax.experimental import pallas as pl
from jax.experimental.pallas import tpu as pltpu
from jax.sharding import Mesh
from jax.sharding import PartitionSpec as P

HEADS = 16
V = 48
PATCH_PIXELS = 4
SOURCES = 5
LATS = 64
PAD = 8

HIGH = lax.Precision.HIGHEST
CLIP_AT = 0.01
LEARN_RATE = 0.01
TABLE_RATE = 0.3
WEIGHT_DECAY = 0.1
FIRST_DECAY = 0.5
SECOND_DECAY = 0.5
EPSILON = 1e-08
NORM_EPSILON = 1e-05
AXES = ("y", "c", "z", "x")
BF = jnp.bfloat16
F32 = jnp.float32


class Grid:
    def __init__(self, mesh):
        nv, npatch = mesh.shape["var"], mesh.shape["patch"]
        self.sizes = {"y": nv // 2, "c": 2, "z": npatch // 2, "x": 2}
        self.mesh = Mesh(mesh.devices.reshape(tuple(self.sizes.values())), AXES)
        self.nv, self.np = nv, npatch
        self.fast = self.sizes["y"] == 2 and self.sizes["z"] == 4

    def flat(self, move):
        s = [self.sizes[a] for a in AXES]
        pairs = []
        for y in range(s[0]):
            for c in range(s[1]):
                for z in range(s[2]):
                    for x in range(s[3]):
                        ty, tc, tz, tx = move(y, c, z, x)
                        src = ((y * s[1] + c) * s[2] + z) * s[3] + x
                        dst = ((ty * s[1] + tc) * s[2] + tz) * s[3] + tx
                        pairs.append((src, dst))
        return pairs

    def permute(self, value, move):
        return lax.ppermute(value, AXES, self.flat(move))

    def swap(self, value, axis, bit=1):
        return lax.ppermute(value, axis, [(i, i ^ bit) for i in range(self.sizes[axis])])

    def total(self, value, axes=AXES):
        for axis in axes:
            bit = 1
            while bit < self.sizes[axis]:
                value = jax.tree.map(lambda v: v + self.swap(v, axis, bit), value)
                bit *= 2
        return value

    def spread(self, value, axes):
        count = math.prod(self.sizes[a] for a in axes)
        held = jnp.zeros((count,) + value.shape, value.dtype)
        held = lax.dynamic_update_index_in_dim(held, value, lax.axis_index(axes), 0)
        return self.total(held, axes)

    def along(self, first):
        def move(y, c, z, x):
            if (c == 0) == first:
                return (y ^ 1, c, z, x)
            return (y, c, z, x ^ 1)

        return move

    def gather(self, piece):
        return lax.all_gather(piece, AXES).reshape(self.nv, self.np, *piece.shape)

    def scatter(self, parts):
        nv, npatch, rows, w = parts.shape
        flat = parts.reshape(nv * npatch * rows, w)
        return lax.psum_scatter(flat, AXES, scatter_dimension=0, tiled=True).astype(F32)

    def gate(self, values, before):
        return lax.optimization_barrier((values, before))[0] if before else values

    def hop(self, value, *steps):
        for axis, bit in steps:
            value = value + self.swap(value, axis, bit)
        return value

    def begin(self, before, *moves):
        operands = self.gate([v for _, v in moves], before)
        return [fn(v) for (fn, _), v in zip(moves, operands)]

    def far_z(self, piece):
        return self.swap(piece, "z", 2)

    def next_z(self, pair):
        return self.swap(pair, "z", 1)

    def near(self, line):
        return self.permute(line, self.along(False))

    def far(self, both):
        return self.permute(both, self.along(True))

    def core(self, value):
        return self.swap(value, "c")

    def phase(self, state, number):
        kept, sent = state
        if number == 0:
            return kept, self.swap(sent, "c")
        if number in (1, 2):
            return kept, self.permute(sent, self.along(number == 1))
        return kept, self.swap(sent, "z", 1 if number == 3 else 2)

    def split(self, state):
        kept, got = state

        def add(left, right):
            return (left.astype(F32) + right.astype(F32)).astype(BF)

        half = kept.shape[0] // 2
        return add(kept[:half], got[:half]), add(kept[half:], got[half:])


def whole(chunks):
    nv, npatch, rows, w = chunks.shape
    return jnp.transpose(chunks, (0, 2, 1, 3)).reshape(nv * rows, npatch * w)


def chunked(value, nv, npatch):
    r, c = value.shape
    return jnp.transpose(value.reshape(nv, r // nv, npatch, c // npatch), (0, 2, 1, 3))


def latitude_table():
    levels = jnp.arange(2 * LATS).astype(F32)
    cosine = jnp.cos(((levels + 0.5) / (2 * LATS) - 0.5) * math.pi)
    scaled = cosine / jnp.mean(cosine)
    index = 2 * jnp.arange(LATS)[:, None] + jnp.arange(PATCH_PIXELS)[None, :] // 2
    return scaled[index]


def layer_norm(value, gain):
    center = value - jnp.mean(value, axis=-1, keepdims=True)
    spread = jnp.mean(center * center, axis=-1, keepdims=True)
    return center * lax.rsqrt(spread + NORM_EPSILON) * gain


def exact_gelu(value):
    return jax.nn.gelu(value, approximate=False)


def adam_update(master, first, second, grad, factor, steps, rate):
    clipped = grad * factor
    new_first = FIRST_DECAY * first + (1.0 - FIRST_DECAY) * clipped
    new_second = SECOND_DECAY * second + (1.0 - SECOND_DECAY) * clipped * clipped
    first_hat = new_first / (1.0 - jnp.power(FIRST_DECAY, steps))
    second_hat = new_second / (1.0 - jnp.power(SECOND_DECAY, steps))
    new_master = master - rate * (
        first_hat / (jnp.sqrt(second_hat) + EPSILON) + WEIGHT_DECAY * master
    )
    return (new_master, new_first, new_second, new_master.astype(BF))


def dot(a, b, dims, batch=((), ()), precision=None):
    return lax.dot_general(
        a, b, (dims, batch), precision=precision, preferred_element_type=F32
    )


NN = ((1,), (0,))
NT = ((1,), (1,))
TN = ((0,), (0,))


def body(
    grid,
    pixels,
    targets,
    masks,
    lengths,
    groups,
    latitudes,
    step_count,
    square_master,
    square_first,
    square_second,
    dense_master,
    dense_first,
    dense_second,
    head_master,
    head_first,
    head_second,
    table_master,
    table_first,
    table_second,
):
    nv, npatch = grid.nv, grid.np
    micro, items, _, cap, own_pixels = pixels.shape
    rows = micro * cap
    width = square_master.shape[1] * nv
    size = width // HEADS
    scale = size ** (-0.5)
    band, strip = square_master.shape[1:]
    ff_strip = dense_master.shape[2]
    ho = head_master.shape[1] * npatch
    base = 5 * V + cap
    table_band = table_master.shape[0]
    table_pad = -table_band % PAD
    my_band = lax.axis_index(("y", "c"))
    my_strip = lax.axis_index(("z", "x"))

    square_low = square_master.astype(BF)
    dense_low = dense_master.astype(BF)
    head_low = head_master.astype(BF)
    table_low = table_master.astype(BF)
    first = jnp.concatenate(
        [
            jnp.pad(table_low, ((0, table_pad), (0, 0))),
            square_low[2],
            square_low[3],
        ],
        axis=0,
    )
    first = grid.gather(first)
    table = whole(first[:, :, :table_band])
    start = table_band + table_pad
    wv = whole(first[:, :, start : start + band])
    wa = whole(first[:, :, start + band : start + 2 * band])
    second = grid.gather(square_low[4:8].reshape(4 * band, strip))
    wqkv = jnp.concatenate(
        [whole(second[:, :, k * band : (k + 1) * band]) for k in range(3)], axis=1
    )
    wo = whole(second[:, :, 3 * band :])
    w1 = whole(grid.gather(dense_low[0]))
    w2 = whole(grid.gather(dense_low[1]))
    head = whole(grid.gather(head_low))

    slots = jnp.arange(cap)
    lat_table = latitude_table()
    valid = masks[:, 0, 0].astype(F32) * (slots[None] < lengths[:, 0, 0][:, None]).astype(F32)[..., None]
    lat_onehot = (latitudes[:, 0, 0][..., None] == jnp.arange(LATS)).astype(F32)
    wpix = jnp.einsum("mcl,lk->mck", lat_onehot, lat_table, precision=HIGH) * valid
    weighted = jnp.tile(wpix.reshape(rows, PATCH_PIXELS), (1, V))
    count = grid.total(jnp.sum(valid))

    parts = pixels[:, :, 0]
    mine = lax.all_to_all(parts, ("y", "c"), split_axis=1, concat_axis=3, tiled=True)[:, 0]
    pix = jnp.transpose(mine.reshape(rows, V, PATCH_PIXELS), (0, 2, 1)).astype(F32)

    query = table[base + SOURCES]
    query_own = lax.dynamic_slice_in_dim(query, my_band * band, band)
    qv = dot(query_own[None], square_low[0], NN)[0]
    qv_own = grid.total(qv, ("y", "c")).astype(BF)
    col_head = (my_strip * strip + jnp.arange(strip)) // size
    head_mask = (col_head[:, None] == jnp.arange(HEADS)[None]).astype(F32)
    u_part = dot(square_low[1].astype(F32) * qv_own.astype(F32)[None], head_mask, NN, precision=HIGH)
    u_band = (grid.total(u_part, ("z", "x")) * scale).astype(BF)
    u = grid.spread(u_band, ("y", "c")).reshape(width, HEADS)
    rows_t = jnp.concatenate(
        [
            jnp.transpose(table[: PATCH_PIXELS * V].reshape(V, PATCH_PIXELS, width), (1, 0, 2)).reshape(-1, width),
            table[PATCH_PIXELS * V : base],
        ],
        axis=0,
    )
    tv = dot(rows_t, wv, NN)
    tu = dot(rows_t, u, NN)
    nk = PATCH_PIXELS * V
    n5 = nk + V
    scores = (
        jnp.einsum("ckv,kvh->chv", pix, tu[:nk].reshape(PATCH_PIXELS, V, HEADS), precision=HIGH)
        + tu[nk:n5].T[None]
        + jnp.tile(tu[n5:], (micro, 1))[:, :, None]
    )
    pa = jax.nn.softmax(scores, axis=-1)
    pal = pa.astype(BF).astype(F32)
    mass = jnp.sum(pal, axis=-1)
    fold = jnp.concatenate(
        [(pal[:, :, None] * pix[:, None]).reshape(rows, HEADS, nk), pal], axis=2
    )
    tv_heads = tv.reshape(-1, HEADS, size)
    pos_v = jnp.tile(tv_heads[n5:], (micro, 1, 1))
    agg = (
        jnp.einsum("chn,nhe->che", fold, tv_heads[:n5], precision=HIGH)
        + mass[:, :, None] * pos_v
    )
    gathered = agg.reshape(rows, width).astype(BF)

    gain_one = table[base + SOURCES + 1].astype(F32)
    gain_two = table[base + SOURCES + 2].astype(F32)
    onehot = (groups[:, 0, 0][:, None] == jnp.arange(SOURCES)).astype(F32)
    src = jnp.dot(onehot, table[base : base + SOURCES].astype(F32), precision=HIGH)
    x0 = dot(gathered, wa, NN) + jnp.repeat(src, cap, axis=0)
    h1 = layer_norm(x0, gain_one).astype(BF)
    qkv = dot(h1, wqkv, NN).astype(BF)
    q, k, vv = (
        qkv[:, i * width : (i + 1) * width].reshape(micro, cap, HEADS, size) for i in range(3)
    )
    keymask = slots[None] < lengths[:, 0, 0][:, None]
    raw = jnp.einsum("mqhe,mkhe->mhqk", q, k, preferred_element_type=F32) * scale
    probs = jax.nn.softmax(jnp.where(keymask[:, None, None], raw, -1e30), axis=-1)
    probs_low = probs.astype(BF)
    o = jnp.einsum("mhqk,mkhe->mqhe", probs_low, vv, preferred_element_type=F32)
    o = o.reshape(rows, width).astype(BF)
    x1 = x0 + dot(o, wo, NN)
    h2 = layer_norm(x1, gain_two).astype(BF)
    f = dot(h2, w1, NN)
    act = exact_gelu(f).astype(BF)
    x2 = x1 + dot(act, w2, NT)
    x2_low = x2.astype(BF)
    pred = dot(x2_low, head, NN)
    diff = pred - targets[:, 0, 0].astype(F32).reshape(rows, ho)
    loss_local = jnp.sum(weighted * diff * diff)
    dpred = (2.0 * weighted * diff / count).astype(BF)

    d_head = dot(x2_low, dpred, TN)
    dx2 = dot(dpred, head, NT)
    dx2_low = dx2.astype(BF)
    d_down = dot(dx2_low, act, TN)
    dact = dot(dx2_low, w2, NN)
    _, gelu_back = jax.vjp(exact_gelu, f)
    df = gelu_back(dact)[0].astype(BF)
    d_up = dot(h2, df, TN)
    dh2 = dot(df, w1, NT)
    _, norm_back = jax.vjp(layer_norm, x1, gain_two)
    dx1n, d_gain_two = norm_back(dh2)
    dx1 = dx2 + dx1n
    dx1_low = dx1.astype(BF)
    d_wo = dot(o, dx1_low, TN)
    do = dot(dx1_low, wo, NT).astype(BF).reshape(micro, cap, HEADS, size)
    dprobs = jnp.einsum("mqhe,mkhe->mhqk", do, vv, preferred_element_type=F32)
    dvv = jnp.einsum("mhqk,mqhe->mkhe", probs_low, do, preferred_element_type=F32)
    ds = (probs * (dprobs - jnp.sum(probs * dprobs, axis=-1, keepdims=True))).astype(BF)
    dq = jnp.einsum("mhqk,mkhe->mqhe", ds, k, preferred_element_type=F32) * scale
    dk = jnp.einsum("mhqk,mqhe->mkhe", ds, q, preferred_element_type=F32) * scale
    dqkv = jnp.concatenate([t.reshape(rows, width) for t in (dq, dk, dvv)], axis=1).astype(BF)
    d_wqkv = dot(h1, dqkv, TN)
    dh1 = dot(dqkv, wqkv, NT)
    _, norm_back = jax.vjp(layer_norm, x0, gain_one)
    dx0n, d_gain_one = norm_back(dh1)
    dx0 = dx1 + dx0n
    d_src = jnp.dot(onehot.T, jnp.sum(dx0.reshape(micro, cap, width), axis=1), precision=HIGH)
    dx0_low = dx0.astype(BF)
    d_wa = dot(gathered, dx0_low, TN)
    dagg = dot(dx0_low, wa, NT).astype(BF).astype(F32).reshape(rows, HEADS, size)

    dfold = jnp.einsum("che,nhe->chn", dagg, tv_heads[:n5], precision=HIGH)
    dpal = (
        jnp.sum(dfold[:, :, :nk].reshape(rows, HEADS, PATCH_PIXELS, V) * pix[:, None], axis=2)
        + dfold[:, :, nk:]
        + jnp.sum(dagg * pos_v, axis=-1)[:, :, None]
    )
    dsv = (pa * (dpal - jnp.sum(pa * dpal, axis=-1, keepdims=True))).astype(BF).astype(F32)
    g_rows = jnp.einsum("chn,che->nhe", fold, dagg, precision=HIGH).reshape(n5, width)
    g_pos = jnp.sum((mass[:, :, None] * dagg).reshape(micro, cap, width), axis=0)
    s_rows = jnp.concatenate(
        [
            jnp.einsum("ckv,chv->kvh", pix, dsv, precision=HIGH).reshape(nk, HEADS),
            jnp.sum(dsv, axis=0).T,
            jnp.sum(jnp.sum(dsv, axis=-1).reshape(micro, cap, HEADS), axis=0),
        ],
        axis=0,
    )
    g_table = jnp.concatenate(
        [
            jnp.transpose(g_rows[:nk].reshape(PATCH_PIXELS, V, width), (1, 0, 2)).reshape(nk, width),
            g_rows[nk:],
            g_pos,
            d_src,
            jnp.zeros((1, width), F32),
            d_gain_one[None],
            d_gain_two[None],
        ],
        axis=0,
    )
    s_table = jnp.concatenate(
        [
            jnp.transpose(s_rows[:nk].reshape(PATCH_PIXELS, V, HEADS), (1, 0, 2)).reshape(nk, HEADS),
            s_rows[nk:],
        ],
        axis=0,
    )

    def to_owner(value):
        return grid.scatter(chunked(value.astype(BF), nv, npatch))

    down_sum = to_owner(d_down)
    up_sum = to_owner(d_up)
    s_sum = grid.total(s_table)
    low_part = jnp.concatenate(
        [
            jnp.pad(chunked(g_table.astype(BF), nv, npatch), ((0, 0), (0, 0), (0, table_pad), (0, 0))),
            chunked(d_wa.astype(BF), nv, npatch),
        ],
        axis=2,
    )
    low_sum = grid.scatter(low_part)
    g_own = low_sum[:table_band]
    wa_sum = low_sum[table_band + table_pad :]
    attn_sum = grid.scatter(
        jnp.concatenate(
            [chunked(d_wqkv[:, i * width : (i + 1) * width].astype(BF), nv, npatch) for i in range(3)]
            + [chunked(d_wo.astype(BF), nv, npatch)],
            axis=2,
        )
    )
    head_sum = to_owner(d_head)

    g_low = g_own.astype(BF)
    g_column = grid.spread(g_low, ("y", "c")).reshape(nv * table_band, strip)[:base]
    g_line = jnp.transpose(grid.spread(g_low, ("z", "x")), (1, 0, 2)).reshape(table_band, width)
    table_own_band = lax.dynamic_slice_in_dim(table, my_band * band, band, 1)
    value_sum = dot(table_own_band[:base], g_column, TN)
    du_own = dot(table_own_band[:base].astype(F32), s_sum, TN, precision=HIGH)
    du_cols = dot(du_own, head_mask, NT, precision=HIGH)
    key_sum = du_cols * qv_own.astype(F32)[None] * scale
    dqv = grid.total(jnp.sum(square_low[1].astype(F32) * du_cols, axis=0) * scale, ("y", "c"))
    query_sum = query_own.astype(F32)[:, None] * dqv[None]
    dquery = jnp.sum(square_low[0].astype(F32) * dqv[None], axis=1)
    dquery = lax.dynamic_update_slice_in_dim(jnp.zeros((width,), F32), dquery, my_band * band, 0)
    dquery = grid.total(dquery)
    table_row = my_band * table_band + jnp.arange(table_band)
    s_pad = jnp.pad(s_sum, ((0, nv * table_band - base), (0, 0)))
    s_own = lax.dynamic_slice_in_dim(s_pad, my_band * table_band, table_band, 0)
    wv_rows = lax.dynamic_slice_in_dim(wv, my_strip * strip, strip, 0)
    u_rows = lax.dynamic_slice_in_dim(u, my_strip * strip, strip, 0)
    d_rows = dot(g_line, wv_rows, NT) + dot(s_own, u_rows.astype(F32), NT, precision=HIGH)
    dq_own = lax.dynamic_slice_in_dim(dquery, my_strip * strip, strip, 0)
    table_sum = jnp.where((table_row < base)[:, None], d_rows, g_own)
    table_sum = jnp.where((table_row == base + SOURCES)[:, None], dq_own[None], table_sum)
    square_sum = jnp.concatenate(
        [query_sum[None], key_sum[None], value_sum[None], wa_sum[None], attn_sum.reshape(4, band, strip)],
        axis=0,
    )
    dense_sum = jnp.stack([up_sum, down_sum])
    shards = (square_sum, dense_sum, head_sum, table_sum)
    sumsq = sum(jnp.sum(s * s) for s in shards)
    both = grid.total(jnp.stack([loss_local, sumsq]))
    loss = both[0] / count
    norm = jnp.sqrt(both[1])
    factor = jnp.minimum(1.0, CLIP_AT / norm)
    steps = step_count[0].astype(F32)
    sq = adam_update(square_master, square_first, square_second, shards[0], factor, steps, LEARN_RATE)
    de = adam_update(dense_master, dense_first, dense_second, shards[1], factor, steps, LEARN_RATE)
    hd = adam_update(head_master, head_first, head_second, shards[2], factor, steps, LEARN_RATE)
    tb = adam_update(table_master, table_first, table_second, shards[3], factor, steps, TABLE_RATE)
    return (loss, norm, *sq, *de, *hd, *tb)


NZ = 4
BANDS = 4
STRIPS = 8
NT_DIMS = (((1,), (1,)), ((), ()))
NN_DIMS = (((1,), (0,)), ((), ()))
TN_DIMS = (((0,), (0,)), ((), ()))
VMEM_LIMIT = 56 * 1024 * 1024


def mm(a, b):
    return lax.dot_general(a, b, NN_DIMS, preferred_element_type=F32)


def mm_nt(a, b):
    return lax.dot_general(a, b, NT_DIMS, preferred_element_type=F32)


def mm_tn(a, b):
    return lax.dot_general(a, b, TN_DIMS, preferred_element_type=F32)


def zflip(k):
    return (k % 2) * 2 + k // 2


def span(index, extent):
    return pl.ds(pl.multiple_of(index * extent, extent), extent)


def spots(core):
    out = []
    for owner in (core, 1 - core):
        for a in range(2):
            for b in range(2):
                out.append((a, b, owner) if owner == 0 else (b, a, owner))
    return out


def by_core(co, fn):
    for core in range(2):

        @pl.when(co[1] == core)
        def _(core=core):
            fn(core)


def forward_step(co, k, x_ref, chunks, row, band, w, put):
    back = co[2] ^ zflip(k)

    def run(core):
        places = spots(core)
        for fx in range(2):
            total = None
            for index, (fy, px, owner) in enumerate(places):
                if px != fx:
                    continue
                r = (co[0] ^ fy) * 2 + owner
                part = mm(x_ref[:, span(r, band)], chunks[index][0, row : row + band])
                total = part if total is None else total + part
            put(back * 2 + (co[3] ^ fx), total)

    by_core(co, run)


def backward_step(co, k, dy_ref, chunks, row, band, w, acc_ref, fresh):
    back = co[2] ^ zflip(k)

    def run(core):
        places = spots(core)
        for owner in range(2):
            for fy in range(2):
                total = None
                for index, (py, fx, who) in enumerate(places):
                    if (py, who) != (fy, owner):
                        continue
                    p = back * 2 + (co[3] ^ fx)
                    part = mm_nt(dy_ref[:, span(p, w)], chunks[index][0, row : row + band])
                    total = part if total is None else total + part
                r = (co[0] ^ fy) * 2 + owner

                @pl.when(fresh)
                def _():
                    acc_ref[:, span(r, band)] = total

                @pl.when(jnp.logical_not(fresh))
                def _():
                    acc_ref[:, span(r, band)] += total

    by_core(co, run)


def smem():
    return pl.BlockSpec(memory_space=pltpu.SMEM)


def full(shape):
    zeros = (0,) * len(shape)
    return pl.BlockSpec(shape, lambda i: zeros)


def steps_of(rows, w, first=0, block=0):
    def at(b):
        return pl.BlockSpec(
            (1, rows, w), lambda i: (b * NZ + jnp.clip(i - first, 0, NZ - 1), block, 0)
        )

    return [at(0), at(1)] * 4


def twice(arrays):
    return [v for v in arrays for _ in range(2)]


def call(kernel, name, grid, in_specs, outs, out_specs, scratch, flops, moved, *args):
    return pl.pallas_call(
        kernel,
        name=name,
        grid=grid,
        in_specs=in_specs,
        out_shape=outs,
        out_specs=out_specs,
        scratch_shapes=scratch,
        compiler_params=pltpu.CompilerParams(
            vmem_limit_bytes=VMEM_LIMIT
        ),
        cost_estimate=pl.CostEstimate(flops=flops, bytes_accessed=moved, transcendentals=0),
    )(*args)


def shape(*dims, dtype=F32):
    return jax.ShapeDtypeStruct(dims, dtype)


def norm(value, gain):
    center = value - jnp.mean(value, axis=-1, keepdims=True)
    spread = jnp.mean(center * center, axis=-1, keepdims=True)
    return center * lax.rsqrt(spread + NORM_EPSILON) * gain


def norm_grad(value, gain, grad):
    center = value - jnp.mean(value, axis=-1, keepdims=True)
    spread = jnp.mean(center * center, axis=-1, keepdims=True)
    inverse = lax.rsqrt(spread + NORM_EPSILON)
    unit = center * inverse
    inner = grad * gain
    out = inverse * (
        inner
        - jnp.mean(inner, axis=-1, keepdims=True)
        - unit * jnp.mean(inner * unit, axis=-1, keepdims=True)
    )
    return out, jnp.sum(grad * unit, axis=0, keepdims=True)


def half_masks(rows):
    lane = lax.broadcasted_iota(jnp.int32, (rows, 128), 1)
    return [(lane < 64).astype(BF), (lane >= 64).astype(BF)]


def assemble_kernel(co, *refs, band, offset, tall, extra):
    chunks, (table_ref, more_ref, value_ref) = refs[:8], refs[8:]
    k = pl.program_id(0)
    back = co[2] ^ zflip(k)

    def run(core):
        for index, (fy, fx, owner) in enumerate(spots(core)):
            r = (co[0] ^ fy) * 2 + owner
            p = back * 2 + (co[3] ^ fx)
            table_ref[span(r, tall), span(p, 128)] = chunks[index][0, offset : offset + tall]
            more_ref[r, p] = chunks[index][0, offset + tall : offset + tall + extra]
            value_ref[span(r, band), span(p, 128)] = chunks[index][0, :band]

    by_core(co, run)


def square_kernel(co, *refs, band):
    chunks, outs = refs[:8], refs[8:]
    k = pl.program_id(0)

    def run(core):
        for index, (fy, fx, owner) in enumerate(spots(core)):
            r = (co[0] ^ fy) * 2 + owner
            p = (co[2] ^ zflip(k)) * 2 + (co[3] ^ fx)
            for part, out_ref in enumerate(outs):
                out_ref[span(r, band), span(p, 128)] = chunks[index][0, part * band : (part + 1) * band]

    by_core(co, run)


def product_kernel(co, x_ref, *refs, band, w):
    chunks, out_ref = refs[:8], refs[8]

    def put(p, total):
        out_ref[:, span(p, w)] = total.astype(out_ref.dtype)

    forward_step(co, pl.program_id(0), x_ref, chunks, 0, band, w, put)


def pool_kernel(x_ref, e_ref, tu_ref, tv_ref, agg_ref, a_ref, pa_ref):
    j = pl.program_id(0)
    x, e = x_ref[...], e_ref[...]
    rows, n = x.shape
    masks = half_masks(n)
    lane = lax.broadcasted_iota(jnp.int32, (n, 128), 1)
    keep = lax.broadcasted_iota(jnp.int32, (rows, 128), 1) < V
    total = None
    for half in range(2):
        column = jnp.sum(jnp.where(lane == 2 * j + half, tu_ref[...], 0.0), axis=1, keepdims=True)
        m = e.astype(F32) * column
        high = m.astype(BF)
        rest = (m - high.astype(F32)).astype(BF)
        s = mm(x, high) + mm(x, rest)
        s = jnp.where(keep, s, -1e30)
        s = jnp.exp(s - jnp.max(s, axis=-1, keepdims=True))
        pa = s / jnp.sum(s, axis=-1, keepdims=True)
        wide = mm_nt(pa.astype(BF), e)
        a = (x.astype(F32) * wide).astype(BF)
        pa_ref[half] = pa
        a_ref[half] = a
        part = mm(a, tv_ref[...] * masks[half])
        total = part if total is None else total + part
    agg_ref[...] = total.astype(BF)


def enter_kernel(co, agg_ref, src_ref, gain_ref, *refs, band):
    chunks, (x0_ref, h1_ref) = refs[:8], refs[8:]
    k = pl.program_id(0)

    def put(p, total):
        x0_ref[:, span(p, 128)] = total

    forward_step(co, k, agg_ref, chunks, 0, band, 128, put)

    @pl.when(k == NZ - 1)
    def _():
        cap = x0_ref.shape[0] // src_ref.shape[0]
        for m in range(src_ref.shape[0]):
            x0_ref[m * cap : (m + 1) * cap] += src_ref[m : m + 1]
        h1_ref[...] = norm(x0_ref[...], gain_ref[...]).astype(BF)


def attend_kernel(co, lens, x0_ref, h1_ref, gain_ref, *refs, band, scale):
    qkv_chunks, o_chunks = refs[:8], refs[8:16]
    qkv_ref, p_ref, o_ref, x1_ref, h2_ref = refs[16:]
    i = pl.program_id(0)
    micro = lens.shape[0]
    width = x0_ref.shape[1]
    cap = x0_ref.shape[0] // micro

    @pl.when(i < NZ)
    def _():
        for part in range(3):

            def put(p, total, part=part):
                col = pl.multiple_of(part * width + p * 128, 128)
                qkv_ref[:, pl.ds(col, 128)] = total.astype(BF)

            forward_step(co, i, h1_ref, qkv_chunks, part * band, band, 128, put)

    @pl.when(i == NZ - 1)
    def _():
        masks = half_masks(cap)
        key = lax.broadcasted_iota(jnp.int32, (cap, cap), 1)

        @pl.loop(0, width // 128)
        def _(j):
            for m in range(micro):
                rows = slice(m * cap, (m + 1) * cap)
                q = qkv_ref[rows, span(j, 128)]
                kk = qkv_ref[rows, pl.ds(pl.multiple_of(width + j * 128, 128), 128)]
                vv = qkv_ref[rows, pl.ds(pl.multiple_of(2 * width + j * 128, 128), 128)]
                total = None
                for half in range(2):
                    s = mm_nt(q * masks[half], kk) * scale
                    s = jnp.where(key < lens[m], s, -1e30)
                    s = jnp.exp(s - jnp.max(s, axis=-1, keepdims=True))
                    p = s / jnp.sum(s, axis=-1, keepdims=True)
                    p_ref[2 * j + half, m] = p
                    part = mm(p.astype(BF), vv * masks[half])
                    total = part if total is None else total + part
                o_ref[rows, span(j, 128)] = total.astype(BF)

    @pl.when(i >= NZ)
    def _():
        def put(p, total):
            x1_ref[:, span(p, 128)] = x0_ref[:, span(p, 128)] + total

        forward_step(co, i - NZ, o_ref, o_chunks, 0, band, 128, put)

    @pl.when(i == 2 * NZ - 1)
    def _():
        h2_ref[...] = norm(x1_ref[...], gain_ref[...]).astype(BF)


def up_kernel(co, h2_ref, *refs, band, w):
    chunks, (act_ref, slope_ref) = refs[:8], refs[8:]

    def put(p, f):
        bell = jnp.exp(-0.5 * f * f)
        t = 1.0 / (1.0 + (0.3275911 * 0.5**0.5) * jnp.abs(f))
        tail = t * (1.061405429 * 0.5)
        for term in (-1.453152027, 1.421413741, -0.284496736, 0.254829592):
            tail = t * (0.5 * term + tail)
        tail = tail * bell
        share = jnp.where(f < 0.0, tail, 1.0 - tail)
        act_ref[:, span(p, w)] = (f * share).astype(BF)
        slope_ref[:, span(p, w)] = share + f * bell * ((2.0 * math.pi) ** -0.5)

    forward_step(co, pl.program_id(0), h2_ref, chunks, 0, band, w, put)


def down_kernel(co, count, x1_ref, act_ref, slope_ref, head_ref, target_ref, weight_ref, *refs, band, w):
    chunks = refs[:8]
    loss_ref, dx2_ref, dx2_low_ref, dhead_ref, df_ref = refs[8:13]
    acc_ref = refs[13]
    i = pl.program_id(0)

    @pl.when(i < NZ)
    def _():
        backward_step(co, i, act_ref, chunks, 0, band, w, acc_ref, i == 0)

    @pl.when(i == NZ - 1)
    def _():
        x2 = (x1_ref[...] + acc_ref[...]).astype(BF)
        diff = mm(x2, head_ref[...]) - target_ref[...].astype(F32)
        weighted = weight_ref[...] * diff
        loss_ref[...] = jnp.broadcast_to(jnp.sum(weighted * diff), loss_ref.shape)
        dpred = (2.0 * weighted / count[0]).astype(BF)
        dhead_ref[...] = mm_tn(x2, dpred).astype(BF)
        dx2 = mm_nt(dpred, head_ref[...])
        dx2_ref[...] = dx2
        dx2_low_ref[...] = dx2.astype(BF)

    @pl.when(i >= NZ)
    def _():
        def put(p, dact):
            df_ref[:, span(p, w)] = (dact * slope_ref[:, span(p, w)]).astype(BF)

        forward_step(co, i - NZ, dx2_low_ref, chunks, 0, band, w, put)


def owner_place(co, i, owner):
    a, b, k = i // (2 * NZ), (i // NZ) % 2, i % NZ
    fy = jnp.where(owner == 0, a, b)
    fx = jnp.where(owner == 0, b, a)
    return (co[0] ^ fy) * 2 + owner, (co[2] ^ zflip(k)) * 2 + (co[3] ^ fx)


def targets(co, keep_ref, send_ref):
    return [
        (out, owner, j)
        for out, owner in ((keep_ref, co[1]), (send_ref, 1 - co[1]))
        for j in range(NZ)
    ]


def grad_kernel(co, x_ref, dy_ref, keep_ref, send_ref, xt_ref, *, band, w):
    i = pl.program_id(0)

    @pl.when(i == 0)
    def _():
        xt_ref[...] = x_ref[...].T

    for out_ref, owner, j in targets(co, keep_ref, send_ref):
        r, p = owner_place(co, i * NZ + j, owner)
        out_ref[j] = mm(xt_ref[span(r, band)], dy_ref[:, span(p, w)]).astype(BF)


def qkv_grad_kernel(co, h1_ref, dqkv_ref, keep_ref, send_ref, ht_ref, *, band):
    i = pl.program_id(0)
    width = h1_ref.shape[1]

    @pl.when(i == 0)
    def _():
        ht_ref[...] = h1_ref[...].T

    for out_ref, owner, j in targets(co, keep_ref, send_ref):
        r, p = owner_place(co, i * NZ + j, owner)
        h1 = ht_ref[span(r, band)]
        for part in range(3):
            col = pl.multiple_of(part * width + p * 128, 128)
            got = mm(h1, dqkv_ref[:, pl.ds(col, 128)])
            out_ref[j, part * band : (part + 1) * band] = got.astype(BF)


def pair_grad_kernel(co, o_ref, agg_ref, dx1_ref, dx0_ref, keep_ref, send_ref, ot_ref, at_ref, *, band):
    i = pl.program_id(0)

    @pl.when(i == 0)
    def _():
        ot_ref[...] = o_ref[...].T
        at_ref[...] = agg_ref[...].T

    for out_ref, owner, j in targets(co, keep_ref, send_ref):
        r, p = owner_place(co, i * NZ + j, owner)
        got = mm(ot_ref[span(r, band)], dx1_ref[:, span(p, 128)])
        out_ref[j, :band] = got.astype(BF)
        got = mm(at_ref[span(r, band)], dx0_ref[:, span(p, 128)])
        out_ref[j, band:] = got.astype(BF)


def rows_kernel(co, g_ref, head_ref, keep_ref, send_ref, *, tall):
    i = pl.program_id(0)
    for out_ref, owner, j in targets(co, keep_ref, send_ref):
        r, p = owner_place(co, i * NZ + j, owner)
        out_ref[j, :tall] = g_ref[span(r, tall), span(p, 128)]
        out_ref[j, tall:] = head_ref[r, p]


def up_back_kernel(co, df_ref, x1_ref, gain_ref, dx2_ref, *refs, band, w):
    chunks, (dx1_ref, dx1_low_ref, dgain_ref, acc_ref) = refs[:8], refs[8:]
    k = pl.program_id(0)
    backward_step(co, k, df_ref, chunks, 0, band, w, acc_ref, k == 0)

    @pl.when(k == NZ - 1)
    def _():
        out, dgain = norm_grad(x1_ref[...], gain_ref[...], acc_ref[...])
        dx1 = dx2_ref[...] + out
        dx1_ref[...] = dx1
        dx1_low_ref[...] = dx1.astype(BF)
        dgain_ref[...] = dgain


def attend_back_kernel(co, dx1_low_ref, qkv_ref, p_ref, *refs, band, scale):
    o_chunks = refs[:8]
    dqkv_ref, acc_ref, do_ref = refs[8:]
    i = pl.program_id(0)
    micro = p_ref.shape[1]
    width = dx1_low_ref.shape[1]
    cap = dx1_low_ref.shape[0] // micro

    @pl.when(i < NZ)
    def _():
        backward_step(co, i, dx1_low_ref, o_chunks, 0, band, 128, acc_ref, i == 0)

    @pl.when(i == NZ - 1)
    def _():
        do_ref[...] = acc_ref[...].astype(BF)
        masks = half_masks(cap)

        @pl.loop(0, width // 128)
        def _(j):
            for m in range(micro):
                rows = slice(m * cap, (m + 1) * cap)
                k_at = pl.ds(pl.multiple_of(width + j * 128, 128), 128)
                v_at = pl.ds(pl.multiple_of(2 * width + j * 128, 128), 128)
                q, kk, vv = qkv_ref[rows, span(j, 128)], qkv_ref[rows, k_at], qkv_ref[rows, v_at]
                do = do_ref[rows, span(j, 128)]
                dq = dk = dv = None
                for half in range(2):
                    p = p_ref[2 * j + half, m]
                    do_half = do * masks[half]
                    dp = mm_nt(do_half, vv)
                    moved = p * dp
                    ds = (moved - p * jnp.sum(moved, axis=-1, keepdims=True)).astype(BF)
                    parts = (
                        mm(ds, kk * masks[half]),
                        mm_tn(ds, q * masks[half]),
                        mm_tn(p.astype(BF), do_half),
                    )
                    if dq is None:
                        dq, dk, dv = parts
                    else:
                        dq, dk, dv = dq + parts[0], dk + parts[1], dv + parts[2]
                dqkv_ref[rows, span(j, 128)] = (dq * scale).astype(BF)
                dqkv_ref[rows, k_at] = (dk * scale).astype(BF)
                dqkv_ref[rows, v_at] = dv.astype(BF)


def leave_kernel(co, dx1_ref, dqkv_ref, x0_ref, gain_ref, *refs, band):
    qkv_chunks, a_chunks = refs[:8], refs[8:16]
    dx0_low_ref, dgain_ref, dsum_ref, dagg_ref, acc_ref = refs[16:]
    i = pl.program_id(0)
    micro = dsum_ref.shape[0]
    width = x0_ref.shape[1]
    cap = x0_ref.shape[0] // micro

    @pl.when(i < NZ)
    def _():
        back = co[2] ^ zflip(i)

        def run(core):
            places = spots(core)
            for owner in range(2):
                for fy in range(2):
                    total = None
                    for index, (py, fx, who) in enumerate(places):
                        if (py, who) != (fy, owner):
                            continue
                        p = back * 2 + (co[3] ^ fx)
                        for part in range(3):
                            col = pl.multiple_of(part * width + p * 128, 128)
                            got = mm_nt(
                                dqkv_ref[:, pl.ds(col, 128)],
                                qkv_chunks[index][0, part * band : (part + 1) * band],
                            )
                            total = got if total is None else total + got
                    r = (co[0] ^ fy) * 2 + owner

                    @pl.when(i == 0)
                    def _():
                        acc_ref[:, span(r, band)] = total

                    @pl.when(i > 0)
                    def _():
                        acc_ref[:, span(r, band)] += total

        by_core(co, run)

    @pl.when(i == NZ - 1)
    def _():
        out, dgain = norm_grad(x0_ref[...], gain_ref[...], acc_ref[...])
        dx0 = dx1_ref[...] + out
        dx0_low_ref[...] = dx0.astype(BF)
        dgain_ref[...] = dgain
        for m in range(micro):
            dsum_ref[m : m + 1] = jnp.sum(dx0[m * cap : (m + 1) * cap], axis=0, keepdims=True)

    @pl.when(i >= NZ)
    def _():
        backward_step(co, i - NZ, dx0_low_ref, a_chunks, 0, band, 128, acc_ref, i == NZ)

    @pl.when(i == 2 * NZ - 1)
    def _():
        dagg_ref[...] = acc_ref[...].astype(BF)


def pool_back_kernel(x_ref, e_ref, tv_ref, a_ref, pa_ref, dagg_ref, g_ref, s_ref):
    x, e, dagg = x_ref[...].astype(F32), e_ref[...], dagg_ref[...]
    masks = half_masks(dagg.shape[0])
    total = None
    for half in range(2):
        part = dagg * masks[half]
        moved = mm_nt(part, tv_ref[...]) * x
        high = moved.astype(BF)
        rest = (moved - high.astype(F32)).astype(BF)
        dpal = mm(high, e) + mm(rest, e)
        pa = pa_ref[half]
        inner = pa * dpal
        ds = (inner - pa * jnp.sum(inner, axis=-1, keepdims=True)).astype(BF)
        s_ref[0, half : half + 1] = jnp.sum(mm_nt(ds, e) * x, axis=0, keepdims=True)
        got = mm_tn(a_ref[half], part)
        total = got if total is None else total + got
    g_ref[...] = total


def table_layout(cap, band, tall):
    n = BANDS * tall
    nk = PATCH_PIXELS * V
    select = np.zeros((nk, n), np.float32)
    fixed = np.zeros((cap, n), np.float32)
    var_of = np.zeros((n, 128), np.float32)
    for row in range(5 * V + cap):
        lane = (row // band) * tall + row % band
        if row < nk:
            select[row, lane] = 1.0
            var_of[lane, row // PATCH_PIXELS] = 1.0
        elif row < 5 * V:
            fixed[:, lane] = 1.0
            var_of[lane, row - nk] = 1.0
        else:
            fixed[row - 5 * V, lane] = 1.0
            var_of[lane, :V] = 1.0
    return select, fixed, var_of


def fast_body(
    grid,
    pixels,
    targets,
    masks,
    lengths,
    groups,
    latitudes,
    step_count,
    square_master,
    square_first,
    square_second,
    dense_master,
    dense_first,
    dense_second,
    head_master,
    head_first,
    head_second,
    table_master,
    table_first,
    table_second,
):
    micro, items, _, cap, own_pixels = pixels.shape
    rows = micro * cap
    band, strip = square_master.shape[1:]
    width = band * BANDS
    size = width // HEADS
    scale = size ** (-0.5)
    w = dense_master.shape[2]
    ff = w * STRIPS
    ho = head_master.shape[1] * STRIPS
    base = 5 * V + cap
    table_band = table_master.shape[0]
    tall = table_band + -table_band % 16
    n = BANDS * tall
    head_rows = head_master.size // strip
    y, c, z, x = (lax.axis_index(a) for a in AXES)
    co = jnp.stack([y, c, z, x]).astype(jnp.int32)
    my_band = y * 2 + c
    my_strip = z * 2 + x
    select, fixed, var_of = table_layout(cap, table_band, tall)

    def lane_of(row):
        return (row // table_band) * tall + row % table_band

    square_low = square_master.astype(BF)
    dense_low = dense_master.astype(BF)
    low_rows = 2 * band + tall + head_rows
    low = jnp.concatenate(
        [
            square_low[2],
            square_low[3],
            jnp.pad(table_master.astype(BF), ((0, tall - table_band), (0, 0))),
            head_master.astype(BF).reshape(head_rows, strip),
        ],
        axis=0,
    )
    attn = square_low[4:8].reshape(4 * band, strip)
    slots = jnp.arange(cap)
    lens = lengths[:, 0, 0]
    valid = masks[:, 0, 0].astype(F32) * (slots[None] < lens[:, None]).astype(F32)[..., None]
    lat_onehot = (latitudes[:, 0, 0][..., None] == jnp.arange(LATS)).astype(F32)
    wpix = jnp.einsum("mcl,lk->mck", lat_onehot, latitude_table(), precision=HIGH) * valid
    weighted = jnp.tile(wpix.reshape(rows, PATCH_PIXELS), (1, V))
    var_of = jnp.asarray(var_of, BF)
    query_row = base + SOURCES
    col_head = (my_strip * strip + jnp.arange(strip)) // size
    head_mask = (col_head[:, None] == jnp.arange(HEADS)[None]).astype(F32)
    wide, line, one = full((rows, width)), full((1, width)), shape(1, width)
    pair = pl.BlockSpec((rows, 128), lambda j: (0, j))
    src_at = lane_of(base)
    row = jnp.where(my_band == query_row // table_band, 1.0, 0.0) * table_master[query_row % table_band]
    first_pack = lax.dynamic_update_slice_in_dim(
        jnp.zeros((width,), F32), row.astype(BF).astype(F32), my_strip * strip, 0
    )
    first_pack = jnp.concatenate([first_pack, jnp.broadcast_to(jnp.sum(valid), (128,))])
    first_pack = grid.hop(first_pack, ("z", 1), ("z", 2))

    bundles = [low, attn, dense_low[0], dense_low[1], square_low[:2].reshape(2 * band, strip)]
    stack, join = lambda i, v: jnp.stack([bundles[i], v]), lambda a, b: jnp.concatenate([a, b], axis=0)
    z2, z1, near, far, core = grid.far_z, grid.next_z, grid.near, grid.far, grid.core
    (a0,) = grid.begin([first_pack], (z2, bundles[0]))
    p0 = stack(0, a0)
    b0, a1 = got = grid.begin([a0], (z1, p0), (z2, bundles[1]))
    l0, p1 = join(p0, b0), stack(1, a1)
    pack = grid.hop(first_pack, ("x", 1), ("y", 1), ("c", 1))
    query, count = pack[:width].astype(BF), pack[width]
    query_own = lax.dynamic_slice_in_dim(query, my_band * band, band)
    spread = jnp.tile(jnp.asarray(fixed), (micro, 1))
    for fy in range(2):
        for fc in range(2):
            other = (y ^ fy) * 2 + (c ^ fc)
            piece = lax.dynamic_index_in_dim(pixels[:, :, 0], other, 1, False)
            if fy or fc:
                piece = grid.permute(piece, lambda a, b, d, e, fy=fy, fc=fc: (a ^ fy, b ^ fc, d, e))
            pick = lax.dynamic_slice_in_dim(
                jnp.asarray(select, BF), other * own_pixels, own_pixels, 0
            )
            spread = spread + mm(piece.reshape(rows, own_pixels), pick)
    spread = spread.astype(BF)
    qv = dot(query_own[None], square_low[0], NN)[0]
    qv_own = grid.hop(qv, ("y", 1), ("c", 1)).astype(BF)
    u_part = dot(square_low[1].astype(F32) * qv_own.astype(F32)[None], head_mask, NN, precision=HIGH)
    u_part = lax.dynamic_update_slice_in_dim(jnp.zeros((width, HEADS), F32), u_part, my_band * band, 0)
    u_part = grid.hop(u_part, ("x", 1))
    n0, b1 = got = grid.begin([got, qv_own, spread], (near, l0), (z1, p1))
    f0, l1 = join(l0, n0), join(p1, b1)
    u_part = grid.hop(u_part, ("y", 1), ("c", 1))
    r0, n1, a2 = got = grid.begin([got, u_part], (far, f0), (near, l1), (z2, bundles[2]))
    f1, p2 = join(l1, n1), stack(2, a2)
    (b2,) = grid.begin([], (z1, p2))
    u_part = grid.hop(u_part, ("z", 1))
    l2 = join(p2, b2)
    c0, d0, r1, a3 = got = grid.begin(
        [got, b2, u_part], (core, f0), (core, r0), (far, f1), (z2, bundles[3])
    )
    p3 = stack(3, a3)
    (b3,) = grid.begin([], (z1, p3))
    u_part = grid.hop(u_part, ("z", 2))
    l3 = join(p3, b3)
    low = twice([f0, r0, c0, d0])
    n2, c1, d1, a4 = got = grid.begin(
        [got, b3, u_part], (near, l2), (core, f1), (core, r1), (z2, bundles[4])
    )
    f2, p4 = join(l2, n2), stack(4, a4)
    u = (u_part * scale).astype(BF)
    table, heads, wv = call(
        lambda *r: assemble_kernel(*r, band=band, offset=2 * band, tall=tall, extra=head_rows),
        "assemble",
        (NZ,),
        [smem()] + steps_of(low_rows, 128),
        (
            shape(n, width, dtype=BF),
            shape(BANDS, STRIPS, head_rows, 128, dtype=BF),
            shape(width, width, dtype=BF),
        ),
        (full((n, width)), full((BANDS, STRIPS, head_rows, 128)), full((width, width))),
        [],
        0,
        1 << 23,
        co,
        *low,
    )
    head = whole(heads.reshape(BANDS, STRIPS, band, ho // STRIPS))
    tv = call(
        lambda *r: product_kernel(*r, band=band, w=128),
        "table_values",
        (NZ,),
        [smem(), full((n, width))] + steps_of(band, 128),
        shape(n, width, dtype=BF),
        full((n, width)),
        [],
        2 * n * width * width,
        1 << 22,
        co,
        table,
        *low,
    )
    tu = jnp.pad(dot(table, u, NN), ((0, 0), (0, 128 - HEADS)))
    attn = twice([f1, r1, c1, d1])
    r2, n3, b4 = got = grid.begin([got, tv, u], (far, f2), (near, l3), (z1, p4))
    f3, l4 = join(l3, n3), join(p4, b4)
    tu, head, weighted = grid.gate((tu, head, weighted), [n2])
    tu = grid.gate(tu, [head, weighted])
    agg, fold, pa = call(
        pool_kernel,
        "pool",
        (HEADS // 2,),
        [full((rows, n)), full((n, 128)), full((n, 128)), pl.BlockSpec((n, 128), lambda j: (0, j))],
        (shape(rows, width, dtype=BF), shape(HEADS, rows, n, dtype=BF), shape(HEADS, rows, 128)),
        (
            pair,
            pl.BlockSpec((2, rows, n), lambda j: (j, 0, 0)),
            pl.BlockSpec((2, rows, 128), lambda j: (j, 0, 0)),
        ),
        [],
        12 * HEADS * rows * n * 128,
        1 << 23,
        spread,
        var_of,
        tu,
        tv,
    )

    gain_one = table[lane_of(base + SOURCES + 1)].astype(F32)[None]
    gain_two = table[lane_of(base + SOURCES + 2)].astype(F32)[None]
    onehot = (groups[:, 0, 0][:, None] == jnp.arange(SOURCES)).astype(F32)
    src = dot(onehot, table[src_at : src_at + SOURCES].astype(F32), NN, precision=HIGH)
    x0, h1 = call(
        lambda *r: enter_kernel(*r, band=band),
        "enter",
        (NZ,),
        [smem(), wide, full((micro, width)), line] + steps_of(band, 128, 0, 1),
        (shape(rows, width), shape(rows, width, dtype=BF)),
        (wide, wide),
        [],
        2 * rows * width * width,
        1 << 22,
        co,
        agg,
        src,
        gain_one,
        *low,
    )
    c2, d2, r3, n4 = got = grid.begin(
        [got, h1], (core, f2), (core, r2), (far, f3), (near, l4)
    )
    f4 = join(l4, n4)
    up = twice([f2, r2, c2, d2])
    qkv, probs, o, x1, h2 = call(
        lambda *r: attend_kernel(*r, band=band, scale=scale),
        "attend",
        (2 * NZ,),
        [smem(), smem(), wide, wide, line]
        + steps_of(3 * band, 128)
        + steps_of(band, 128, NZ, 3),
        (
            shape(rows, 3 * width, dtype=BF),
            shape(HEADS, micro, cap, cap),
            shape(rows, width, dtype=BF),
            shape(rows, width),
            shape(rows, width, dtype=BF),
        ),
        (full((rows, 3 * width)), full((HEADS, micro, cap, cap)), wide, wide, wide),
        [],
        8 * rows * width * width + 8 * rows * cap * width,
        1 << 24,
        co,
        lens,
        x0,
        h1,
        gain_two,
        *attn,
        *attn,
    )
    c3, d3, r4 = got = grid.begin([got, h2], (core, f3), (core, r3), (far, f4))
    down = twice([f3, r3, c3, d3])
    act, slope = call(
        lambda *r: up_kernel(*r, band=band, w=w),
        "up",
        (NZ,),
        [smem(), wide] + steps_of(band, w),
        (shape(rows, ff, dtype=BF), shape(rows, ff)),
        (full((rows, ff)), full((rows, ff))),
        [],
        2 * rows * width * ff,
        1 << 24,
        co,
        h2,
        *up,
    )
    wq_parts = [f4, r4, *grid.begin([got, act], (core, f4), (core, r4))]
    act = grid.gate(act, [r4])
    loss_part, dx2, dx2_low, d_head, df = call(
        lambda *r: down_kernel(*r, band=band, w=w),
        "down",
        (2 * NZ,),
        [smem(), smem(), wide, full((rows, ff)), full((rows, ff)), full((width, ho)), full((rows, ho)), full((rows, ho))]
        + [pl.BlockSpec((1, band, w), lambda i, b=b: (b * NZ + i % NZ, 0, 0)) for b in range(2)] * 4,
        (
            shape(8, 128),
            shape(rows, width),
            shape(rows, width, dtype=BF),
            shape(width, ho, dtype=BF),
            shape(rows, ff, dtype=BF),
        ),
        (full((8, 128)), wide, wide, full((width, ho)), full((rows, ff))),
        [pltpu.VMEM((rows, width), F32)],
        4 * rows * width * ff,
        1 << 25,
        co,
        count[None],
        x1,
        act,
        slope,
        head,
        targets[:, 0, 0].reshape(rows, ho),
        weighted,
        *down,
    )

    place = lambda height, wid: pl.BlockSpec((NZ, height, wid), lambda i: (i, 0, 0))

    turned = [pltpu.VMEM((width, rows), BF)]

    def sent(kernel, name, height, wid, flops, scratch, *args):
        out = shape(4 * NZ, height, wid, dtype=BF)
        return call(
            kernel,
            name,
            (NZ,),
            [smem()] + [full(a.shape) for a in args],
            (out, out),
            (place(height, wid),) * 2,
            scratch,
            flops,
            32 * height * wid * 2 + 4 * 1024 * 1024,
            co,
            *args,
        )

    dense_grad = lambda *r: grad_kernel(*r, band=band, w=w)
    flow, done = {}, {}

    def stage(work, before):
        gated = grid.gate([flow[name] for name, _ in work], before)
        arrived = []
        for (name, number), state in zip(work, gated):
            state = grid.phase(state, number)
            arrived.append(state[1])
            if number < 4:
                flow[name] = grid.split(state)
            else:
                done[name] = state[0].astype(F32) + state[1].astype(F32)
        return arrived

    flow["down"] = sent(dense_grad, "down_grad", band, w, 2 * rows * width * ff, turned, dx2_low, act)
    df = grid.gate(df, [flow["down"]])
    flow["up"] = sent(dense_grad, "up_grad", band, w, 2 * rows * width * ff, turned, h2, df)
    got = stage([("down", 0)], [])
    df = grid.gate(df, [flow["up"], flow["down"]])
    dx1, dx1_low, d_gain_two = call(
        lambda *r: up_back_kernel(*r, band=band, w=w),
        "up_back",
        (NZ,),
        [smem(), full((rows, ff)), wide, line, wide] + steps_of(band, w),
        (shape(rows, width), shape(rows, width, dtype=BF), one),
        (wide, wide, line),
        [pltpu.VMEM((rows, width), F32)],
        2 * rows * width * ff,
        1 << 24,
        co,
        df,
        x1,
        gain_two,
        dx2,
        *up,
    )
    dqkv = call(
        lambda *r: attend_back_kernel(*r, band=band, scale=scale),
        "attend_back",
        (NZ,),
        [smem(), wide, full((rows, 3 * width)), full((HEADS, micro, cap, cap))]
        + steps_of(band, 128, 0, 3),
        shape(rows, 3 * width, dtype=BF),
        full((rows, 3 * width)),
        [pltpu.VMEM((rows, width), F32), pltpu.VMEM((rows, width), BF)],
        2 * rows * width * width + 12 * rows * cap * width,
        1 << 22,
        co,
        dx1_low,
        qkv,
        probs,
        *attn,
    )
    got = stage([("down", 1), ("up", 0)], [got, flow["up"]])
    dqkv = grid.gate(dqkv, [got, flow["up"], flow["down"]])
    got = stage([("down", 2), ("up", 1)], [got, dqkv])
    flow["qkv"] = sent(
        lambda *r: qkv_grad_kernel(*r, band=band),
        "qkv_grad",
        3 * band,
        128,
        6 * rows * width * width,
        turned,
        h1,
        dqkv,
    )
    dx0_low, d_gain_one, dx0_sum, dagg = call(
        lambda *r: leave_kernel(*r, band=band),
        "leave",
        (2 * NZ,),
        [smem(), wide, full((rows, 3 * width)), wide, line]
        + steps_of(3 * band, 128)
        + steps_of(band, 128, NZ, 1),
        (
            shape(rows, width, dtype=BF),
            one,
            shape(micro, width),
            shape(rows, width, dtype=BF),
        ),
        (wide, line, full((micro, width)), wide),
        [pltpu.VMEM((rows, width), F32)],
        8 * rows * width * width,
        1 << 23,
        co,
        dx1,
        dqkv,
        x0,
        gain_one,
        *attn,
        *low,
    )
    got_core = stage([("qkv", 0)], [])
    dx0_low, dx1_low = grid.gate((dx0_low, dx1_low), [got, got_core, flow["down"], flow["up"]])
    got = stage([("down", 3), ("up", 2), ("qkv", 1)], [got, got_core, dagg])
    flow["pair"] = sent(
        lambda *r: pair_grad_kernel(*r, band=band),
        "pair_grad",
        2 * band,
        128,
        4 * rows * width * width,
        turned * 2,
        o,
        agg,
        dx1_low,
        dx0_low,
    )
    dagg = grid.gate(dagg, [flow["pair"]])
    got_core = stage([("pair", 0)], [])
    g_rows, s_rows = call(
        pool_back_kernel,
        "pool_back",
        (HEADS // 2,),
        [
            full((rows, n)),
            full((n, 128)),
            pl.BlockSpec((n, 128), lambda j: (0, j)),
            pl.BlockSpec((2, rows, n), lambda j: (j, 0, 0)),
            pl.BlockSpec((2, rows, 128), lambda j: (j, 0, 0)),
            pair,
        ],
        (shape(n, width), shape(HEADS // 2, 2, n)),
        (pl.BlockSpec((n, 128), lambda j: (0, j)), pl.BlockSpec((1, 2, n), lambda j: (j, 0, 0))),
        [],
        14 * HEADS * rows * n * 128,
        1 << 23,
        spread,
        var_of,
        tv,
        fold,
        pa,
        dagg,
    )
    extra = jnp.concatenate(
        [
            jnp.zeros((src_at, width), F32),
            dot(onehot, dx0_sum, TN, precision=HIGH),
            jnp.zeros((1, width), F32),
            d_gain_one,
            d_gain_two,
            jnp.zeros((n - src_at - SOURCES - 3, width), F32),
        ],
        axis=0,
    )
    s_rows = grid.gate(s_rows, got)
    got = stage([("down", 4), ("up", 3), ("qkv", 2), ("pair", 1)], [got, got_core, g_rows])
    s_sum = grid.hop(s_rows.reshape(HEADS, n), ("c", 1), ("y", 1))
    flow["rows"] = sent(
        lambda *r: rows_kernel(*r, tall=tall),
        "rows",
        tall + head_rows,
        128,
        0,
        [],
        (g_rows + extra).astype(BF),
        chunked(d_head, BANDS, STRIPS).reshape(BANDS, STRIPS, head_rows, 128),
    )
    got_core = stage([("rows", 0)], [])
    got = stage([("up", 4), ("qkv", 3), ("pair", 2), ("rows", 1)], [got, got_core, s_sum])
    s_sum = grid.hop(s_sum, ("x", 1))
    got = stage([("qkv", 4), ("pair", 3), ("rows", 2)], [got, s_sum])
    wq_parts = grid.gate(wq_parts, got)
    s_sum = grid.hop(s_sum, ("z", 1))
    got = stage([("pair", 4), ("rows", 3)], [got, s_sum])
    s_sum = grid.hop(s_sum, ("z", 2))
    got = stage([("rows", 4)], [got, s_sum])
    wq, wk = call(
        lambda *r: square_kernel(*r, band=band),
        "squares",
        (NZ,),
        [smem()] + steps_of(2 * band, 128),
        (shape(width, width, dtype=BF),) * 2,
        (full((width, width)),) * 2,
        [],
        0,
        1 << 20,
        co,
        *twice(wq_parts),
    )
    u_heads = (jnp.arange(width)[:, None] // size == jnp.arange(HEADS)[None]).astype(F32)
    du = dot(table.astype(F32), s_sum, ((0,), (1,)), precision=HIGH)
    du_cols = dot(lax.dynamic_slice_in_dim(du, my_band * band, band), head_mask, NT, precision=HIGH)
    dqv_heads = dot(du, wk.astype(F32), TN, precision=HIGH) * scale
    dqv_all = jnp.sum(dqv_heads * u_heads.T, axis=0)
    dqv = lax.dynamic_slice_in_dim(dqv_all, my_strip * strip, strip)
    dq_own = jnp.sum(
        lax.dynamic_slice_in_dim(wq, my_strip * strip, strip, 0).astype(F32) * dqv_all[None], axis=1
    )
    table_own = lax.dynamic_slice_in_dim(table, my_band * band, band, 1)
    g_own = done["rows"][0][:tall]
    g_low = g_own.astype(BF)
    g_column = grid.spread(g_low, ("y", "c")).reshape(n, strip)
    g_line = jnp.transpose(grid.spread(g_low, ("z", "x")), (1, 0, 2)).reshape(tall, width)
    down_sum, up_sum = done["down"][0], done["up"][0]
    wa_sum = done["pair"][0][band:]
    attn_sum = (done["qkv"][0].reshape(3, band, strip), done["pair"][0][:band])
    head_sum = done["rows"][0][tall:].reshape(head_master.shape)

    row_of = np.full((n,), base + SOURCES + 3)
    for row in range(base + SOURCES + 3):
        row_of[lane_of(row)] = row
    row_of = jnp.asarray(row_of)
    g_column = jnp.where((row_of < base)[:, None], g_column, 0.0).astype(BF)
    value_sum = dot(table_own, g_column, TN)
    key_sum = du_cols * qv_own.astype(F32)[None] * scale
    query_sum = query_own.astype(F32)[:, None] * dqv[None]
    s_own = lax.dynamic_slice_in_dim(s_sum, my_band * tall, tall, 1)
    wv_rows = lax.dynamic_slice_in_dim(wv, my_strip * strip, strip, 0)
    u_rows = lax.dynamic_slice_in_dim(u, my_strip * strip, strip, 0).astype(F32)
    d_rows = dot(g_line, wv_rows, NT) + dot(s_own, u_rows, ((0,), (1,)), precision=HIGH)
    own_row = lax.dynamic_slice_in_dim(row_of, my_band * tall, tall)[:, None]
    table_sum = jnp.where(own_row < base, d_rows, g_own)
    table_sum = jnp.where(own_row == base + SOURCES, dq_own[None], table_sum)[:table_band]
    square_sums = (query_sum, key_sum, value_sum, wa_sum, *attn_sum)
    sumsq = sum(jnp.sum(s * s) for s in (*square_sums, up_sum, down_sum, head_sum, table_sum))
    both = grid.total(jnp.stack([loss_part[0, 0], sumsq]))
    loss = both[0] / count
    grad_norm = jnp.sqrt(both[1])
    factor = jnp.minimum(1.0, CLIP_AT / grad_norm)
    steps = step_count[0].astype(F32)
    square_sum = jnp.concatenate([s.reshape(-1, band, strip) for s in square_sums], axis=0)
    dense_sum = jnp.stack([up_sum, down_sum])
    sq = adam_update(square_master, square_first, square_second, square_sum, factor, steps, LEARN_RATE)
    de = adam_update(dense_master, dense_first, dense_second, dense_sum, factor, steps, LEARN_RATE)
    hd = adam_update(head_master, head_first, head_second, head_sum, factor, steps, LEARN_RATE)
    tb = adam_update(table_master, table_first, table_second, table_sum, factor, steps, TABLE_RATE)
    return (loss, grad_norm, *sq, *de, *hd, *tb)


def solution(mesh):
    grid = Grid(mesh)
    var, patch = ("y", "c"), ("z", "x")
    item = P(None, var, patch)
    weight = P(None, var, patch)
    flat = P(var, patch)
    in_specs = (
        P(None, None, patch, None, var),
        item,
        item,
        item,
        item,
        item,
        P(),
        *(weight,) * 6,
        *(flat,) * 6,
    )
    out_specs = (P(), P(), *(weight,) * 8, *(flat,) * 8)

    def step(*args):
        return (fast_body if grid.fast else body)(grid, *args)

    return jax.shard_map(step, mesh=grid.mesh, in_specs=in_specs, out_specs=out_specs, check_vma=False)
```

```python
import math

import jax
import jax.numpy as jnp
import numpy as np
from jax import lax
from jax.experimental import pallas as pl
from jax.experimental.pallas import tpu as pltpu
from jax.sharding import Mesh
from jax.sharding import PartitionSpec as P

HEADS = 16
V = 48
PATCH_PIXELS = 4
SOURCES = 5
LATS = 64
PAD = 8

HIGH = lax.Precision.HIGHEST
CLIP_AT = 0.01
LEARN_RATE = 0.01
TABLE_RATE = 0.3
WEIGHT_DECAY = 0.1
FIRST_DECAY = 0.5
SECOND_DECAY = 0.5
EPSILON = 1e-08
NORM_EPSILON = 1e-05
AXES = ("y", "c", "z", "x")
BF = jnp.bfloat16
F32 = jnp.float32


class Grid:
    def __init__(self, mesh):
        nv, npatch = mesh.shape["var"], mesh.shape["patch"]
        self.sizes = {"y": nv // 2, "c": 2, "z": npatch // 2, "x": 2}
        self.mesh = Mesh(mesh.devices.reshape(tuple(self.sizes.values())), AXES)
        self.nv, self.np = nv, npatch
        self.fast = self.sizes["y"] == 2 and self.sizes["z"] == 4

    def flat(self, move):
        s = [self.sizes[a] for a in AXES]
        pairs = []
        for y in range(s[0]):
            for c in range(s[1]):
                for z in range(s[2]):
                    for x in range(s[3]):
                        ty, tc, tz, tx = move(y, c, z, x)
                        src = ((y * s[1] + c) * s[2] + z) * s[3] + x
                        dst = ((ty * s[1] + tc) * s[2] + tz) * s[3] + tx
                        pairs.append((src, dst))
        return pairs

    def permute(self, value, move):
        return lax.ppermute(value, AXES, self.flat(move))

    def swap(self, value, axis, bit=1):
        return lax.ppermute(value, axis, [(i, i ^ bit) for i in range(self.sizes[axis])])

    def total(self, value, axes=AXES):
        for axis in axes:
            bit = 1
            while bit < self.sizes[axis]:
                value = jax.tree.map(lambda v: v + self.swap(v, axis, bit), value)
                bit *= 2
        return value

    def spread(self, value, axes):
        count = math.prod(self.sizes[a] for a in axes)
        held = jnp.zeros((count,) + value.shape, value.dtype)
        held = lax.dynamic_update_index_in_dim(held, value, lax.axis_index(axes), 0)
        return self.total(held, axes)

    def along(self, first):
        def move(y, c, z, x):
            if (c == 0) == first:
                return (y ^ 1, c, z, x)
            return (y, c, z, x ^ 1)

        return move

    def gather(self, piece):
        return lax.all_gather(piece, AXES).reshape(self.nv, self.np, *piece.shape)

    def scatter(self, parts):
        nv, npatch, rows, w = parts.shape
        flat = parts.reshape(nv * npatch * rows, w)
        return lax.psum_scatter(flat, AXES, scatter_dimension=0, tiled=True).astype(F32)

    def gate(self, values, before):
        empty = isinstance(before, list) and not before
        return values if empty else lax.optimization_barrier((values, before))[0]

    def hop(self, value, *steps):
        for axis, bit in steps:
            value = value + self.swap(value, axis, bit)
        return value

    def rounds(self, value, axes):
        if "c" in axes:
            value = value + self.swap(value, "c")
        if "y" in axes:
            both = self.permute(value, lambda y, c, z, x: (y ^ 1, c, z, x ^ 1))
            value = (value + self.swap(value, "x")) + (self.swap(value, "y") + both)
        elif "x" in axes:
            value = value + self.swap(value, "x")
        if "z" in axes:
            third = self.swap(value, "z", 3)
            value = (value + self.swap(value, "z", 1)) + (self.swap(value, "z", 2) + third)
        return value

    def collect(self, value, axis):
        count = self.sizes[axis]
        here = lax.axis_index(axis)
        got = [value] + [self.swap(value, axis, flip) for flip in range(1, count)]
        out = []
        for place in range(count):
            piece = got[count - 1]
            for flip in range(count - 1):
                piece = jnp.where((here ^ flip) == place, got[flip], piece)
            out.append(piece)
        return jnp.stack(out)

    def begin(self, before, *moves):
        operands = self.gate([v for _, v in moves], before)
        return [fn(v) for (fn, _), v in zip(moves, operands)]

    def far_z(self, piece):
        return self.swap(piece, "z", 2)

    def next_z(self, pair):
        return self.swap(pair, "z", 1)

    def near(self, line):
        return self.permute(line, self.along(False))

    def far(self, both):
        return self.permute(both, self.along(True))

    def core(self, value):
        return self.swap(value, "c")


def whole(chunks):
    nv, npatch, rows, w = chunks.shape
    return jnp.transpose(chunks, (0, 2, 1, 3)).reshape(nv * rows, npatch * w)


def chunked(value, nv, npatch):
    r, c = value.shape
    return jnp.transpose(value.reshape(nv, r // nv, npatch, c // npatch), (0, 2, 1, 3))


def latitude_table():
    levels = jnp.arange(2 * LATS).astype(F32)
    cosine = jnp.cos(((levels + 0.5) / (2 * LATS) - 0.5) * math.pi)
    scaled = cosine / jnp.mean(cosine)
    index = 2 * jnp.arange(LATS)[:, None] + jnp.arange(PATCH_PIXELS)[None, :] // 2
    return scaled[index]


def layer_norm(value, gain):
    center = value - jnp.mean(value, axis=-1, keepdims=True)
    spread = jnp.mean(center * center, axis=-1, keepdims=True)
    return center * lax.rsqrt(spread + NORM_EPSILON) * gain


def exact_gelu(value):
    return jax.nn.gelu(value, approximate=False)


def adam_update(master, first, second, grad, factor, steps, rate):
    clipped = grad * factor
    new_first = FIRST_DECAY * first + (1.0 - FIRST_DECAY) * clipped
    new_second = SECOND_DECAY * second + (1.0 - SECOND_DECAY) * clipped * clipped
    first_hat = new_first / (1.0 - jnp.power(FIRST_DECAY, steps))
    second_hat = new_second / (1.0 - jnp.power(SECOND_DECAY, steps))
    new_master = master - rate * (
        first_hat / (jnp.sqrt(second_hat) + EPSILON) + WEIGHT_DECAY * master
    )
    return (new_master, new_first, new_second, new_master.astype(BF))


def dot(a, b, dims, batch=((), ()), precision=None):
    return lax.dot_general(
        a, b, (dims, batch), precision=precision, preferred_element_type=F32
    )


NN = ((1,), (0,))
NT = ((1,), (1,))
TN = ((0,), (0,))


def body(
    grid,
    pixels,
    targets,
    masks,
    lengths,
    groups,
    latitudes,
    step_count,
    square_master,
    square_first,
    square_second,
    dense_master,
    dense_first,
    dense_second,
    head_master,
    head_first,
    head_second,
    table_master,
    table_first,
    table_second,
):
    nv, npatch = grid.nv, grid.np
    micro, items, _, cap, own_pixels = pixels.shape
    rows = micro * cap
    width = square_master.shape[1] * nv
    size = width // HEADS
    scale = size ** (-0.5)
    band, strip = square_master.shape[1:]
    ff_strip = dense_master.shape[2]
    ho = head_master.shape[1] * npatch
    base = 5 * V + cap
    table_band = table_master.shape[0]
    table_pad = -table_band % PAD
    my_band = lax.axis_index(("y", "c"))
    my_strip = lax.axis_index(("z", "x"))

    square_low = square_master.astype(BF)
    dense_low = dense_master.astype(BF)
    head_low = head_master.astype(BF)
    table_low = table_master.astype(BF)
    first = jnp.concatenate(
        [
            jnp.pad(table_low, ((0, table_pad), (0, 0))),
            square_low[2],
            square_low[3],
        ],
        axis=0,
    )
    first = grid.gather(first)
    table = whole(first[:, :, :table_band])
    start = table_band + table_pad
    wv = whole(first[:, :, start : start + band])
    wa = whole(first[:, :, start + band : start + 2 * band])
    second = grid.gather(square_low[4:8].reshape(4 * band, strip))
    wqkv = jnp.concatenate(
        [whole(second[:, :, k * band : (k + 1) * band]) for k in range(3)], axis=1
    )
    wo = whole(second[:, :, 3 * band :])
    w1 = whole(grid.gather(dense_low[0]))
    w2 = whole(grid.gather(dense_low[1]))
    head = whole(grid.gather(head_low))

    slots = jnp.arange(cap)
    lat_table = latitude_table()
    valid = masks[:, 0, 0].astype(F32) * (slots[None] < lengths[:, 0, 0][:, None]).astype(F32)[..., None]
    lat_onehot = (latitudes[:, 0, 0][..., None] == jnp.arange(LATS)).astype(F32)
    wpix = jnp.einsum("mcl,lk->mck", lat_onehot, lat_table, precision=HIGH) * valid
    weighted = jnp.tile(wpix.reshape(rows, PATCH_PIXELS), (1, V))
    count = grid.total(jnp.sum(valid))

    parts = pixels[:, :, 0]
    mine = lax.all_to_all(parts, ("y", "c"), split_axis=1, concat_axis=3, tiled=True)[:, 0]
    pix = jnp.transpose(mine.reshape(rows, V, PATCH_PIXELS), (0, 2, 1)).astype(F32)

    query = table[base + SOURCES]
    query_own = lax.dynamic_slice_in_dim(query, my_band * band, band)
    qv = dot(query_own[None], square_low[0], NN)[0]
    qv_own = grid.total(qv, ("y", "c")).astype(BF)
    col_head = (my_strip * strip + jnp.arange(strip)) // size
    head_mask = (col_head[:, None] == jnp.arange(HEADS)[None]).astype(F32)
    u_part = dot(square_low[1].astype(F32) * qv_own.astype(F32)[None], head_mask, NN, precision=HIGH)
    u_band = (grid.total(u_part, ("z", "x")) * scale).astype(BF)
    u = grid.spread(u_band, ("y", "c")).reshape(width, HEADS)
    rows_t = jnp.concatenate(
        [
            jnp.transpose(table[: PATCH_PIXELS * V].reshape(V, PATCH_PIXELS, width), (1, 0, 2)).reshape(-1, width),
            table[PATCH_PIXELS * V : base],
        ],
        axis=0,
    )
    tv = dot(rows_t, wv, NN)
    tu = dot(rows_t, u, NN)
    nk = PATCH_PIXELS * V
    n5 = nk + V
    scores = (
        jnp.einsum("ckv,kvh->chv", pix, tu[:nk].reshape(PATCH_PIXELS, V, HEADS), precision=HIGH)
        + tu[nk:n5].T[None]
        + jnp.tile(tu[n5:], (micro, 1))[:, :, None]
    )
    pa = jax.nn.softmax(scores, axis=-1)
    pal = pa.astype(BF).astype(F32)
    mass = jnp.sum(pal, axis=-1)
    fold = jnp.concatenate(
        [(pal[:, :, None] * pix[:, None]).reshape(rows, HEADS, nk), pal], axis=2
    )
    tv_heads = tv.reshape(-1, HEADS, size)
    pos_v = jnp.tile(tv_heads[n5:], (micro, 1, 1))
    agg = (
        jnp.einsum("chn,nhe->che", fold, tv_heads[:n5], precision=HIGH)
        + mass[:, :, None] * pos_v
    )
    gathered = agg.reshape(rows, width).astype(BF)

    gain_one = table[base + SOURCES + 1].astype(F32)
    gain_two = table[base + SOURCES + 2].astype(F32)
    onehot = (groups[:, 0, 0][:, None] == jnp.arange(SOURCES)).astype(F32)
    src = jnp.dot(onehot, table[base : base + SOURCES].astype(F32), precision=HIGH)
    x0 = dot(gathered, wa, NN) + jnp.repeat(src, cap, axis=0)
    h1 = layer_norm(x0, gain_one).astype(BF)
    qkv = dot(h1, wqkv, NN).astype(BF)
    q, k, vv = (
        qkv[:, i * width : (i + 1) * width].reshape(micro, cap, HEADS, size) for i in range(3)
    )
    keymask = slots[None] < lengths[:, 0, 0][:, None]
    raw = jnp.einsum("mqhe,mkhe->mhqk", q, k, preferred_element_type=F32) * scale
    probs = jax.nn.softmax(jnp.where(keymask[:, None, None], raw, -1e30), axis=-1)
    probs_low = probs.astype(BF)
    o = jnp.einsum("mhqk,mkhe->mqhe", probs_low, vv, preferred_element_type=F32)
    o = o.reshape(rows, width).astype(BF)
    x1 = x0 + dot(o, wo, NN)
    h2 = layer_norm(x1, gain_two).astype(BF)
    f = dot(h2, w1, NN)
    act = exact_gelu(f).astype(BF)
    x2 = x1 + dot(act, w2, NT)
    x2_low = x2.astype(BF)
    pred = dot(x2_low, head, NN)
    diff = pred - targets[:, 0, 0].astype(F32).reshape(rows, ho)
    loss_local = jnp.sum(weighted * diff * diff)
    dpred = (2.0 * weighted * diff / count).astype(BF)

    d_head = dot(x2_low, dpred, TN)
    dx2 = dot(dpred, head, NT)
    dx2_low = dx2.astype(BF)
    d_down = dot(dx2_low, act, TN)
    dact = dot(dx2_low, w2, NN)
    _, gelu_back = jax.vjp(exact_gelu, f)
    df = gelu_back(dact)[0].astype(BF)
    d_up = dot(h2, df, TN)
    dh2 = dot(df, w1, NT)
    _, norm_back = jax.vjp(layer_norm, x1, gain_two)
    dx1n, d_gain_two = norm_back(dh2)
    dx1 = dx2 + dx1n
    dx1_low = dx1.astype(BF)
    d_wo = dot(o, dx1_low, TN)
    do = dot(dx1_low, wo, NT).astype(BF).reshape(micro, cap, HEADS, size)
    dprobs = jnp.einsum("mqhe,mkhe->mhqk", do, vv, preferred_element_type=F32)
    dvv = jnp.einsum("mhqk,mqhe->mkhe", probs_low, do, preferred_element_type=F32)
    ds = (probs * (dprobs - jnp.sum(probs * dprobs, axis=-1, keepdims=True))).astype(BF)
    dq = jnp.einsum("mhqk,mkhe->mqhe", ds, k, preferred_element_type=F32) * scale
    dk = jnp.einsum("mhqk,mqhe->mkhe", ds, q, preferred_element_type=F32) * scale
    dqkv = jnp.concatenate([t.reshape(rows, width) for t in (dq, dk, dvv)], axis=1).astype(BF)
    d_wqkv = dot(h1, dqkv, TN)
    dh1 = dot(dqkv, wqkv, NT)
    _, norm_back = jax.vjp(layer_norm, x0, gain_one)
    dx0n, d_gain_one = norm_back(dh1)
    dx0 = dx1 + dx0n
    d_src = jnp.dot(onehot.T, jnp.sum(dx0.reshape(micro, cap, width), axis=1), precision=HIGH)
    dx0_low = dx0.astype(BF)
    d_wa = dot(gathered, dx0_low, TN)
    dagg = dot(dx0_low, wa, NT).astype(BF).astype(F32).reshape(rows, HEADS, size)

    dfold = jnp.einsum("che,nhe->chn", dagg, tv_heads[:n5], precision=HIGH)
    dpal = (
        jnp.sum(dfold[:, :, :nk].reshape(rows, HEADS, PATCH_PIXELS, V) * pix[:, None], axis=2)
        + dfold[:, :, nk:]
        + jnp.sum(dagg * pos_v, axis=-1)[:, :, None]
    )
    dsv = (pa * (dpal - jnp.sum(pa * dpal, axis=-1, keepdims=True))).astype(BF).astype(F32)
    g_rows = jnp.einsum("chn,che->nhe", fold, dagg, precision=HIGH).reshape(n5, width)
    g_pos = jnp.sum((mass[:, :, None] * dagg).reshape(micro, cap, width), axis=0)
    s_rows = jnp.concatenate(
        [
            jnp.einsum("ckv,chv->kvh", pix, dsv, precision=HIGH).reshape(nk, HEADS),
            jnp.sum(dsv, axis=0).T,
            jnp.sum(jnp.sum(dsv, axis=-1).reshape(micro, cap, HEADS), axis=0),
        ],
        axis=0,
    )
    g_table = jnp.concatenate(
        [
            jnp.transpose(g_rows[:nk].reshape(PATCH_PIXELS, V, width), (1, 0, 2)).reshape(nk, width),
            g_rows[nk:],
            g_pos,
            d_src,
            jnp.zeros((1, width), F32),
            d_gain_one[None],
            d_gain_two[None],
        ],
        axis=0,
    )
    s_table = jnp.concatenate(
        [
            jnp.transpose(s_rows[:nk].reshape(PATCH_PIXELS, V, HEADS), (1, 0, 2)).reshape(nk, HEADS),
            s_rows[nk:],
        ],
        axis=0,
    )

    def to_owner(value):
        return grid.scatter(chunked(value.astype(BF), nv, npatch))

    down_sum = to_owner(d_down)
    up_sum = to_owner(d_up)
    s_sum = grid.total(s_table)
    low_part = jnp.concatenate(
        [
            jnp.pad(chunked(g_table.astype(BF), nv, npatch), ((0, 0), (0, 0), (0, table_pad), (0, 0))),
            chunked(d_wa.astype(BF), nv, npatch),
        ],
        axis=2,
    )
    low_sum = grid.scatter(low_part)
    g_own = low_sum[:table_band]
    wa_sum = low_sum[table_band + table_pad :]
    attn_sum = grid.scatter(
        jnp.concatenate(
            [chunked(d_wqkv[:, i * width : (i + 1) * width].astype(BF), nv, npatch) for i in range(3)]
            + [chunked(d_wo.astype(BF), nv, npatch)],
            axis=2,
        )
    )
    head_sum = to_owner(d_head)

    g_low = g_own.astype(BF)
    g_column = grid.spread(g_low, ("y", "c")).reshape(nv * table_band, strip)[:base]
    g_line = jnp.transpose(grid.spread(g_low, ("z", "x")), (1, 0, 2)).reshape(table_band, width)
    table_own_band = lax.dynamic_slice_in_dim(table, my_band * band, band, 1)
    value_sum = dot(table_own_band[:base], g_column, TN)
    du_own = dot(table_own_band[:base].astype(F32), s_sum, TN, precision=HIGH)
    du_cols = dot(du_own, head_mask, NT, precision=HIGH)
    key_sum = du_cols * qv_own.astype(F32)[None] * scale
    dqv = grid.total(jnp.sum(square_low[1].astype(F32) * du_cols, axis=0) * scale, ("y", "c"))
    query_sum = query_own.astype(F32)[:, None] * dqv[None]
    dquery = jnp.sum(square_low[0].astype(F32) * dqv[None], axis=1)
    dquery = lax.dynamic_update_slice_in_dim(jnp.zeros((width,), F32), dquery, my_band * band, 0)
    dquery = grid.total(dquery)
    table_row = my_band * table_band + jnp.arange(table_band)
    s_pad = jnp.pad(s_sum, ((0, nv * table_band - base), (0, 0)))
    s_own = lax.dynamic_slice_in_dim(s_pad, my_band * table_band, table_band, 0)
    wv_rows = lax.dynamic_slice_in_dim(wv, my_strip * strip, strip, 0)
    u_rows = lax.dynamic_slice_in_dim(u, my_strip * strip, strip, 0)
    d_rows = dot(g_line, wv_rows, NT) + dot(s_own, u_rows.astype(F32), NT, precision=HIGH)
    dq_own = lax.dynamic_slice_in_dim(dquery, my_strip * strip, strip, 0)
    table_sum = jnp.where((table_row < base)[:, None], d_rows, g_own)
    table_sum = jnp.where((table_row == base + SOURCES)[:, None], dq_own[None], table_sum)
    square_sum = jnp.concatenate(
        [query_sum[None], key_sum[None], value_sum[None], wa_sum[None], attn_sum.reshape(4, band, strip)],
        axis=0,
    )
    dense_sum = jnp.stack([up_sum, down_sum])
    shards = (square_sum, dense_sum, head_sum, table_sum)
    sumsq = sum(jnp.sum(s * s) for s in shards)
    both = grid.total(jnp.stack([loss_local, sumsq]))
    loss = both[0] / count
    norm = jnp.sqrt(both[1])
    factor = jnp.minimum(1.0, CLIP_AT / norm)
    steps = step_count[0].astype(F32)
    sq = adam_update(square_master, square_first, square_second, shards[0], factor, steps, LEARN_RATE)
    de = adam_update(dense_master, dense_first, dense_second, shards[1], factor, steps, LEARN_RATE)
    hd = adam_update(head_master, head_first, head_second, shards[2], factor, steps, LEARN_RATE)
    tb = adam_update(table_master, table_first, table_second, shards[3], factor, steps, TABLE_RATE)
    return (loss, norm, *sq, *de, *hd, *tb)


NZ = 4
BANDS = 4
STRIPS = 8
NT_DIMS = (((1,), (1,)), ((), ()))
NN_DIMS = (((1,), (0,)), ((), ()))
TN_DIMS = (((0,), (0,)), ((), ()))
VMEM_LIMIT = 56 * 1024 * 1024


def mm(a, b):
    return lax.dot_general(a, b, NN_DIMS, preferred_element_type=F32)


def mm_nt(a, b):
    return lax.dot_general(a, b, NT_DIMS, preferred_element_type=F32)


def mm_tn(a, b):
    return lax.dot_general(a, b, TN_DIMS, preferred_element_type=F32)


def zflip(k):
    return (k % 2) * 2 + k // 2


def span(index, extent):
    return pl.ds(pl.multiple_of(index * extent, extent), extent)


def spots(core):
    out = []
    for owner in (core, 1 - core):
        for a in range(2):
            for b in range(2):
                out.append((a, b, owner) if owner == 0 else (b, a, owner))
    return out


def by_core(co, fn):
    for core in range(2):

        @pl.when(co[1] == core)
        def _(core=core):
            fn(core)


def forward_step(co, k, x_ref, chunks, row, band, w, put):
    back = co[2] ^ zflip(k)

    def run(core):
        places = spots(core)
        for fx in range(2):
            total = None
            for index, (fy, px, owner) in enumerate(places):
                if px != fx:
                    continue
                r = (co[0] ^ fy) * 2 + owner
                part = mm(x_ref[:, span(r, band)], chunks[index][0, row : row + band])
                total = part if total is None else total + part
            put(back * 2 + (co[3] ^ fx), total)

    by_core(co, run)


def backward_step(co, k, dy_ref, chunks, row, band, w, acc_ref, fresh):
    back = co[2] ^ zflip(k)

    def run(core):
        places = spots(core)
        for owner in range(2):
            for fy in range(2):
                total = None
                for index, (py, fx, who) in enumerate(places):
                    if (py, who) != (fy, owner):
                        continue
                    p = back * 2 + (co[3] ^ fx)
                    part = mm_nt(dy_ref[:, span(p, w)], chunks[index][0, row : row + band])
                    total = part if total is None else total + part
                r = (co[0] ^ fy) * 2 + owner

                @pl.when(fresh)
                def _():
                    acc_ref[:, span(r, band)] = total

                @pl.when(jnp.logical_not(fresh))
                def _():
                    acc_ref[:, span(r, band)] += total

    by_core(co, run)


def by_place(co, fn):
    for core in range(2):
        for x in range(2):

            @pl.when((co[1] == core) & (co[3] == x))
            def _(core=core, x=x):
                fn(core, x)


def pair_of(chunks, core, x, flip_y, owner, rows):
    found = [None, None]
    for index, (fy, fx, who) in enumerate(spots(core)):
        if (fy, who) == (flip_y, owner):
            found[fx ^ x] = chunks[index][0, rows]
    return jnp.concatenate(found, axis=1)


def forward_pair(co, k, x_ref, chunks, row, band, put):
    back = co[2] ^ zflip(k)

    def run(core, x):
        total = None
        for owner in range(2):
            for fy in range(2):
                r = (co[0] ^ fy) * 2 + owner
                w = pair_of(chunks, core, x, fy, owner, slice(row, row + band))
                part = mm(x_ref[:, span(r, band)], w)
                total = part if total is None else total + part
        put(back, total)

    by_place(co, run)


def backward_pair(co, k, dy_ref, chunks, parts, band, acc_ref, fresh):
    back = co[2] ^ zflip(k)
    width = dy_ref.shape[1] // parts

    def run(core, x):
        for owner in range(2):
            for fy in range(2):
                total = None
                for part in range(parts):
                    w = pair_of(chunks, core, x, fy, owner, slice(part * band, (part + 1) * band))
                    col = pl.multiple_of(part * width + back * 256, 256)
                    got = mm_nt(dy_ref[:, pl.ds(col, 256)], w)
                    total = got if total is None else total + got
                r = (co[0] ^ fy) * 2 + owner

                @pl.when(fresh)
                def _():
                    acc_ref[:, span(r, band)] = total

                @pl.when(jnp.logical_not(fresh))
                def _():
                    acc_ref[:, span(r, band)] += total

    by_place(co, run)


def smem():
    return pl.BlockSpec(memory_space=pltpu.SMEM)


def full(shape):
    zeros = (0,) * len(shape)
    return pl.BlockSpec(shape, lambda i: zeros)


def steps_of(rows, w, first=0, block=0):
    def at(b):
        return pl.BlockSpec(
            (1, rows, w), lambda i: (b * NZ + jnp.clip(i - first, 0, NZ - 1), block, 0)
        )

    return [at(0), at(1)] * 4


def twice(arrays):
    return [v for v in arrays for _ in range(2)]


def call(kernel, name, grid, in_specs, outs, out_specs, scratch, flops, moved, *args):
    return pl.pallas_call(
        kernel,
        name=name,
        grid=grid,
        in_specs=in_specs,
        out_shape=outs,
        out_specs=out_specs,
        scratch_shapes=scratch,
        compiler_params=pltpu.CompilerParams(
            vmem_limit_bytes=VMEM_LIMIT
        ),
        cost_estimate=pl.CostEstimate(flops=flops, bytes_accessed=moved, transcendentals=0),
    )(*args)


def shape(*dims, dtype=F32):
    return jax.ShapeDtypeStruct(dims, dtype)


def norm(value, gain):
    center = value - jnp.mean(value, axis=-1, keepdims=True)
    spread = jnp.mean(center * center, axis=-1, keepdims=True)
    return center * lax.rsqrt(spread + NORM_EPSILON) * gain


def norm_grad(value, gain, grad):
    center = value - jnp.mean(value, axis=-1, keepdims=True)
    spread = jnp.mean(center * center, axis=-1, keepdims=True)
    inverse = lax.rsqrt(spread + NORM_EPSILON)
    unit = center * inverse
    inner = grad * gain
    out = inverse * (
        inner
        - jnp.mean(inner, axis=-1, keepdims=True)
        - unit * jnp.mean(inner * unit, axis=-1, keepdims=True)
    )
    return out, jnp.sum(grad * unit, axis=0, keepdims=True)


def half_masks(rows):
    lane = lax.broadcasted_iota(jnp.int32, (rows, 128), 1)
    return [(lane < 64).astype(BF), (lane >= 64).astype(BF)]


def assemble_kernel(co, *refs, band, offset, tall, extra):
    chunks, (table_ref, more_ref, value_ref) = refs[:8], refs[8:]
    k = pl.program_id(0)
    back = co[2] ^ zflip(k)

    def run(core):
        for index, (fy, fx, owner) in enumerate(spots(core)):
            r = (co[0] ^ fy) * 2 + owner
            p = back * 2 + (co[3] ^ fx)
            table_ref[span(r, tall), span(p, 128)] = chunks[index][0, offset : offset + tall]
            more = chunks[index][0, offset + tall : offset + tall + extra].astype(F32)
            half = extra // 2
            for part in range(2):
                col = pl.multiple_of(r * band + part * 128, 128)
                more_ref[span(p, half), pl.ds(col, 128)] = more[part * half : (part + 1) * half]
            value_ref[span(r, band), span(p, 128)] = chunks[index][0, :band]

    by_core(co, run)


def square_kernel(co, *refs, band):
    chunks, outs = refs[:8], refs[8:]
    k = pl.program_id(0)

    def run(core):
        for index, (fy, fx, owner) in enumerate(spots(core)):
            r = (co[0] ^ fy) * 2 + owner
            p = (co[2] ^ zflip(k)) * 2 + (co[3] ^ fx)
            for part, out_ref in enumerate(outs):
                out_ref[span(r, band), span(p, 128)] = chunks[index][0, part * band : (part + 1) * band]

    by_core(co, run)


def product_kernel(co, x_ref, *refs, band):
    chunks, out_ref = refs[:8], refs[8]

    def put(p, total):
        out_ref[:, span(p, 256)] = total.astype(out_ref.dtype)

    forward_pair(co, pl.program_id(0), x_ref, chunks, 0, band, put)


def pool_kernel(x_ref, e_ref, tu_ref, tv_ref, agg_ref, a_ref, pa_ref):
    j = pl.program_id(0)
    x, e = x_ref[...], e_ref[...]
    wide_x, wide_e = x.astype(F32), e.astype(F32)
    rows, n = x.shape
    masks = half_masks(n)
    lane = lax.broadcasted_iota(jnp.int32, (n, 128), 1)
    keep = lax.broadcasted_iota(jnp.int32, (rows, 128), 1) < V
    for pair in range(2):
        total = None
        for half in range(2):
            head = 2 * pair + half
            column = jnp.sum(jnp.where(lane == 4 * j + head, tu_ref[...], 0.0), axis=1, keepdims=True)
            m = wide_e * column
            high = m.astype(BF)
            rest = (m - high.astype(F32)).astype(BF)
            s = mm(x, high) + mm(x, rest)
            s = jnp.where(keep, s, -1e30)
            s = jnp.exp(s - jnp.max(s, axis=-1, keepdims=True))
            pa = s * (1.0 / jnp.sum(s, axis=-1, keepdims=True))
            wide = mm_nt(pa.astype(BF), e)
            a = (wide_x * wide).astype(BF)
            pa_ref[head] = pa
            a_ref[head] = a
            part = mm(a, tv_ref[:, pair * 128 : (pair + 1) * 128] * masks[half])
            total = part if total is None else total + part
        agg_ref[:, pair * 128 : (pair + 1) * 128] = total.astype(BF)


def enter_kernel(co, agg_ref, src_ref, gain_ref, *refs, band):
    chunks, (x0_ref, h1_ref) = refs[:8], refs[8:]
    k = pl.program_id(0)

    def put(p, total):
        x0_ref[:, span(p, 256)] = total

    forward_pair(co, k, agg_ref, chunks, 0, band, put)

    @pl.when(k == NZ - 1)
    def _():
        cap = x0_ref.shape[0] // src_ref.shape[0]
        for m in range(src_ref.shape[0]):
            x0_ref[m * cap : (m + 1) * cap] += src_ref[m : m + 1]
        h1_ref[...] = norm(x0_ref[...], gain_ref[...]).astype(BF)


def attend_kernel(co, lens, x0_ref, h1_ref, gain_ref, *refs, band, scale):
    qkv_chunks, o_chunks = refs[:8], refs[8:16]
    qkv_ref, p_ref, o_ref, x1_ref, h2_ref = refs[16:]
    i = pl.program_id(0)
    micro = lens.shape[0]
    width = x0_ref.shape[1]
    cap = x0_ref.shape[0] // micro

    @pl.when(i < NZ)
    def _():
        for part in range(3):

            def put(p, total, part=part):
                col = pl.multiple_of(part * width + p * 256, 256)
                qkv_ref[:, pl.ds(col, 256)] = total.astype(BF)

            forward_pair(co, i, h1_ref, qkv_chunks, part * band, band, put)

    @pl.when(i == NZ - 1)
    def _():
        masks = half_masks(cap)
        key = lax.broadcasted_iota(jnp.int32, (cap, cap), 1)

        @pl.loop(0, width // 128, unroll=2)
        def _(j):
            for m in range(micro):
                rows = slice(m * cap, (m + 1) * cap)
                q = qkv_ref[rows, span(j, 128)]
                kk = qkv_ref[rows, pl.ds(pl.multiple_of(width + j * 128, 128), 128)]
                vv = qkv_ref[rows, pl.ds(pl.multiple_of(2 * width + j * 128, 128), 128)]
                total = None
                for half in range(2):
                    s = mm_nt(q * masks[half], kk) * scale
                    s = jnp.where(key < lens[m], s, -1e30)
                    s = jnp.exp(s - jnp.max(s, axis=-1, keepdims=True))
                    p = s * (1.0 / jnp.sum(s, axis=-1, keepdims=True))
                    p_ref[2 * j + half, m] = p
                    part = mm(p.astype(BF), vv * masks[half])
                    total = part if total is None else total + part
                o_ref[rows, span(j, 128)] = total.astype(BF)

    @pl.when(i >= NZ)
    def _():
        def put(p, total):
            x1_ref[:, span(p, 256)] = x0_ref[:, span(p, 256)] + total

        forward_pair(co, i - NZ, o_ref, o_chunks, 0, band, put)

    @pl.when(i == 2 * NZ - 1)
    def _():
        h2_ref[...] = norm(x1_ref[...], gain_ref[...]).astype(BF)


def up_kernel(co, h2_ref, *refs, band, w):
    chunks, (act_ref, slope_ref) = refs[:8], refs[8:]

    def put(p, f):
        bell = jnp.exp(-0.5 * f * f)
        t = 1.0 / (1.0 + (0.3275911 * 0.5**0.5) * jnp.abs(f))
        tail = t * (1.061405429 * 0.5)
        for term in (-1.453152027, 1.421413741, -0.284496736, 0.254829592):
            tail = t * (0.5 * term + tail)
        tail = tail * bell
        share = jnp.where(f < 0.0, tail, 1.0 - tail)
        act_ref[:, span(p, w)] = (f * share).astype(BF)
        slope_ref[:, span(p, w)] = (share + f * bell * ((2.0 * math.pi) ** -0.5)).astype(BF)

    forward_step(co, pl.program_id(0), h2_ref, chunks, 0, band, w, put)


def down_kernel(co, count, x1_ref, act_ref, slope_ref, head_ref, target_ref, weight_ref, *refs, band, w):
    chunks = refs[:8]
    loss_ref, dx2_ref, dx2_low_ref, dhead_ref, df_ref = refs[8:13]
    acc_ref = refs[13]
    i = pl.program_id(0)

    @pl.when(i < NZ)
    def _():
        backward_step(co, i, act_ref, chunks, 0, band, w, acc_ref, i == 0)

    @pl.when(i == NZ - 1)
    def _():
        x2 = (x1_ref[...] + acc_ref[...]).astype(BF)
        head = head_ref[...].astype(BF)
        diff = mm_nt(x2, head) - target_ref[...].astype(F32)
        weighted = weight_ref[...] * diff
        loss_ref[...] = jnp.broadcast_to(jnp.sum(weighted * diff), loss_ref.shape)
        dpred = (2.0 * weighted / count[0]).astype(BF)
        dhead_ref[...] = mm_tn(dpred, x2)
        dx2 = mm(dpred, head)
        dx2_ref[...] = dx2
        dx2_low_ref[...] = dx2.astype(BF)

    @pl.when(i >= NZ)
    def _():
        def put(p, dact):
            df_ref[:, span(p, w)] = (dact * slope_ref[:, span(p, w)].astype(F32)).astype(BF)

        forward_step(co, i - NZ, dx2_low_ref, chunks, 0, band, w, put)


def owner_place(co, i, owner):
    a, b, k = i // (2 * NZ), (i // NZ) % 2, i % NZ
    fy = jnp.where(owner == 0, a, b)
    fx = jnp.where(owner == 0, b, a)
    return (co[0] ^ fy) * 2 + owner, (co[2] ^ zflip(k)) * 2 + (co[3] ^ fx)


def targets(co, keep_ref, send_ref):
    return [
        (out, owner, j)
        for out, owner in ((keep_ref, co[1]), (send_ref, 1 - co[1]))
        for j in range(NZ)
    ]


def grad_kernel(co, x_ref, dy_ref, keep_ref, send_ref, xt_ref, *, band, w):
    i = pl.program_id(0)

    @pl.when(i == 0)
    def _():
        xt_ref[...] = x_ref[...].T

    for out_ref, owner, j in targets(co, keep_ref, send_ref):
        r, p = owner_place(co, i * NZ + j, owner)
        out_ref[j] = mm(xt_ref[span(r, band)], dy_ref[:, span(p, w)]).astype(BF)


def pair_places(co, k, keep_ref, send_ref):
    out = []
    for out_ref, owner in ((keep_ref, co[1]), (send_ref, 1 - co[1])):
        for fy in range(2):
            at = []
            for half in range(2):
                fx = co[3] ^ half
                at.append(jnp.where(owner == 0, fy * 2 + fx, fx * 2 + fy))
            out.append((out_ref, (co[0] ^ fy) * 2 + owner, co[2] ^ zflip(k), at))
    return out


def attention_grad_kernel(co, h1_ref, o_ref, dqkv_ref, dx1_ref, keep_ref, send_ref, ht_ref, ot_ref, *, band):
    k = pl.program_id(0)
    width = h1_ref.shape[1]

    @pl.when(k == 0)
    def _():
        ht_ref[...] = h1_ref[...].T
        ot_ref[...] = o_ref[...].T

    for out_ref, r, back, at in pair_places(co, k, keep_ref, send_ref):
        for part in range(4):
            if part < 3:
                col = pl.multiple_of(part * width + back * 256, 256)
                got = mm(ht_ref[span(r, band)], dqkv_ref[:, pl.ds(col, 256)])
            else:
                got = mm(ot_ref[span(r, band)], dx1_ref[:, span(back, 256)])
            for half in range(2):
                out_ref[at[half], 0, part * band : (part + 1) * band] = got[
                    :, half * 128 : (half + 1) * 128
                ].astype(BF)


def low_grad_kernel(
    co, groups, agg_ref, dx0_ref, g_ref, sum_ref, gain_ref, head_ref, keep_ref, send_ref, at_ref, gl_ref, *, band, tall, top
):
    k = pl.program_id(0)
    n = g_ref.shape[0]
    piece = head_ref.shape[0] // STRIPS

    @pl.when(k == 0)
    def _():
        at_ref[...] = agg_ref[...].T
        gl_ref[: n - 16] = g_ref[: n - 16].astype(BF)
        last = g_ref[n - 16 :]
        row = lax.broadcasted_iota(jnp.int32, last.shape, 0)
        for m in range(sum_ref.shape[0]):
            last += jnp.where(row == top + groups[m], sum_ref[m : m + 1], 0.0)
        for m in range(2):
            last += jnp.where(row == top + SOURCES + 1 + m, gain_ref[m : m + 1], 0.0)
        gl_ref[n - 16 :] = last.astype(BF)

    for out_ref, r, back, at in pair_places(co, k, keep_ref, send_ref):
        got = mm(at_ref[span(r, band)], dx0_ref[:, span(back, 256)])
        for half in range(2):
            p = back * 2 + half
            out_ref[at[half], 0, :band] = got[:, half * 128 : (half + 1) * 128].astype(BF)
            out_ref[at[half], 0, band : band + tall] = gl_ref[span(r, tall), span(p, 128)]
            head = [
                head_ref[span(p, piece), pl.ds(pl.multiple_of(r * band + part * 128, 128), 128)]
                for part in range(2)
            ]
            out_ref[at[half], 0, band + tall :] = jnp.concatenate(head, axis=0).astype(BF)


def up_back_kernel(co, df_ref, x1_ref, gain_ref, dx2_ref, *refs, band, w):
    chunks, (dx1_ref, dx1_low_ref, dgain_ref, acc_ref) = refs[:8], refs[8:]
    k = pl.program_id(0)
    backward_step(co, k, df_ref, chunks, 0, band, w, acc_ref, k == 0)

    @pl.when(k == NZ - 1)
    def _():
        out, dgain = norm_grad(x1_ref[...], gain_ref[...], acc_ref[...])
        dx1 = dx2_ref[...] + out
        dx1_ref[...] = dx1
        dx1_low_ref[...] = dx1.astype(BF)
        dgain_ref[...] = dgain


def attend_back_kernel(co, dx1_low_ref, qkv_ref, p_ref, *refs, band, scale):
    o_chunks = refs[:8]
    dqkv_ref, acc_ref, do_ref = refs[8:]
    i = pl.program_id(0)
    micro = p_ref.shape[1]
    width = dx1_low_ref.shape[1]
    cap = dx1_low_ref.shape[0] // micro

    @pl.when(i < NZ)
    def _():
        backward_pair(co, i, dx1_low_ref, o_chunks, 1, band, acc_ref, i == 0)

    @pl.when(i == NZ - 1)
    def _():
        do_ref[...] = acc_ref[...].astype(BF)
        masks = half_masks(cap)

        @pl.loop(0, width // 128, unroll=2)
        def _(j):
            for m in range(micro):
                rows = slice(m * cap, (m + 1) * cap)
                k_at = pl.ds(pl.multiple_of(width + j * 128, 128), 128)
                v_at = pl.ds(pl.multiple_of(2 * width + j * 128, 128), 128)
                q, kk, vv = qkv_ref[rows, span(j, 128)], qkv_ref[rows, k_at], qkv_ref[rows, v_at]
                do = do_ref[rows, span(j, 128)]
                dq = dk = dv = None
                for half in range(2):
                    p = p_ref[2 * j + half, m]
                    do_half = do * masks[half]
                    dp = mm_nt(do_half, vv)
                    moved = p * dp
                    ds = (moved - p * jnp.sum(moved, axis=-1, keepdims=True)).astype(BF)
                    parts = (
                        mm(ds, kk * masks[half]),
                        mm_tn(ds, q * masks[half]),
                        mm_tn(p.astype(BF), do_half),
                    )
                    if dq is None:
                        dq, dk, dv = parts
                    else:
                        dq, dk, dv = dq + parts[0], dk + parts[1], dv + parts[2]
                dqkv_ref[rows, span(j, 128)] = (dq * scale).astype(BF)
                dqkv_ref[rows, k_at] = (dk * scale).astype(BF)
                dqkv_ref[rows, v_at] = dv.astype(BF)


def leave_kernel(co, dx1_ref, dqkv_ref, x0_ref, gain_ref, *refs, band):
    qkv_chunks, a_chunks = refs[:8], refs[8:16]
    dx0_low_ref, dgain_ref, dsum_ref, dagg_ref, acc_ref = refs[16:]
    i = pl.program_id(0)
    micro = dsum_ref.shape[0]
    width = x0_ref.shape[1]
    cap = x0_ref.shape[0] // micro

    @pl.when(i < NZ)
    def _():
        backward_pair(co, i, dqkv_ref, qkv_chunks, 3, band, acc_ref, i == 0)

    @pl.when(i == NZ - 1)
    def _():
        out, dgain = norm_grad(x0_ref[...], gain_ref[...], acc_ref[...])
        dx0 = dx1_ref[...] + out
        dx0_low_ref[...] = dx0.astype(BF)
        dgain_ref[...] = dgain
        for m in range(micro):
            dsum_ref[m : m + 1] = jnp.sum(dx0[m * cap : (m + 1) * cap], axis=0, keepdims=True)

    @pl.when(i >= NZ)
    def _():
        backward_pair(co, i - NZ, dx0_low_ref, a_chunks, 1, band, acc_ref, i == NZ)

    @pl.when(i == 2 * NZ - 1)
    def _():
        dagg_ref[...] = acc_ref[...].astype(BF)


def pool_back_kernel(x_ref, e_ref, tv_ref, a_ref, pa_ref, dagg_ref, g_ref, s_ref):
    x, e = x_ref[...].astype(F32), e_ref[...]
    masks = half_masks(x.shape[0])
    for pair in range(2):
        at = slice(pair * 128, (pair + 1) * 128)
        total = None
        for half in range(2):
            head = 2 * pair + half
            part = dagg_ref[:, at] * masks[half]
            dpal = mm((mm_nt(part, tv_ref[:, at]) * x).astype(BF), e)
            pa = pa_ref[head]
            inner = pa * dpal
            ds = (inner - pa * jnp.sum(inner, axis=-1, keepdims=True)).astype(BF)
            s_ref[0, head : head + 1] = jnp.sum(mm_nt(ds, e) * x, axis=0, keepdims=True)
            got = mm_tn(a_ref[head], part)
            total = got if total is None else total + got
        g_ref[:, at] = total


def table_layout(cap, band, tall):
    n = BANDS * tall
    nk = PATCH_PIXELS * V
    select = np.zeros((nk, n), np.float32)
    fixed = np.zeros((cap, n), np.float32)
    var_of = np.zeros((n, 128), np.float32)
    for row in range(5 * V + cap):
        lane = (row // band) * tall + row % band
        if row < nk:
            select[row, lane] = 1.0
            var_of[lane, row // PATCH_PIXELS] = 1.0
        elif row < 5 * V:
            fixed[:, lane] = 1.0
            var_of[lane, row - nk] = 1.0
        else:
            fixed[row - 5 * V, lane] = 1.0
            var_of[lane, :V] = 1.0
    return select, fixed, var_of


def fast_body(
    grid,
    pixels,
    targets,
    masks,
    lengths,
    groups,
    latitudes,
    step_count,
    square_master,
    square_first,
    square_second,
    dense_master,
    dense_first,
    dense_second,
    head_master,
    head_first,
    head_second,
    table_master,
    table_first,
    table_second,
):
    micro, items, _, cap, own_pixels = pixels.shape
    rows = micro * cap
    band, strip = square_master.shape[1:]
    width = band * BANDS
    size = width // HEADS
    scale = size ** (-0.5)
    w = dense_master.shape[2]
    ff = w * STRIPS
    ho = head_master.shape[1] * STRIPS
    base = 5 * V + cap
    table_band = table_master.shape[0]
    tall = table_band + -table_band % 16
    n = BANDS * tall
    head_rows = head_master.size // strip
    y, c, z, x = (lax.axis_index(a) for a in AXES)
    co = jnp.stack([y, c, z, x]).astype(jnp.int32)
    my_band = y * 2 + c
    my_strip = z * 2 + x
    select, fixed, var_of = table_layout(cap, table_band, tall)

    def lane_of(row):
        return (row // table_band) * tall + row % table_band

    square_low = square_master.astype(BF)
    dense_low = dense_master.astype(BF)
    low_rows = 2 * band + tall + head_rows
    low = jnp.concatenate(
        [
            square_low[2],
            square_low[3],
            jnp.pad(table_master.astype(BF), ((0, tall - table_band), (0, 0))),
            jnp.transpose(
                head_master.astype(BF).T.reshape(ho // STRIPS, 2, strip), (1, 0, 2)
            ).reshape(head_rows, strip),
        ],
        axis=0,
    )
    attn = square_low[4:8].reshape(4 * band, strip)
    slots = jnp.arange(cap)
    lens = lengths[:, 0, 0]
    valid = masks[:, 0, 0].astype(F32) * (slots[None] < lens[:, None]).astype(F32)[..., None]
    lat_onehot = (latitudes[:, 0, 0][..., None] == jnp.arange(LATS)).astype(F32)
    wpix = jnp.einsum("mcl,lk->mck", lat_onehot, latitude_table(), precision=HIGH) * valid
    weighted = jnp.tile(wpix.reshape(rows, PATCH_PIXELS), (1, V))
    var_of = jnp.asarray(var_of, BF)
    query_row = base + SOURCES
    col_head = (my_strip * strip + jnp.arange(strip)) // size
    head_mask = (col_head[:, None] == jnp.arange(HEADS)[None]).astype(F32)
    wide, line, one = full((rows, width)), full((1, width)), shape(1, width)
    pair = pl.BlockSpec((rows, 256), lambda j: (0, j))
    src_at = lane_of(base)
    row = jnp.where(my_band == query_row // table_band, 1.0, 0.0) * table_master[query_row % table_band]
    first_pack = lax.dynamic_update_slice_in_dim(
        jnp.zeros((width,), F32), row.astype(BF).astype(F32), my_strip * strip, 0
    )
    first_pack = jnp.concatenate([first_pack, jnp.broadcast_to(jnp.sum(valid), (128,))])

    bundles = [low, attn, dense_low[0], dense_low[1], square_low[:2].reshape(2 * band, strip)]
    stack, join = lambda i, v: jnp.stack([bundles[i], v]), lambda a, b: jnp.concatenate([a, b], axis=0)
    z2, z1, near, far, core = grid.far_z, grid.next_z, grid.near, grid.far, grid.core
    (a0,) = grid.begin([], (z2, bundles[0]))
    first_pack = grid.hop(grid.gate(first_pack, [a0]), ("z", 1), ("z", 2))
    p0 = stack(0, a0)
    b0, a1 = got = grid.begin([a0, first_pack], (z1, p0), (z2, bundles[1]))
    l0, p1 = join(p0, b0), stack(1, a1)
    pack = grid.hop(first_pack, ("x", 1))
    pack = grid.hop(pack, ("y", 1), ("c", 1))
    query, count = pack[:width].astype(BF), pack[width]
    query_own = lax.dynamic_slice_in_dim(query, my_band * band, band)
    spread = jnp.tile(jnp.asarray(fixed), (micro, 1))
    for fy in range(2):
        for fc in range(2):
            other = (y ^ fy) * 2 + (c ^ fc)
            piece = lax.dynamic_index_in_dim(pixels[:, :, 0], other, 1, False)
            if fy or fc:
                piece = grid.permute(piece, lambda a, b, d, e, fy=fy, fc=fc: (a ^ fy, b ^ fc, d, e))
            pick = lax.dynamic_slice_in_dim(
                jnp.asarray(select, BF), other * own_pixels, own_pixels, 0
            )
            spread = spread + mm(piece.reshape(rows, own_pixels), pick)
    spread = spread.astype(BF)
    qv = dot(query_own[None], square_low[0], NN)[0]
    qv_own = grid.hop(qv, ("y", 1), ("c", 1)).astype(BF)
    u_part = dot(square_low[1].astype(F32) * qv_own.astype(F32)[None], head_mask, NN, precision=HIGH)
    u_part = lax.dynamic_update_slice_in_dim(jnp.zeros((width, HEADS), F32), u_part, my_band * band, 0)
    u_part = grid.hop(u_part, ("x", 1))
    n0, b1 = got = grid.begin([got, qv_own, spread], (near, l0), (z1, p1))
    f0, l1 = join(l0, n0), join(p1, b1)
    u_part = grid.hop(u_part, ("y", 1), ("c", 1), ("z", 1))
    r0, n1, a2 = got = grid.begin([got, u_part], (far, f0), (near, l1), (z2, bundles[2]))
    f1, p2 = join(l1, n1), stack(2, a2)
    (b2,) = grid.begin([], (z1, p2))
    l2 = join(p2, b2)
    c0, d0, r1, a3 = got = grid.begin(
        [got, b2, u_part], (core, f0), (core, r0), (far, f1), (z2, bundles[3])
    )
    p3 = stack(3, a3)
    u_part = grid.hop(u_part, ("z", 2))
    low = twice([f0, r0, c0, d0])
    n2, c1, d1, b3 = got = grid.begin(
        [got, u_part], (near, l2), (core, f1), (core, r1), (z1, p3)
    )
    f2, l3 = join(l2, n2), join(p3, b3)
    u = (u_part * scale).astype(BF)
    table, head, wv = call(
        lambda *r: assemble_kernel(*r, band=band, offset=2 * band, tall=tall, extra=head_rows),
        "assemble",
        (NZ,),
        [smem()] + steps_of(low_rows, 128),
        (
            shape(n, width, dtype=BF),
            shape(ho, width),
            shape(width, width, dtype=BF),
        ),
        (full((n, width)), full((ho, width)), full((width, width))),
        [],
        0,
        1 << 23,
        co,
        *low,
    )
    tv = call(
        lambda *r: product_kernel(*r, band=band),
        "table_values",
        (NZ,),
        [smem(), full((n, width))] + steps_of(band, 128),
        shape(n, width, dtype=BF),
        full((n, width)),
        [],
        2 * n * width * width,
        1 << 22,
        co,
        table,
        *low,
    )
    tu = jnp.pad(dot(table, u, NN), ((0, 0), (0, 128 - HEADS)))
    attn = twice([f1, r1, c1, d1])
    r2, n3, a4 = got = grid.begin([got, u, tv], (far, f2), (near, l3), (z2, bundles[4]))
    f3, p4 = join(l3, n3), stack(4, a4)
    tu, weighted = grid.gate((tu, weighted), [n2])
    tu = grid.gate(tu, [weighted])
    agg, fold, pa = call(
        pool_kernel,
        "pool",
        (HEADS // 4,),
        [full((rows, n)), full((n, 128)), full((n, 128)), pl.BlockSpec((n, 256), lambda j: (0, j))],
        (shape(rows, width, dtype=BF), shape(HEADS, rows, n, dtype=BF), shape(HEADS, rows, 128)),
        (
            pair,
            pl.BlockSpec((4, rows, n), lambda j: (j, 0, 0)),
            pl.BlockSpec((4, rows, 128), lambda j: (j, 0, 0)),
        ),
        [],
        12 * HEADS * rows * n * 128,
        1 << 23,
        spread,
        var_of,
        tu,
        tv,
    )

    gain_one = table[lane_of(base + SOURCES + 1)].astype(F32)[None]
    gain_two = table[lane_of(base + SOURCES + 2)].astype(F32)[None]
    onehot = (groups[:, 0, 0][:, None] == jnp.arange(SOURCES)).astype(F32)
    src = dot(onehot, table[src_at : src_at + SOURCES].astype(F32), NN, precision=HIGH)
    x0, h1 = call(
        lambda *r: enter_kernel(*r, band=band),
        "enter",
        (NZ,),
        [smem(), wide, full((micro, width)), line] + steps_of(band, 128, 0, 1),
        (shape(rows, width), shape(rows, width, dtype=BF)),
        (wide, wide),
        [],
        2 * rows * width * width,
        1 << 22,
        co,
        agg,
        src,
        gain_one,
        *low,
    )
    c2, d2, r3, b4 = got = grid.begin([got, h1], (core, f2), (core, r2), (far, f3), (z1, p4))
    l4 = join(p4, b4)
    up = twice([f2, r2, c2, d2])
    qkv, probs, o, x1, h2 = call(
        lambda *r: attend_kernel(*r, band=band, scale=scale),
        "attend",
        (2 * NZ,),
        [smem(), smem(), wide, wide, line]
        + steps_of(3 * band, 128)
        + steps_of(band, 128, NZ, 3),
        (
            shape(rows, 3 * width, dtype=BF),
            shape(HEADS, micro, cap, cap),
            shape(rows, width, dtype=BF),
            shape(rows, width),
            shape(rows, width, dtype=BF),
        ),
        (full((rows, 3 * width)), full((HEADS, micro, cap, cap)), wide, wide, wide),
        [],
        8 * rows * width * width + 8 * rows * cap * width,
        1 << 24,
        co,
        lens,
        x0,
        h1,
        gain_two,
        *attn,
        *attn,
    )
    c3, d3, n4 = got = grid.begin([got, h2], (core, f3), (core, r3), (near, l4))
    f4 = join(l4, n4)
    down = twice([f3, r3, c3, d3])
    act, slope = call(
        lambda *r: up_kernel(*r, band=band, w=w),
        "up",
        (NZ,),
        [smem(), wide] + steps_of(band, w),
        (shape(rows, ff, dtype=BF), shape(rows, ff, dtype=BF)),
        (full((rows, ff)), full((rows, ff))),
        [],
        2 * rows * width * ff,
        1 << 24,
        co,
        h2,
        *up,
    )
    act = grid.gate(act, [n4])
    (r4,) = grid.begin([act], (far, f4))
    wq_parts = [f4, r4, *grid.begin([], (core, f4), (core, r4))]
    loss_part, dx2, dx2_low, d_head, df = call(
        lambda *r: down_kernel(*r, band=band, w=w),
        "down",
        (2 * NZ,),
        [smem(), smem(), wide, full((rows, ff)), full((rows, ff)), full((ho, width)), full((rows, ho)), full((rows, ho))]
        + [pl.BlockSpec((1, band, w), lambda i, b=b: (b * NZ + i % NZ, 0, 0)) for b in range(2)] * 4,
        (
            shape(8, 128),
            shape(rows, width),
            shape(rows, width, dtype=BF),
            shape(ho, width),
            shape(rows, ff, dtype=BF),
        ),
        (full((8, 128)), wide, wide, full((ho, width)), full((rows, ff))),
        [pltpu.VMEM((rows, width), F32)],
        4 * rows * width * ff,
        1 << 25,
        co,
        count[None],
        x1,
        act,
        slope,
        head,
        targets[:, 0, 0].reshape(rows, ho),
        weighted,
        *down,
    )

    place = lambda height, wid: pl.BlockSpec((NZ, height, wid), lambda i: (i, 0, 0))

    turned = [pltpu.VMEM((width, rows), BF)]

    def sent(kernel, name, height, wid, flops, scratch, *args):
        out = shape(4 * NZ, height, wid, dtype=BF)
        return call(
            kernel,
            name,
            (NZ,),
            [smem()] + [full(a.shape) for a in args],
            (out, out),
            (place(height, wid),) * 2,
            scratch,
            flops,
            32 * height * wid * 2 + 4 * 1024 * 1024,
            co,
            *args,
        )

    def sent_pairs(kernel, name, height, flops, scratch, *args):
        out = shape(4, NZ, height, 128, dtype=BF)
        block = pl.BlockSpec((4, 1, height, 128), lambda k: (0, k, 0, 0))
        keep, send = call(
            kernel,
            name,
            (NZ,),
            [smem()] + [smem() if a.ndim == 1 else full(a.shape) for a in args],
            (out, out),
            (block, block),
            scratch,
            flops,
            32 * height * 128 * 2,
            co,
            *args,
        )
        return keep.reshape(4 * NZ, height, 128), send.reshape(4 * NZ, height, 128)

    dense_grad = lambda *r: grad_kernel(*r, band=band, w=w)
    flow = {}
    flow["down"] = sent(dense_grad, "down_grad", band, w, 2 * rows * width * ff, turned, dx2_low, act)
    df = grid.gate(df, [flow["down"]])
    flow["up"] = sent(dense_grad, "up_grad", band, w, 2 * rows * width * ff, turned, h2, df)
    far, near, core, z1, z2 = grid.far, grid.near, grid.core, grid.next_z, grid.far_z

    def plus(left, right):
        return (left.astype(F32) + right.astype(F32)).astype(BF)

    def quarters(kept, got):
        return [plus(kept[i * NZ : (i + 1) * NZ], got[i * NZ : (i + 1) * NZ]) for i in range(4)]

    def halves(kept, got):
        return plus(kept[:2], got[:2]), plus(kept[2:], got[2:])

    def ends(kept, got):
        return plus(kept[:1], got[:1]), plus(kept[1:], got[1:])

    (got,) = grid.begin([r4], (core, flow["down"][1]))
    dq = quarters(flow["down"][0], got)
    df = grid.gate(df, [flow["up"], dq])
    (f1d,) = grid.begin([dq, flow["up"]], (far, dq[3]))
    got = core(flow["up"][1])
    dx1, dx1_low, d_gain_two = call(
        lambda *r: up_back_kernel(*r, band=band, w=w),
        "up_back",
        (NZ,),
        [smem(), full((rows, ff)), wide, line, wide] + steps_of(band, w),
        (shape(rows, width), shape(rows, width, dtype=BF), one),
        (wide, wide, line),
        [pltpu.VMEM((rows, width), F32)],
        2 * rows * width * ff,
        1 << 24,
        co,
        df,
        x1,
        gain_two,
        dx2,
        *up,
    )
    uq = quarters(flow["up"][0], got)
    d_side = plus(dq[1], f1d)
    dx1_low = grid.gate(dx1_low, [f1d, uq])
    (f0d,) = grid.begin([f1d, uq, dx1], (far, dq[2]))
    dqkv = call(
        lambda *r: attend_back_kernel(*r, band=band, scale=scale),
        "attend_back",
        (NZ,),
        [smem(), wide, full((rows, 3 * width)), full((HEADS, micro, cap, cap))]
        + steps_of(band, 128, 0, 3),
        shape(rows, 3 * width, dtype=BF),
        full((rows, 3 * width)),
        [pltpu.VMEM((rows, width), F32), pltpu.VMEM((rows, width), BF)],
        2 * rows * width * width + 12 * rows * cap * width,
        1 << 22,
        co,
        dx1_low,
        qkv,
        probs,
        *attn,
    )
    d_line = plus(dq[0], f0d)
    dqkv = grid.gate(dqkv, [f0d, d_side])
    (f1u,) = grid.begin([f0d, dqkv], (far, uq[3]))
    flow["attn"] = sent_pairs(
        lambda *r: attention_grad_kernel(*r, band=band),
        "attention_grad",
        4 * band,
        8 * rows * width * width,
        turned * 2,
        h1,
        o,
        dqkv,
        dx1_low,
    )
    u_side = plus(uq[1], f1u)
    dqkv = grid.gate(dqkv, [f1u, flow["attn"]])
    f0u, nd = grid.begin([f1u, flow["attn"]], (far, uq[2]), (near, d_side))
    got = core(grid.gate(flow["attn"][1], f1u))
    dx0_low, d_gain_one, dx0_sum, dagg = call(
        lambda *r: leave_kernel(*r, band=band),
        "leave",
        (2 * NZ,),
        [smem(), wide, full((rows, 3 * width)), wide, line]
        + steps_of(3 * band, 128)
        + steps_of(band, 128, NZ, 1),
        (
            shape(rows, width, dtype=BF),
            one,
            shape(micro, width),
            shape(rows, width, dtype=BF),
        ),
        (wide, line, full((micro, width)), wide),
        [pltpu.VMEM((rows, width), F32)],
        8 * rows * width * width,
        1 << 23,
        co,
        dx1,
        dqkv,
        x0,
        gain_one,
        *attn,
        *low,
    )
    u_line = plus(uq[0], f0u)
    d_half = halves(d_line, nd)
    dagg = grid.gate(dagg, [f0u, nd])
    nu, z1d = grid.begin([f0u, nd, dagg], (near, u_side), (z1, d_half[1]))
    g_rows, s_rows = call(
        pool_back_kernel,
        "pool_back",
        (HEADS // 4,),
        [
            full((rows, n)),
            full((n, 128)),
            pl.BlockSpec((n, 256), lambda j: (0, j)),
            pl.BlockSpec((4, rows, n), lambda j: (j, 0, 0)),
            pl.BlockSpec((4, rows, 128), lambda j: (j, 0, 0)),
            pair,
        ],
        (shape(n, width), shape(HEADS // 4, 4, n)),
        (pl.BlockSpec((n, 256), lambda j: (0, j)), pl.BlockSpec((1, 4, n), lambda j: (j, 0, 0))),
        [],
        14 * HEADS * rows * n * 128,
        1 << 23,
        spread,
        var_of,
        tv,
        fold,
        pa,
        dagg,
    )
    aq = quarters(flow["attn"][0], got)
    u_half = halves(u_line, nu)
    d_end = ends(d_half[0], z1d)
    dx0_low = grid.gate(dx0_low, [g_rows, nu, z1d])
    f1a, z1u = grid.begin([nu, z1d, g_rows], (far, aq[3]), (z1, u_half[1]))
    flow["low"] = sent_pairs(
        lambda *r: low_grad_kernel(*r, band=band, tall=tall, top=src_at - (n - 16)),
        "low_grad",
        band + tall + head_rows,
        2 * rows * width * width,
        [*turned, pltpu.VMEM((n, width), BF)],
        groups[:, 0, 0],
        agg,
        dx0_low,
        g_rows,
        dx0_sum,
        jnp.concatenate([d_gain_one, d_gain_two], axis=0),
        d_head,
    )
    a_side = plus(aq[1], f1a)
    u_end = ends(u_half[0], z1u)
    lk, ls = flow["low"]
    f0a, na, z2d, z2u, got = grid.begin(
        [f1a, z1u, lk], (far, aq[2]), (near, a_side), (z2, d_end[1]), (z2, u_end[1]), (core, ls)
    )
    lq = [plus(lk[: 2 * NZ], got[: 2 * NZ]), plus(lk[2 * NZ :], got[2 * NZ :])]
    fl = far(lq[1])
    down_sum = (d_end[0].astype(F32) + z2d.astype(F32))[0]
    up_sum = (u_end[0].astype(F32) + z2u.astype(F32))[0]
    a_half = halves(plus(aq[0], f0a), na)
    l_side, l_line = plus(lq[0][NZ:], fl[NZ:]), plus(lq[0][:NZ], fl[:NZ])
    nl, z1a = grid.begin([f0a, na, z2d, z2u, fl], (near, l_side), (z1, a_half[1]))
    l_half = halves(l_line, nl)
    z1l = z1(l_half[1])
    s_sum = grid.hop(grid.gate(s_rows.reshape(HEADS, n), nl), ("x", 1), ("c", 1), ("y", 1))
    a_end, l_end = ends(a_half[0], z1a), ends(l_half[0], z1l)
    z2l, z2a = grid.begin([z1a, z1l], (z2, l_end[1]), (z2, a_end[1]))
    s_sum = grid.hop(grid.gate(s_sum, [z1a, z1l]), ("z", 1), ("z", 2))
    wq_parts = grid.gate(wq_parts, z2l)
    wq, wk = call(
        lambda *r: square_kernel(*r, band=band),
        "squares",
        (NZ,),
        [smem()] + steps_of(2 * band, 128),
        (shape(width, width, dtype=BF),) * 2,
        (full((width, width)),) * 2,
        [],
        0,
        1 << 20,
        co,
        *twice(wq_parts),
    )
    low_sum, attn_sum = (
        (kept[0].astype(F32) + got.astype(F32))[0] for kept, got in ((l_end, z2l), (a_end, z2a))
    )
    u_heads = (jnp.arange(width)[:, None] // size == jnp.arange(HEADS)[None]).astype(F32)
    du = dot(table.astype(F32), s_sum, ((0,), (1,)), precision=HIGH)
    du_cols = dot(lax.dynamic_slice_in_dim(du, my_band * band, band), head_mask, NT, precision=HIGH)
    dqv_heads = dot(du, wk.astype(F32), TN, precision=HIGH) * scale
    dqv_all = jnp.sum(dqv_heads * u_heads.T, axis=0)
    dqv = lax.dynamic_slice_in_dim(dqv_all, my_strip * strip, strip)
    dq_own = jnp.sum(
        lax.dynamic_slice_in_dim(wq, my_strip * strip, strip, 0).astype(F32) * dqv_all[None], axis=1
    )
    table_own = lax.dynamic_slice_in_dim(table, my_band * band, band, 1)
    g_own = low_sum[band : band + tall]
    g_low = g_own.astype(BF)
    g_column = grid.collect(grid.collect(g_low, "c"), "y").reshape(n, strip)
    g_line = grid.collect(grid.collect(g_low, "x"), "z").reshape(STRIPS, tall, strip)
    g_line = jnp.transpose(g_line, (1, 0, 2)).reshape(tall, width)
    wa_sum = low_sum[:band]
    head_sum = low_sum[band + tall :].reshape(2, ho // STRIPS, strip)
    head_sum = jnp.transpose(head_sum, (1, 0, 2)).reshape(ho // STRIPS, band).T

    row_of = np.full((n,), base + SOURCES + 3)
    for row in range(base + SOURCES + 3):
        row_of[lane_of(row)] = row
    row_of = jnp.asarray(row_of)
    g_column = jnp.where((row_of < base)[:, None], g_column, 0.0).astype(BF)
    value_sum = dot(table_own, g_column, TN)
    key_sum = du_cols * qv_own.astype(F32)[None] * scale
    query_sum = query_own.astype(F32)[:, None] * dqv[None]
    s_own = lax.dynamic_slice_in_dim(s_sum, my_band * tall, tall, 1)
    wv_rows = lax.dynamic_slice_in_dim(wv, my_strip * strip, strip, 0)
    u_rows = lax.dynamic_slice_in_dim(u, my_strip * strip, strip, 0).astype(F32)
    d_rows = dot(g_line, wv_rows, NT) + dot(s_own, u_rows, ((0,), (1,)), precision=HIGH)
    own_row = lax.dynamic_slice_in_dim(row_of, my_band * tall, tall)[:, None]
    table_sum = jnp.where(own_row < base, d_rows, g_own)
    table_sum = jnp.where(own_row == base + SOURCES, dq_own[None], table_sum)[:table_band]
    square_sums = (query_sum, key_sum, value_sum, wa_sum, attn_sum)
    sumsq = sum(jnp.sum(s * s) for s in (*square_sums, up_sum, down_sum, head_sum, table_sum))
    both = grid.rounds(jnp.stack([loss_part[0, 0], sumsq]), AXES)
    loss = both[0] / count
    grad_norm = jnp.sqrt(both[1])
    factor = jnp.minimum(1.0, CLIP_AT / grad_norm)
    steps = step_count[0].astype(F32)
    square_sum = jnp.concatenate([s.reshape(-1, band, strip) for s in square_sums], axis=0)
    dense_sum = jnp.stack([up_sum, down_sum])
    sq = adam_update(square_master, square_first, square_second, square_sum, factor, steps, LEARN_RATE)
    de = adam_update(dense_master, dense_first, dense_second, dense_sum, factor, steps, LEARN_RATE)
    hd = adam_update(head_master, head_first, head_second, head_sum, factor, steps, LEARN_RATE)
    tb = adam_update(table_master, table_first, table_second, table_sum, factor, steps, TABLE_RATE)
    return (loss, grad_norm, *sq, *de, *hd, *tb)


def solution(mesh):
    grid = Grid(mesh)
    var, patch = ("y", "c"), ("z", "x")
    item = P(None, var, patch)
    weight = P(None, var, patch)
    flat = P(var, patch)
    in_specs = (
        P(None, None, patch, None, var),
        item,
        item,
        item,
        item,
        item,
        P(),
        *(weight,) * 6,
        *(flat,) * 6,
    )
    out_specs = (P(), P(), *(weight,) * 8, *(flat,) * 8)

    def step(*args):
        return (fast_body if grid.fast else body)(grid, *args)

    return jax.shard_map(step, mesh=grid.mesh, in_specs=in_specs, out_specs=out_specs, check_vma=False)
```

```python
import math

import jax
import jax.numpy as jnp
import numpy as np
from jax import lax
from jax.experimental import pallas as pl
from jax.experimental.pallas import tpu as pltpu
from jax.sharding import Mesh
from jax.sharding import PartitionSpec as P

HEADS = 16
V = 48
PATCH_PIXELS = 4
SOURCES = 5
LATS = 64
PAD = 8

HIGH = lax.Precision.HIGHEST
CLIP_AT = 0.01
LEARN_RATE = 0.01
TABLE_RATE = 0.3
WEIGHT_DECAY = 0.1
FIRST_DECAY = 0.5
SECOND_DECAY = 0.5
EPSILON = 1e-08
NORM_EPSILON = 1e-05
AXES = ("y", "c", "z", "x")
BF = jnp.bfloat16
F32 = jnp.float32


class Grid:
    def __init__(self, mesh):
        nv, npatch = mesh.shape["var"], mesh.shape["patch"]
        self.sizes = {"y": nv // 2, "c": 2, "z": npatch // 2, "x": 2}
        self.mesh = Mesh(mesh.devices.reshape(tuple(self.sizes.values())), AXES)
        self.nv, self.np = nv, npatch
        self.fast = self.sizes["y"] == 2 and self.sizes["z"] == 4

    def flat(self, move):
        s = [self.sizes[a] for a in AXES]
        pairs = []
        for y in range(s[0]):
            for c in range(s[1]):
                for z in range(s[2]):
                    for x in range(s[3]):
                        ty, tc, tz, tx = move(y, c, z, x)
                        src = ((y * s[1] + c) * s[2] + z) * s[3] + x
                        dst = ((ty * s[1] + tc) * s[2] + tz) * s[3] + tx
                        pairs.append((src, dst))
        return pairs

    def permute(self, value, move):
        return lax.ppermute(value, AXES, self.flat(move))

    def swap(self, value, axis, bit=1):
        return lax.ppermute(value, axis, [(i, i ^ bit) for i in range(self.sizes[axis])])

    def total(self, value, axes=AXES):
        for axis in axes:
            bit = 1
            while bit < self.sizes[axis]:
                value = jax.tree.map(lambda v: v + self.swap(v, axis, bit), value)
                bit *= 2
        return value

    def spread(self, value, axes):
        count = math.prod(self.sizes[a] for a in axes)
        held = jnp.zeros((count,) + value.shape, value.dtype)
        held = lax.dynamic_update_index_in_dim(held, value, lax.axis_index(axes), 0)
        return self.total(held, axes)

    def along(self, first):
        def move(y, c, z, x):
            if (c == 0) == first:
                return (y ^ 1, c, z, x)
            return (y, c, z, x ^ 1)

        return move

    def gather(self, piece):
        return lax.all_gather(piece, AXES).reshape(self.nv, self.np, *piece.shape)

    def scatter(self, parts):
        nv, npatch, rows, w = parts.shape
        flat = parts.reshape(nv * npatch * rows, w)
        return lax.psum_scatter(flat, AXES, scatter_dimension=0, tiled=True).astype(F32)

    def gate(self, values, before):
        empty = isinstance(before, list) and not before
        return values if empty else lax.optimization_barrier((values, before))[0]

    def hop(self, value, *steps):
        for axis, bit in steps:
            value = value + self.swap(value, axis, bit)
        return value

    def rounds(self, value, axes):
        if "c" in axes:
            value = value + self.swap(value, "c")
        if "y" in axes:
            both = self.permute(value, lambda y, c, z, x: (y ^ 1, c, z, x ^ 1))
            value = (value + self.swap(value, "x")) + (self.swap(value, "y") + both)
        elif "x" in axes:
            value = value + self.swap(value, "x")
        if "z" in axes:
            third = self.swap(value, "z", 3)
            value = (value + self.swap(value, "z", 1)) + (self.swap(value, "z", 2) + third)
        return value

    def collect(self, value, axis):
        count = self.sizes[axis]
        here = lax.axis_index(axis)
        got = [value] + [self.swap(value, axis, flip) for flip in range(1, count)]
        out = []
        for place in range(count):
            piece = got[count - 1]
            for flip in range(count - 1):
                piece = jnp.where((here ^ flip) == place, got[flip], piece)
            out.append(piece)
        return jnp.stack(out)

    def begin(self, before, *moves):
        operands = self.gate([v for _, v in moves], before)
        return [fn(v) for (fn, _), v in zip(moves, operands)]

    def far_z(self, piece):
        return self.swap(piece, "z", 2)

    def next_z(self, pair):
        return self.swap(pair, "z", 1)

    def near(self, line):
        return self.permute(line, self.along(False))

    def far(self, both):
        return self.permute(both, self.along(True))

    def core(self, value):
        return self.swap(value, "c")


def whole(chunks):
    nv, npatch, rows, w = chunks.shape
    return jnp.transpose(chunks, (0, 2, 1, 3)).reshape(nv * rows, npatch * w)


def chunked(value, nv, npatch):
    r, c = value.shape
    return jnp.transpose(value.reshape(nv, r // nv, npatch, c // npatch), (0, 2, 1, 3))


def latitude_table():
    levels = jnp.arange(2 * LATS).astype(F32)
    cosine = jnp.cos(((levels + 0.5) / (2 * LATS) - 0.5) * math.pi)
    scaled = cosine / jnp.mean(cosine)
    index = 2 * jnp.arange(LATS)[:, None] + jnp.arange(PATCH_PIXELS)[None, :] // 2
    return scaled[index]


def layer_norm(value, gain):
    center = value - jnp.mean(value, axis=-1, keepdims=True)
    spread = jnp.mean(center * center, axis=-1, keepdims=True)
    return center * lax.rsqrt(spread + NORM_EPSILON) * gain


def exact_gelu(value):
    return jax.nn.gelu(value, approximate=False)


def adam_update(master, first, second, grad, factor, steps, rate):
    clipped = grad * factor
    new_first = FIRST_DECAY * first + (1.0 - FIRST_DECAY) * clipped
    new_second = SECOND_DECAY * second + (1.0 - SECOND_DECAY) * clipped * clipped
    first_hat = new_first / (1.0 - jnp.power(FIRST_DECAY, steps))
    second_hat = new_second / (1.0 - jnp.power(SECOND_DECAY, steps))
    new_master = master - rate * (
        first_hat / (jnp.sqrt(second_hat) + EPSILON) + WEIGHT_DECAY * master
    )
    return (new_master, new_first, new_second, new_master.astype(BF))


def dot(a, b, dims, batch=((), ()), precision=None):
    return lax.dot_general(
        a, b, (dims, batch), precision=precision, preferred_element_type=F32
    )


NN = ((1,), (0,))
NT = ((1,), (1,))
TN = ((0,), (0,))


def body(
    grid,
    pixels,
    targets,
    masks,
    lengths,
    groups,
    latitudes,
    step_count,
    square_master,
    square_first,
    square_second,
    dense_master,
    dense_first,
    dense_second,
    head_master,
    head_first,
    head_second,
    table_master,
    table_first,
    table_second,
):
    nv, npatch = grid.nv, grid.np
    micro, items, _, cap, own_pixels = pixels.shape
    rows = micro * cap
    width = square_master.shape[1] * nv
    size = width // HEADS
    scale = size ** (-0.5)
    band, strip = square_master.shape[1:]
    ff_strip = dense_master.shape[2]
    ho = head_master.shape[1] * npatch
    base = 5 * V + cap
    table_band = table_master.shape[0]
    table_pad = -table_band % PAD
    my_band = lax.axis_index(("y", "c"))
    my_strip = lax.axis_index(("z", "x"))

    square_low = square_master.astype(BF)
    dense_low = dense_master.astype(BF)
    head_low = head_master.astype(BF)
    table_low = table_master.astype(BF)
    first = jnp.concatenate(
        [
            jnp.pad(table_low, ((0, table_pad), (0, 0))),
            square_low[2],
            square_low[3],
        ],
        axis=0,
    )
    first = grid.gather(first)
    table = whole(first[:, :, :table_band])
    start = table_band + table_pad
    wv = whole(first[:, :, start : start + band])
    wa = whole(first[:, :, start + band : start + 2 * band])
    second = grid.gather(square_low[4:8].reshape(4 * band, strip))
    wqkv = jnp.concatenate(
        [whole(second[:, :, k * band : (k + 1) * band]) for k in range(3)], axis=1
    )
    wo = whole(second[:, :, 3 * band :])
    w1 = whole(grid.gather(dense_low[0]))
    w2 = whole(grid.gather(dense_low[1]))
    head = whole(grid.gather(head_low))

    slots = jnp.arange(cap)
    lat_table = latitude_table()
    valid = masks[:, 0, 0].astype(F32) * (slots[None] < lengths[:, 0, 0][:, None]).astype(F32)[..., None]
    lat_onehot = (latitudes[:, 0, 0][..., None] == jnp.arange(LATS)).astype(F32)
    wpix = jnp.einsum("mcl,lk->mck", lat_onehot, lat_table, precision=HIGH) * valid
    weighted = jnp.tile(wpix.reshape(rows, PATCH_PIXELS), (1, V))
    count = grid.total(jnp.sum(valid))

    parts = pixels[:, :, 0]
    mine = lax.all_to_all(parts, ("y", "c"), split_axis=1, concat_axis=3, tiled=True)[:, 0]
    pix = jnp.transpose(mine.reshape(rows, V, PATCH_PIXELS), (0, 2, 1)).astype(F32)

    query = table[base + SOURCES]
    query_own = lax.dynamic_slice_in_dim(query, my_band * band, band)
    qv = dot(query_own[None], square_low[0], NN)[0]
    qv_own = grid.total(qv, ("y", "c")).astype(BF)
    col_head = (my_strip * strip + jnp.arange(strip)) // size
    head_mask = (col_head[:, None] == jnp.arange(HEADS)[None]).astype(F32)
    u_part = dot(square_low[1].astype(F32) * qv_own.astype(F32)[None], head_mask, NN, precision=HIGH)
    u_band = (grid.total(u_part, ("z", "x")) * scale).astype(BF)
    u = grid.spread(u_band, ("y", "c")).reshape(width, HEADS)
    rows_t = jnp.concatenate(
        [
            jnp.transpose(table[: PATCH_PIXELS * V].reshape(V, PATCH_PIXELS, width), (1, 0, 2)).reshape(-1, width),
            table[PATCH_PIXELS * V : base],
        ],
        axis=0,
    )
    tv = dot(rows_t, wv, NN)
    tu = dot(rows_t, u, NN)
    nk = PATCH_PIXELS * V
    n5 = nk + V
    scores = (
        jnp.einsum("ckv,kvh->chv", pix, tu[:nk].reshape(PATCH_PIXELS, V, HEADS), precision=HIGH)
        + tu[nk:n5].T[None]
        + jnp.tile(tu[n5:], (micro, 1))[:, :, None]
    )
    pa = jax.nn.softmax(scores, axis=-1)
    pal = pa.astype(BF).astype(F32)
    mass = jnp.sum(pal, axis=-1)
    fold = jnp.concatenate(
        [(pal[:, :, None] * pix[:, None]).reshape(rows, HEADS, nk), pal], axis=2
    )
    tv_heads = tv.reshape(-1, HEADS, size)
    pos_v = jnp.tile(tv_heads[n5:], (micro, 1, 1))
    agg = (
        jnp.einsum("chn,nhe->che", fold, tv_heads[:n5], precision=HIGH)
        + mass[:, :, None] * pos_v
    )
    gathered = agg.reshape(rows, width).astype(BF)

    gain_one = table[base + SOURCES + 1].astype(F32)
    gain_two = table[base + SOURCES + 2].astype(F32)
    onehot = (groups[:, 0, 0][:, None] == jnp.arange(SOURCES)).astype(F32)
    src = jnp.dot(onehot, table[base : base + SOURCES].astype(F32), precision=HIGH)
    x0 = dot(gathered, wa, NN) + jnp.repeat(src, cap, axis=0)
    h1 = layer_norm(x0, gain_one).astype(BF)
    qkv = dot(h1, wqkv, NN).astype(BF)
    q, k, vv = (
        qkv[:, i * width : (i + 1) * width].reshape(micro, cap, HEADS, size) for i in range(3)
    )
    keymask = slots[None] < lengths[:, 0, 0][:, None]
    raw = jnp.einsum("mqhe,mkhe->mhqk", q, k, preferred_element_type=F32) * scale
    probs = jax.nn.softmax(jnp.where(keymask[:, None, None], raw, -1e30), axis=-1)
    probs_low = probs.astype(BF)
    o = jnp.einsum("mhqk,mkhe->mqhe", probs_low, vv, preferred_element_type=F32)
    o = o.reshape(rows, width).astype(BF)
    x1 = x0 + dot(o, wo, NN)
    h2 = layer_norm(x1, gain_two).astype(BF)
    f = dot(h2, w1, NN)
    act = exact_gelu(f).astype(BF)
    x2 = x1 + dot(act, w2, NT)
    x2_low = x2.astype(BF)
    pred = dot(x2_low, head, NN)
    diff = pred - targets[:, 0, 0].astype(F32).reshape(rows, ho)
    loss_local = jnp.sum(weighted * diff * diff)
    dpred = (2.0 * weighted * diff / count).astype(BF)

    d_head = dot(x2_low, dpred, TN)
    dx2 = dot(dpred, head, NT)
    dx2_low = dx2.astype(BF)
    d_down = dot(dx2_low, act, TN)
    dact = dot(dx2_low, w2, NN)
    _, gelu_back = jax.vjp(exact_gelu, f)
    df = gelu_back(dact)[0].astype(BF)
    d_up = dot(h2, df, TN)
    dh2 = dot(df, w1, NT)
    _, norm_back = jax.vjp(layer_norm, x1, gain_two)
    dx1n, d_gain_two = norm_back(dh2)
    dx1 = dx2 + dx1n
    dx1_low = dx1.astype(BF)
    d_wo = dot(o, dx1_low, TN)
    do = dot(dx1_low, wo, NT).astype(BF).reshape(micro, cap, HEADS, size)
    dprobs = jnp.einsum("mqhe,mkhe->mhqk", do, vv, preferred_element_type=F32)
    dvv = jnp.einsum("mhqk,mqhe->mkhe", probs_low, do, preferred_element_type=F32)
    ds = (probs * (dprobs - jnp.sum(probs * dprobs, axis=-1, keepdims=True))).astype(BF)
    dq = jnp.einsum("mhqk,mkhe->mqhe", ds, k, preferred_element_type=F32) * scale
    dk = jnp.einsum("mhqk,mqhe->mkhe", ds, q, preferred_element_type=F32) * scale
    dqkv = jnp.concatenate([t.reshape(rows, width) for t in (dq, dk, dvv)], axis=1).astype(BF)
    d_wqkv = dot(h1, dqkv, TN)
    dh1 = dot(dqkv, wqkv, NT)
    _, norm_back = jax.vjp(layer_norm, x0, gain_one)
    dx0n, d_gain_one = norm_back(dh1)
    dx0 = dx1 + dx0n
    d_src = jnp.dot(onehot.T, jnp.sum(dx0.reshape(micro, cap, width), axis=1), precision=HIGH)
    dx0_low = dx0.astype(BF)
    d_wa = dot(gathered, dx0_low, TN)
    dagg = dot(dx0_low, wa, NT).astype(BF).astype(F32).reshape(rows, HEADS, size)

    dfold = jnp.einsum("che,nhe->chn", dagg, tv_heads[:n5], precision=HIGH)
    dpal = (
        jnp.sum(dfold[:, :, :nk].reshape(rows, HEADS, PATCH_PIXELS, V) * pix[:, None], axis=2)
        + dfold[:, :, nk:]
        + jnp.sum(dagg * pos_v, axis=-1)[:, :, None]
    )
    dsv = (pa * (dpal - jnp.sum(pa * dpal, axis=-1, keepdims=True))).astype(BF).astype(F32)
    g_rows = jnp.einsum("chn,che->nhe", fold, dagg, precision=HIGH).reshape(n5, width)
    g_pos = jnp.sum((mass[:, :, None] * dagg).reshape(micro, cap, width), axis=0)
    s_rows = jnp.concatenate(
        [
            jnp.einsum("ckv,chv->kvh", pix, dsv, precision=HIGH).reshape(nk, HEADS),
            jnp.sum(dsv, axis=0).T,
            jnp.sum(jnp.sum(dsv, axis=-1).reshape(micro, cap, HEADS), axis=0),
        ],
        axis=0,
    )
    g_table = jnp.concatenate(
        [
            jnp.transpose(g_rows[:nk].reshape(PATCH_PIXELS, V, width), (1, 0, 2)).reshape(nk, width),
            g_rows[nk:],
            g_pos,
            d_src,
            jnp.zeros((1, width), F32),
            d_gain_one[None],
            d_gain_two[None],
        ],
        axis=0,
    )
    s_table = jnp.concatenate(
        [
            jnp.transpose(s_rows[:nk].reshape(PATCH_PIXELS, V, HEADS), (1, 0, 2)).reshape(nk, HEADS),
            s_rows[nk:],
        ],
        axis=0,
    )

    def to_owner(value):
        return grid.scatter(chunked(value.astype(BF), nv, npatch))

    down_sum = to_owner(d_down)
    up_sum = to_owner(d_up)
    s_sum = grid.total(s_table)
    low_part = jnp.concatenate(
        [
            jnp.pad(chunked(g_table.astype(BF), nv, npatch), ((0, 0), (0, 0), (0, table_pad), (0, 0))),
            chunked(d_wa.astype(BF), nv, npatch),
        ],
        axis=2,
    )
    low_sum = grid.scatter(low_part)
    g_own = low_sum[:table_band]
    wa_sum = low_sum[table_band + table_pad :]
    attn_sum = grid.scatter(
        jnp.concatenate(
            [chunked(d_wqkv[:, i * width : (i + 1) * width].astype(BF), nv, npatch) for i in range(3)]
            + [chunked(d_wo.astype(BF), nv, npatch)],
            axis=2,
        )
    )
    head_sum = to_owner(d_head)

    g_low = g_own.astype(BF)
    g_column = grid.spread(g_low, ("y", "c")).reshape(nv * table_band, strip)[:base]
    g_line = jnp.transpose(grid.spread(g_low, ("z", "x")), (1, 0, 2)).reshape(table_band, width)
    table_own_band = lax.dynamic_slice_in_dim(table, my_band * band, band, 1)
    value_sum = dot(table_own_band[:base], g_column, TN)
    du_own = dot(table_own_band[:base].astype(F32), s_sum, TN, precision=HIGH)
    du_cols = dot(du_own, head_mask, NT, precision=HIGH)
    key_sum = du_cols * qv_own.astype(F32)[None] * scale
    dqv = grid.total(jnp.sum(square_low[1].astype(F32) * du_cols, axis=0) * scale, ("y", "c"))
    query_sum = query_own.astype(F32)[:, None] * dqv[None]
    dquery = jnp.sum(square_low[0].astype(F32) * dqv[None], axis=1)
    dquery = lax.dynamic_update_slice_in_dim(jnp.zeros((width,), F32), dquery, my_band * band, 0)
    dquery = grid.total(dquery)
    table_row = my_band * table_band + jnp.arange(table_band)
    s_pad = jnp.pad(s_sum, ((0, nv * table_band - base), (0, 0)))
    s_own = lax.dynamic_slice_in_dim(s_pad, my_band * table_band, table_band, 0)
    wv_rows = lax.dynamic_slice_in_dim(wv, my_strip * strip, strip, 0)
    u_rows = lax.dynamic_slice_in_dim(u, my_strip * strip, strip, 0)
    d_rows = dot(g_line, wv_rows, NT) + dot(s_own, u_rows.astype(F32), NT, precision=HIGH)
    dq_own = lax.dynamic_slice_in_dim(dquery, my_strip * strip, strip, 0)
    table_sum = jnp.where((table_row < base)[:, None], d_rows, g_own)
    table_sum = jnp.where((table_row == base + SOURCES)[:, None], dq_own[None], table_sum)
    square_sum = jnp.concatenate(
        [query_sum[None], key_sum[None], value_sum[None], wa_sum[None], attn_sum.reshape(4, band, strip)],
        axis=0,
    )
    dense_sum = jnp.stack([up_sum, down_sum])
    shards = (square_sum, dense_sum, head_sum, table_sum)
    sumsq = sum(jnp.sum(s * s) for s in shards)
    both = grid.total(jnp.stack([loss_local, sumsq]))
    loss = both[0] / count
    norm = jnp.sqrt(both[1])
    factor = jnp.minimum(1.0, CLIP_AT / norm)
    steps = step_count[0].astype(F32)
    sq = adam_update(square_master, square_first, square_second, shards[0], factor, steps, LEARN_RATE)
    de = adam_update(dense_master, dense_first, dense_second, shards[1], factor, steps, LEARN_RATE)
    hd = adam_update(head_master, head_first, head_second, shards[2], factor, steps, LEARN_RATE)
    tb = adam_update(table_master, table_first, table_second, shards[3], factor, steps, TABLE_RATE)
    return (loss, norm, *sq, *de, *hd, *tb)


NZ = 4
BANDS = 4
STRIPS = 8
NT_DIMS = (((1,), (1,)), ((), ()))
NN_DIMS = (((1,), (0,)), ((), ()))
TN_DIMS = (((0,), (0,)), ((), ()))
VMEM_LIMIT = 56 * 1024 * 1024


def mm(a, b):
    return lax.dot_general(a, b, NN_DIMS, preferred_element_type=F32)


def mm_nt(a, b):
    return lax.dot_general(a, b, NT_DIMS, preferred_element_type=F32)


def mm_tn(a, b):
    return lax.dot_general(a, b, TN_DIMS, preferred_element_type=F32)


def zflip(k):
    return (k % 2) * 2 + k // 2


def span(index, extent):
    return pl.ds(pl.multiple_of(index * extent, extent), extent)


def spots(core):
    out = []
    for owner in (core, 1 - core):
        for a in range(2):
            for b in range(2):
                out.append((a, b, owner) if owner == 0 else (b, a, owner))
    return out


def by_core(co, fn):
    for core in range(2):

        @pl.when(co[1] == core)
        def _(core=core):
            fn(core)


def forward_step(co, k, x_ref, chunks, row, band, w, put):
    back = co[2] ^ zflip(k)

    def run(core):
        places = spots(core)
        for fx in range(2):
            total = None
            for index, (fy, px, owner) in enumerate(places):
                if px != fx:
                    continue
                r = (co[0] ^ fy) * 2 + owner
                part = mm(x_ref[:, span(r, band)], chunks[index][0, row : row + band])
                total = part if total is None else total + part
            put(back * 2 + (co[3] ^ fx), total)

    by_core(co, run)


def backward_step(co, k, dy_ref, chunks, row, band, w, acc_ref, fresh):
    back = co[2] ^ zflip(k)

    def run(core):
        places = spots(core)
        for owner in range(2):
            for fy in range(2):
                total = None
                for index, (py, fx, who) in enumerate(places):
                    if (py, who) != (fy, owner):
                        continue
                    p = back * 2 + (co[3] ^ fx)
                    part = mm_nt(dy_ref[:, span(p, w)], chunks[index][0, row : row + band])
                    total = part if total is None else total + part
                r = (co[0] ^ fy) * 2 + owner

                @pl.when(fresh)
                def _():
                    acc_ref[:, span(r, band)] = total

                @pl.when(jnp.logical_not(fresh))
                def _():
                    acc_ref[:, span(r, band)] += total

    by_core(co, run)


def by_place(co, fn):
    for core in range(2):
        for x in range(2):

            @pl.when((co[1] == core) & (co[3] == x))
            def _(core=core, x=x):
                fn(core, x)


def pair_of(chunks, core, x, flip_y, owner, rows):
    found = [None, None]
    for index, (fy, fx, who) in enumerate(spots(core)):
        if (fy, who) == (flip_y, owner):
            found[fx ^ x] = chunks[index][0, rows]
    return jnp.concatenate(found, axis=1)


def forward_pair(co, k, x_ref, chunks, row, band, put):
    back = co[2] ^ zflip(k)

    def run(core, x):
        total = None
        for owner in range(2):
            for fy in range(2):
                r = (co[0] ^ fy) * 2 + owner
                w = pair_of(chunks, core, x, fy, owner, slice(row, row + band))
                part = mm(x_ref[:, span(r, band)], w)
                total = part if total is None else total + part
        put(back, total)

    by_place(co, run)


def backward_pair(co, k, dy_ref, chunks, parts, band, acc_ref, fresh):
    back = co[2] ^ zflip(k)
    width = dy_ref.shape[1] // parts

    def run(core, x):
        for owner in range(2):
            for fy in range(2):
                total = None
                for part in range(parts):
                    w = pair_of(chunks, core, x, fy, owner, slice(part * band, (part + 1) * band))
                    col = pl.multiple_of(part * width + back * 256, 256)
                    got = mm_nt(dy_ref[:, pl.ds(col, 256)], w)
                    total = got if total is None else total + got
                r = (co[0] ^ fy) * 2 + owner

                @pl.when(fresh)
                def _():
                    acc_ref[:, span(r, band)] = total

                @pl.when(jnp.logical_not(fresh))
                def _():
                    acc_ref[:, span(r, band)] += total

    by_place(co, run)


def smem():
    return pl.BlockSpec(memory_space=pltpu.SMEM)


def full(shape):
    zeros = (0,) * len(shape)
    return pl.BlockSpec(shape, lambda i: zeros)


def steps_of(rows, w, first=0, block=0):
    def at(b):
        return pl.BlockSpec(
            (1, rows, w), lambda i: (b * NZ + jnp.clip(i - first, 0, NZ - 1), block, 0)
        )

    return [at(0), at(1)] * 4


def twice(arrays):
    return [v for v in arrays for _ in range(2)]


def call(kernel, name, grid, in_specs, outs, out_specs, scratch, flops, moved, *args):
    return pl.pallas_call(
        kernel,
        name=name,
        grid=grid,
        in_specs=in_specs,
        out_shape=outs,
        out_specs=out_specs,
        scratch_shapes=scratch,
        compiler_params=pltpu.CompilerParams(
            vmem_limit_bytes=VMEM_LIMIT
        ),
        cost_estimate=pl.CostEstimate(flops=flops, bytes_accessed=moved, transcendentals=0),
    )(*args)


def shape(*dims, dtype=F32):
    return jax.ShapeDtypeStruct(dims, dtype)


def norm(value, gain):
    center = value - jnp.mean(value, axis=-1, keepdims=True)
    spread = jnp.mean(center * center, axis=-1, keepdims=True)
    return center * lax.rsqrt(spread + NORM_EPSILON) * gain


def norm_grad(value, gain, grad):
    center = value - jnp.mean(value, axis=-1, keepdims=True)
    spread = jnp.mean(center * center, axis=-1, keepdims=True)
    inverse = lax.rsqrt(spread + NORM_EPSILON)
    unit = center * inverse
    inner = grad * gain
    out = inverse * (
        inner
        - jnp.mean(inner, axis=-1, keepdims=True)
        - unit * jnp.mean(inner * unit, axis=-1, keepdims=True)
    )
    return out, jnp.sum(grad * unit, axis=0, keepdims=True)


def half_masks(rows):
    lane = lax.broadcasted_iota(jnp.int32, (rows, 128), 1)
    return [(lane < 64).astype(BF), (lane >= 64).astype(BF)]


def assemble_kernel(co, *refs, band, offset, tall, extra):
    chunks, (table_ref, more_ref, value_ref) = refs[:8], refs[8:]
    k = pl.program_id(0)
    back = co[2] ^ zflip(k)

    def run(core):
        for index, (fy, fx, owner) in enumerate(spots(core)):
            r = (co[0] ^ fy) * 2 + owner
            p = back * 2 + (co[3] ^ fx)
            table_ref[span(r, tall), span(p, 128)] = chunks[index][0, offset : offset + tall]
            more = chunks[index][0, offset + tall : offset + tall + extra].astype(F32)
            half = extra // 2
            for part in range(2):
                col = pl.multiple_of(r * band + part * 128, 128)
                more_ref[span(p, half), pl.ds(col, 128)] = more[part * half : (part + 1) * half]
            value_ref[span(r, band), span(p, 128)] = chunks[index][0, :band]

    by_core(co, run)


def square_kernel(co, *refs, band):
    chunks, outs = refs[:8], refs[8:]
    k = pl.program_id(0)

    def run(core):
        for index, (fy, fx, owner) in enumerate(spots(core)):
            r = (co[0] ^ fy) * 2 + owner
            p = (co[2] ^ zflip(k)) * 2 + (co[3] ^ fx)
            for part, out_ref in enumerate(outs):
                out_ref[span(r, band), span(p, 128)] = chunks[index][0, part * band : (part + 1) * band]

    by_core(co, run)


def product_kernel(co, x_ref, *refs, band):
    chunks, out_ref = refs[:8], refs[8]

    def put(p, total):
        out_ref[:, span(p, 256)] = total.astype(out_ref.dtype)

    forward_pair(co, pl.program_id(0), x_ref, chunks, 0, band, put)


def pool_kernel(x_ref, e_ref, tu_ref, tv_ref, agg_ref, a_ref, pa_ref):
    j = pl.program_id(0)
    x, e = x_ref[...], e_ref[...]
    wide_x, wide_e = x.astype(F32), e.astype(F32)
    rows, n = x.shape
    masks = half_masks(n)
    lane = lax.broadcasted_iota(jnp.int32, (n, 128), 1)
    keep = lax.broadcasted_iota(jnp.int32, (rows, 128), 1) < V
    for pair in range(2):
        total = None
        for half in range(2):
            head = 2 * pair + half
            column = jnp.sum(jnp.where(lane == 4 * j + head, tu_ref[...], 0.0), axis=1, keepdims=True)
            m = wide_e * column
            high = m.astype(BF)
            rest = (m - high.astype(F32)).astype(BF)
            s = mm(x, high) + mm(x, rest)
            s = jnp.where(keep, s, -1e30)
            s = jnp.exp(s - jnp.max(s, axis=-1, keepdims=True))
            pa = s * (1.0 / jnp.sum(s, axis=-1, keepdims=True))
            wide = mm_nt(pa.astype(BF), e)
            a = (wide_x * wide).astype(BF)
            pa_ref[head] = pa
            a_ref[head] = a
            part = mm(a, tv_ref[:, pair * 128 : (pair + 1) * 128] * masks[half])
            total = part if total is None else total + part
        agg_ref[:, pair * 128 : (pair + 1) * 128] = total.astype(BF)


def enter_kernel(co, agg_ref, src_ref, gain_ref, *refs, band):
    chunks, (x0_ref, h1_ref) = refs[:8], refs[8:]
    k = pl.program_id(0)

    def put(p, total):
        x0_ref[:, span(p, 256)] = total

    forward_pair(co, k, agg_ref, chunks, 0, band, put)

    @pl.when(k == NZ - 1)
    def _():
        cap = x0_ref.shape[0] // src_ref.shape[0]
        for m in range(src_ref.shape[0]):
            x0_ref[m * cap : (m + 1) * cap] += src_ref[m : m + 1]
        h1_ref[...] = norm(x0_ref[...], gain_ref[...]).astype(BF)


def attend_kernel(co, lens, x0_ref, h1_ref, gain_ref, *refs, band, scale):
    qkv_chunks, o_chunks = refs[:8], refs[8:16]
    qkv_ref, p_ref, o_ref, x1_ref, h2_ref = refs[16:]
    i = pl.program_id(0)
    micro = lens.shape[0]
    width = x0_ref.shape[1]
    cap = x0_ref.shape[0] // micro

    @pl.when(i < NZ)
    def _():
        for part in range(3):

            def put(p, total, part=part):
                col = pl.multiple_of(part * width + p * 256, 256)
                qkv_ref[:, pl.ds(col, 256)] = total.astype(BF)

            forward_pair(co, i, h1_ref, qkv_chunks, part * band, band, put)

    @pl.when(i == NZ - 1)
    def _():
        masks = half_masks(cap)
        key = lax.broadcasted_iota(jnp.int32, (cap, cap), 1)

        @pl.loop(0, width // 128, unroll=2)
        def _(j):
            for m in range(micro):
                rows = slice(m * cap, (m + 1) * cap)
                q = qkv_ref[rows, span(j, 128)]
                kk = qkv_ref[rows, pl.ds(pl.multiple_of(width + j * 128, 128), 128)]
                vv = qkv_ref[rows, pl.ds(pl.multiple_of(2 * width + j * 128, 128), 128)]
                total = None
                for half in range(2):
                    s = mm_nt(q * masks[half], kk) * scale
                    s = jnp.where(key < lens[m], s, -1e30)
                    s = jnp.exp(s - jnp.max(s, axis=-1, keepdims=True))
                    p = s * (1.0 / jnp.sum(s, axis=-1, keepdims=True))
                    p_ref[2 * j + half, m] = p
                    part = mm(p.astype(BF), vv * masks[half])
                    total = part if total is None else total + part
                o_ref[rows, span(j, 128)] = total.astype(BF)

    @pl.when(i >= NZ)
    def _():
        def put(p, total):
            x1_ref[:, span(p, 256)] = x0_ref[:, span(p, 256)] + total

        forward_pair(co, i - NZ, o_ref, o_chunks, 0, band, put)

    @pl.when(i == 2 * NZ - 1)
    def _():
        h2_ref[...] = norm(x1_ref[...], gain_ref[...]).astype(BF)


def up_kernel(co, h2_ref, *refs, band, w):
    chunks, (act_ref, slope_ref) = refs[:8], refs[8:]

    def put(p, f):
        bell = jnp.exp(-0.5 * f * f)
        t = 1.0 / (1.0 + (0.3275911 * 0.5**0.5) * jnp.abs(f))
        tail = t * (1.061405429 * 0.5)
        for term in (-1.453152027, 1.421413741, -0.284496736, 0.254829592):
            tail = t * (0.5 * term + tail)
        tail = tail * bell
        share = jnp.where(f < 0.0, tail, 1.0 - tail)
        act_ref[:, span(p, w)] = (f * share).astype(BF)
        slope_ref[:, span(p, w)] = (share + f * bell * ((2.0 * math.pi) ** -0.5)).astype(BF)

    forward_step(co, pl.program_id(0), h2_ref, chunks, 0, band, w, put)


def down_kernel(co, count, x1_ref, act_ref, slope_ref, head_ref, target_ref, weight_ref, *refs, band, w):
    chunks = refs[:8]
    loss_ref, dx2_ref, dx2_low_ref, dhead_ref, df_ref = refs[8:13]
    acc_ref = refs[13]
    i = pl.program_id(0)

    @pl.when(i < NZ)
    def _():
        backward_step(co, i, act_ref, chunks, 0, band, w, acc_ref, i == 0)

    @pl.when(i == NZ - 1)
    def _():
        x2 = (x1_ref[...] + acc_ref[...]).astype(BF)
        head = head_ref[...].astype(BF)
        diff = mm_nt(x2, head) - target_ref[...].astype(F32)
        weighted = weight_ref[...] * diff
        loss_ref[...] = jnp.broadcast_to(jnp.sum(weighted * diff), loss_ref.shape)
        dpred = (2.0 * weighted / count[0]).astype(BF)
        dhead_ref[...] = mm_tn(dpred, x2)
        dx2 = mm(dpred, head)
        dx2_ref[...] = dx2
        dx2_low_ref[...] = dx2.astype(BF)

    @pl.when(i >= NZ)
    def _():
        def put(p, dact):
            df_ref[:, span(p, w)] = (dact * slope_ref[:, span(p, w)].astype(F32)).astype(BF)

        forward_step(co, i - NZ, dx2_low_ref, chunks, 0, band, w, put)


def owner_place(co, i, owner):
    a, b, k = i // (2 * NZ), (i // NZ) % 2, i % NZ
    fy = jnp.where(owner == 0, a, b)
    fx = jnp.where(owner == 0, b, a)
    return (co[0] ^ fy) * 2 + owner, (co[2] ^ zflip(k)) * 2 + (co[3] ^ fx)


def targets(co, keep_ref, send_ref):
    return [
        (out, owner, j)
        for out, owner in ((keep_ref, co[1]), (send_ref, 1 - co[1]))
        for j in range(NZ)
    ]


def grad_kernel(co, x_ref, dy_ref, keep_ref, send_ref, xt_ref, *, band, w):
    i = pl.program_id(0)

    @pl.when(i == 0)
    def _():
        xt_ref[...] = x_ref[...].T

    for out_ref, owner, j in targets(co, keep_ref, send_ref):
        r, p = owner_place(co, i * NZ + j, owner)
        out_ref[j] = mm(xt_ref[span(r, band)], dy_ref[:, span(p, w)]).astype(BF)


def pair_places(co, k, keep_ref, send_ref):
    out = []
    for out_ref, owner in ((keep_ref, co[1]), (send_ref, 1 - co[1])):
        for fy in range(2):
            at = []
            for half in range(2):
                fx = co[3] ^ half
                at.append(jnp.where(owner == 0, fy * 2 + fx, fx * 2 + fy))
            out.append((out_ref, (co[0] ^ fy) * 2 + owner, co[2] ^ zflip(k), at))
    return out


def attention_grad_kernel(co, h1_ref, o_ref, dqkv_ref, dx1_ref, keep_ref, send_ref, ht_ref, ot_ref, *, band):
    k = pl.program_id(0)
    width = h1_ref.shape[1]

    @pl.when(k == 0)
    def _():
        ht_ref[...] = h1_ref[...].T
        ot_ref[...] = o_ref[...].T

    for out_ref, r, back, at in pair_places(co, k, keep_ref, send_ref):
        for part in range(4):
            if part < 3:
                col = pl.multiple_of(part * width + back * 256, 256)
                got = mm(ht_ref[span(r, band)], dqkv_ref[:, pl.ds(col, 256)])
            else:
                got = mm(ot_ref[span(r, band)], dx1_ref[:, span(back, 256)])
            for half in range(2):
                out_ref[at[half], 0, part * band : (part + 1) * band] = got[
                    :, half * 128 : (half + 1) * 128
                ].astype(BF)


def low_grad_kernel(
    co, groups, agg_ref, dx0_ref, g_ref, sum_ref, gain_ref, head_ref, keep_ref, send_ref, at_ref, gl_ref, *, band, tall, top
):
    k = pl.program_id(0)
    n = g_ref.shape[0]
    piece = head_ref.shape[0] // STRIPS

    @pl.when(k == 0)
    def _():
        at_ref[...] = agg_ref[...].T
        gl_ref[: n - 16] = g_ref[: n - 16].astype(BF)
        last = g_ref[n - 16 :]
        row = lax.broadcasted_iota(jnp.int32, last.shape, 0)
        for m in range(sum_ref.shape[0]):
            last += jnp.where(row == top + groups[m], sum_ref[m : m + 1], 0.0)
        for m in range(2):
            last += jnp.where(row == top + SOURCES + 1 + m, gain_ref[m : m + 1], 0.0)
        gl_ref[n - 16 :] = last.astype(BF)

    for out_ref, r, back, at in pair_places(co, k, keep_ref, send_ref):
        got = mm(at_ref[span(r, band)], dx0_ref[:, span(back, 256)])
        for half in range(2):
            p = back * 2 + half
            out_ref[at[half], 0, :band] = got[:, half * 128 : (half + 1) * 128].astype(BF)
            out_ref[at[half], 0, band : band + tall] = gl_ref[span(r, tall), span(p, 128)]
            head = [
                head_ref[span(p, piece), pl.ds(pl.multiple_of(r * band + part * 128, 128), 128)]
                for part in range(2)
            ]
            out_ref[at[half], 0, band + tall :] = jnp.concatenate(head, axis=0).astype(BF)


def up_back_kernel(co, df_ref, x1_ref, gain_ref, dx2_ref, *refs, band, w):
    chunks, (dx1_ref, dx1_low_ref, dgain_ref, acc_ref) = refs[:8], refs[8:]
    k = pl.program_id(0)
    backward_step(co, k, df_ref, chunks, 0, band, w, acc_ref, k == 0)

    @pl.when(k == NZ - 1)
    def _():
        out, dgain = norm_grad(x1_ref[...], gain_ref[...], acc_ref[...])
        dx1 = dx2_ref[...] + out
        dx1_ref[...] = dx1
        dx1_low_ref[...] = dx1.astype(BF)
        dgain_ref[...] = dgain


def attend_back_kernel(co, dx1_low_ref, qkv_ref, p_ref, *refs, band, scale):
    o_chunks = refs[:8]
    dqkv_ref, acc_ref, do_ref = refs[8:]
    i = pl.program_id(0)
    micro = p_ref.shape[1]
    width = dx1_low_ref.shape[1]
    cap = dx1_low_ref.shape[0] // micro

    @pl.when(i < NZ)
    def _():
        backward_pair(co, i, dx1_low_ref, o_chunks, 1, band, acc_ref, i == 0)

    @pl.when(i == NZ - 1)
    def _():
        do_ref[...] = acc_ref[...].astype(BF)
        masks = half_masks(cap)

        @pl.loop(0, width // 128, unroll=2)
        def _(j):
            for m in range(micro):
                rows = slice(m * cap, (m + 1) * cap)
                k_at = pl.ds(pl.multiple_of(width + j * 128, 128), 128)
                v_at = pl.ds(pl.multiple_of(2 * width + j * 128, 128), 128)
                q, kk, vv = qkv_ref[rows, span(j, 128)], qkv_ref[rows, k_at], qkv_ref[rows, v_at]
                do = do_ref[rows, span(j, 128)]
                dq = dk = dv = None
                for half in range(2):
                    p = p_ref[2 * j + half, m]
                    do_half = do * masks[half]
                    dp = mm_nt(do_half, vv)
                    moved = p * dp
                    ds = (moved - p * jnp.sum(moved, axis=-1, keepdims=True)).astype(BF)
                    parts = (
                        mm(ds, kk * masks[half]),
                        mm_tn(ds, q * masks[half]),
                        mm_tn(p.astype(BF), do_half),
                    )
                    if dq is None:
                        dq, dk, dv = parts
                    else:
                        dq, dk, dv = dq + parts[0], dk + parts[1], dv + parts[2]
                dqkv_ref[rows, span(j, 128)] = (dq * scale).astype(BF)
                dqkv_ref[rows, k_at] = (dk * scale).astype(BF)
                dqkv_ref[rows, v_at] = dv.astype(BF)


def leave_kernel(co, dx1_ref, dqkv_ref, x0_ref, gain_ref, *refs, band):
    qkv_chunks, a_chunks = refs[:8], refs[8:16]
    dx0_low_ref, dgain_ref, dsum_ref, dagg_ref, acc_ref = refs[16:]
    i = pl.program_id(0)
    micro = dsum_ref.shape[0]
    width = x0_ref.shape[1]
    cap = x0_ref.shape[0] // micro

    @pl.when(i < NZ)
    def _():
        backward_pair(co, i, dqkv_ref, qkv_chunks, 3, band, acc_ref, i == 0)

    @pl.when(i == NZ - 1)
    def _():
        out, dgain = norm_grad(x0_ref[...], gain_ref[...], acc_ref[...])
        dx0 = dx1_ref[...] + out
        dx0_low_ref[...] = dx0.astype(BF)
        dgain_ref[...] = dgain
        for m in range(micro):
            dsum_ref[m : m + 1] = jnp.sum(dx0[m * cap : (m + 1) * cap], axis=0, keepdims=True)

    @pl.when(i >= NZ)
    def _():
        backward_pair(co, i - NZ, dx0_low_ref, a_chunks, 1, band, acc_ref, i == NZ)

    @pl.when(i == 2 * NZ - 1)
    def _():
        dagg_ref[...] = acc_ref[...].astype(BF)


def pool_back_kernel(x_ref, e_ref, tv_ref, a_ref, pa_ref, dagg_ref, g_ref, s_ref):
    x, e = x_ref[...].astype(F32), e_ref[...]
    masks = half_masks(x.shape[0])
    for pair in range(2):
        at = slice(pair * 128, (pair + 1) * 128)
        total = None
        for half in range(2):
            head = 2 * pair + half
            part = dagg_ref[:, at] * masks[half]
            dpal = mm((mm_nt(part, tv_ref[:, at]) * x).astype(BF), e)
            pa = pa_ref[head]
            inner = pa * dpal
            ds = (inner - pa * jnp.sum(inner, axis=-1, keepdims=True)).astype(BF)
            s_ref[0, head : head + 1] = jnp.sum(mm_nt(ds, e) * x, axis=0, keepdims=True)
            got = mm_tn(a_ref[head], part)
            total = got if total is None else total + got
        g_ref[:, at] = total


def table_layout(cap, band, tall):
    n = BANDS * tall
    nk = PATCH_PIXELS * V
    select = np.zeros((nk, n), np.float32)
    fixed = np.zeros((cap, n), np.float32)
    var_of = np.zeros((n, 128), np.float32)
    for row in range(5 * V + cap):
        lane = (row // band) * tall + row % band
        if row < nk:
            select[row, lane] = 1.0
            var_of[lane, row // PATCH_PIXELS] = 1.0
        elif row < 5 * V:
            fixed[:, lane] = 1.0
            var_of[lane, row - nk] = 1.0
        else:
            fixed[row - 5 * V, lane] = 1.0
            var_of[lane, :V] = 1.0
    return select, fixed, var_of


def fast_body(
    grid,
    pixels,
    targets,
    masks,
    lengths,
    groups,
    latitudes,
    step_count,
    square_master,
    square_first,
    square_second,
    dense_master,
    dense_first,
    dense_second,
    head_master,
    head_first,
    head_second,
    table_master,
    table_first,
    table_second,
):
    micro, items, _, cap, own_pixels = pixels.shape
    rows = micro * cap
    band, strip = square_master.shape[1:]
    width = band * BANDS
    size = width // HEADS
    scale = size ** (-0.5)
    w = dense_master.shape[2]
    ff = w * STRIPS
    ho = head_master.shape[1] * STRIPS
    base = 5 * V + cap
    table_band = table_master.shape[0]
    tall = table_band + -table_band % 16
    n = BANDS * tall
    head_rows = head_master.size // strip
    y, c, z, x = (lax.axis_index(a) for a in AXES)
    co = jnp.stack([y, c, z, x]).astype(jnp.int32)
    my_band = y * 2 + c
    my_strip = z * 2 + x
    select, fixed, var_of = table_layout(cap, table_band, tall)

    def lane_of(row):
        return (row // table_band) * tall + row % table_band

    square_low = square_master.astype(BF)
    dense_low = dense_master.astype(BF)
    low_rows = 2 * band + tall + head_rows
    low = jnp.concatenate(
        [
            square_low[2],
            square_low[3],
            jnp.pad(table_master.astype(BF), ((0, tall - table_band), (0, 0))),
            jnp.transpose(
                head_master.astype(BF).T.reshape(ho // STRIPS, 2, strip), (1, 0, 2)
            ).reshape(head_rows, strip),
        ],
        axis=0,
    )
    attn = square_low[4:8].reshape(4 * band, strip)
    slots = jnp.arange(cap)
    lens = lengths[:, 0, 0]
    valid = masks[:, 0, 0].astype(F32) * (slots[None] < lens[:, None]).astype(F32)[..., None]
    lat_onehot = (latitudes[:, 0, 0][..., None] == jnp.arange(LATS)).astype(F32)
    wpix = jnp.einsum("mcl,lk->mck", lat_onehot, latitude_table(), precision=HIGH) * valid
    weighted = jnp.tile(wpix.reshape(rows, PATCH_PIXELS), (1, V))
    var_of = jnp.asarray(var_of, BF)
    query_row = base + SOURCES
    col_head = (my_strip * strip + jnp.arange(strip)) // size
    head_mask = (col_head[:, None] == jnp.arange(HEADS)[None]).astype(F32)
    wide, line, one = full((rows, width)), full((1, width)), shape(1, width)
    pair = pl.BlockSpec((rows, 256), lambda j: (0, j))
    src_at = lane_of(base)
    row = jnp.where(my_band == query_row // table_band, 1.0, 0.0) * table_master[query_row % table_band]
    first_pack = lax.dynamic_update_slice_in_dim(
        jnp.zeros((width,), F32), row.astype(BF).astype(F32), my_strip * strip, 0
    )
    first_pack = jnp.concatenate([first_pack, jnp.broadcast_to(jnp.sum(valid), (128,))])

    bundles = [low, attn, dense_low[0], dense_low[1], square_low[:2].reshape(2 * band, strip)]
    stack, join = lambda i, v: jnp.stack([bundles[i], v]), lambda a, b: jnp.concatenate([a, b], axis=0)
    z2, z1, near, far, core = grid.far_z, grid.next_z, grid.near, grid.far, grid.core
    (a0,) = grid.begin([], (z2, bundles[0]))
    first_pack = grid.hop(grid.gate(first_pack, [a0]), ("z", 1), ("z", 2))
    p0 = stack(0, a0)
    b0, a1 = got = grid.begin([a0, first_pack], (z1, p0), (z2, bundles[1]))
    l0, p1 = join(p0, b0), stack(1, a1)
    pack = grid.hop(first_pack, ("x", 1))
    pack = grid.hop(pack, ("y", 1), ("c", 1))
    query, count = pack[:width].astype(BF), pack[width]
    query_own = lax.dynamic_slice_in_dim(query, my_band * band, band)
    spread = jnp.tile(jnp.asarray(fixed), (micro, 1))
    for fy in range(2):
        for fc in range(2):
            other = (y ^ fy) * 2 + (c ^ fc)
            piece = lax.dynamic_index_in_dim(pixels[:, :, 0], other, 1, False)
            if fy or fc:
                piece = grid.permute(piece, lambda a, b, d, e, fy=fy, fc=fc: (a ^ fy, b ^ fc, d, e))
            pick = lax.dynamic_slice_in_dim(
                jnp.asarray(select, BF), other * own_pixels, own_pixels, 0
            )
            spread = spread + mm(piece.reshape(rows, own_pixels), pick)
    spread = spread.astype(BF)
    qv = dot(query_own[None], square_low[0], NN)[0]
    qv_own = grid.hop(qv, ("y", 1), ("c", 1)).astype(BF)
    u_part = dot(square_low[1].astype(F32) * qv_own.astype(F32)[None], head_mask, NN, precision=HIGH)
    u_part = lax.dynamic_update_slice_in_dim(jnp.zeros((width, HEADS), F32), u_part, my_band * band, 0)
    u_part = grid.hop(u_part, ("x", 1))
    n0, b1 = got = grid.begin([got, qv_own, spread], (near, l0), (z1, p1))
    f0, l1 = join(l0, n0), join(p1, b1)
    u_part = grid.hop(u_part, ("y", 1), ("c", 1), ("z", 1))
    r0, n1, a2 = got = grid.begin([got, u_part], (far, f0), (near, l1), (z2, bundles[2]))
    f1, p2 = join(l1, n1), stack(2, a2)
    (b2,) = grid.begin([], (z1, p2))
    l2 = join(p2, b2)
    c0, d0, r1, a3 = got = grid.begin(
        [got, b2, u_part], (core, f0), (core, r0), (far, f1), (z2, bundles[3])
    )
    p3 = stack(3, a3)
    u_part = grid.hop(u_part, ("z", 2))
    low = twice([f0, r0, c0, d0])
    n2, c1, d1, b3 = got = grid.begin(
        [got, u_part], (near, l2), (core, f1), (core, r1), (z1, p3)
    )
    f2, l3 = join(l2, n2), join(p3, b3)
    u = (u_part * scale).astype(BF)
    table, head, wv = call(
        lambda *r: assemble_kernel(*r, band=band, offset=2 * band, tall=tall, extra=head_rows),
        "assemble",
        (NZ,),
        [smem()] + steps_of(low_rows, 128),
        (
            shape(n, width, dtype=BF),
            shape(ho, width),
            shape(width, width, dtype=BF),
        ),
        (full((n, width)), full((ho, width)), full((width, width))),
        [],
        0,
        1 << 23,
        co,
        *low,
    )
    tv = call(
        lambda *r: product_kernel(*r, band=band),
        "table_values",
        (NZ,),
        [smem(), full((n, width))] + steps_of(band, 128),
        shape(n, width, dtype=BF),
        full((n, width)),
        [],
        2 * n * width * width,
        1 << 22,
        co,
        table,
        *low,
    )
    tu = jnp.pad(dot(table, u, NN), ((0, 0), (0, 128 - HEADS)))
    attn = twice([f1, r1, c1, d1])
    r2, n3, a4 = got = grid.begin([got, u, tv], (far, f2), (near, l3), (z2, bundles[4]))
    f3, p4 = join(l3, n3), stack(4, a4)
    aims = targets[:, 0, 0].reshape(rows, ho)
    tu, weighted, aims = grid.gate((tu, weighted, aims), [n2])
    tu = grid.gate(tu, [weighted, aims])
    agg, fold, pa = call(
        pool_kernel,
        "pool",
        (HEADS // 4,),
        [full((rows, n)), full((n, 128)), full((n, 128)), pl.BlockSpec((n, 256), lambda j: (0, j))],
        (shape(rows, width, dtype=BF), shape(HEADS, rows, n, dtype=BF), shape(HEADS, rows, 128)),
        (
            pair,
            pl.BlockSpec((4, rows, n), lambda j: (j, 0, 0)),
            pl.BlockSpec((4, rows, 128), lambda j: (j, 0, 0)),
        ),
        [],
        12 * HEADS * rows * n * 128,
        1 << 23,
        spread,
        var_of,
        tu,
        tv,
    )

    gain_one = table[lane_of(base + SOURCES + 1)].astype(F32)[None]
    gain_two = table[lane_of(base + SOURCES + 2)].astype(F32)[None]
    onehot = (groups[:, 0, 0][:, None] == jnp.arange(SOURCES)).astype(F32)
    src = dot(onehot, table[src_at : src_at + SOURCES].astype(F32), NN, precision=HIGH)
    x0, h1 = call(
        lambda *r: enter_kernel(*r, band=band),
        "enter",
        (NZ,),
        [smem(), wide, full((micro, width)), line] + steps_of(band, 128, 0, 1),
        (shape(rows, width), shape(rows, width, dtype=BF)),
        (wide, wide),
        [],
        2 * rows * width * width,
        1 << 22,
        co,
        agg,
        src,
        gain_one,
        *low,
    )
    c2, d2, r3, b4 = got = grid.begin([got, h1], (core, f2), (core, r2), (far, f3), (z1, p4))
    l4 = join(p4, b4)
    up = twice([f2, r2, c2, d2])
    qkv, probs, o, x1, h2 = call(
        lambda *r: attend_kernel(*r, band=band, scale=scale),
        "attend",
        (2 * NZ,),
        [smem(), smem(), wide, wide, line]
        + steps_of(3 * band, 128)
        + steps_of(band, 128, NZ, 3),
        (
            shape(rows, 3 * width, dtype=BF),
            shape(HEADS, micro, cap, cap),
            shape(rows, width, dtype=BF),
            shape(rows, width),
            shape(rows, width, dtype=BF),
        ),
        (full((rows, 3 * width)), full((HEADS, micro, cap, cap)), wide, wide, wide),
        [],
        8 * rows * width * width + 8 * rows * cap * width,
        1 << 24,
        co,
        lens,
        x0,
        h1,
        gain_two,
        *attn,
        *attn,
    )
    c3, d3, n4 = got = grid.begin([got, h2], (core, f3), (core, r3), (near, l4))
    f4 = join(l4, n4)
    down = twice([f3, r3, c3, d3])
    act, slope = call(
        lambda *r: up_kernel(*r, band=band, w=w),
        "up",
        (NZ,),
        [smem(), wide] + steps_of(band, w),
        (shape(rows, ff, dtype=BF), shape(rows, ff, dtype=BF)),
        (full((rows, ff)), full((rows, ff))),
        [],
        2 * rows * width * ff,
        1 << 24,
        co,
        h2,
        *up,
    )
    act = grid.gate(act, [n4])
    (r4,) = grid.begin([act], (far, f4))
    wq_parts = [f4, r4, *grid.begin([], (core, f4), (core, r4))]
    loss_part, dx2, dx2_low, d_head, df = call(
        lambda *r: down_kernel(*r, band=band, w=w),
        "down",
        (2 * NZ,),
        [smem(), smem(), wide, full((rows, ff)), full((rows, ff)), full((ho, width)), full((rows, ho)), full((rows, ho))]
        + [pl.BlockSpec((1, band, w), lambda i, b=b: (b * NZ + i % NZ, 0, 0)) for b in range(2)] * 4,
        (
            shape(8, 128),
            shape(rows, width),
            shape(rows, width, dtype=BF),
            shape(ho, width),
            shape(rows, ff, dtype=BF),
        ),
        (full((8, 128)), wide, wide, full((ho, width)), full((rows, ff))),
        [pltpu.VMEM((rows, width), F32)],
        4 * rows * width * ff,
        1 << 25,
        co,
        count[None],
        x1,
        act,
        slope,
        head,
        aims,
        weighted,
        *down,
    )

    place = lambda height, wid: pl.BlockSpec((NZ, height, wid), lambda i: (i, 0, 0))

    turned = [pltpu.VMEM((width, rows), BF)]

    def sent(kernel, name, height, wid, flops, scratch, *args):
        out = shape(4 * NZ, height, wid, dtype=BF)
        return call(
            kernel,
            name,
            (NZ,),
            [smem()] + [full(a.shape) for a in args],
            (out, out),
            (place(height, wid),) * 2,
            scratch,
            flops,
            32 * height * wid * 2 + 4 * 1024 * 1024,
            co,
            *args,
        )

    def sent_pairs(kernel, name, height, flops, scratch, *args):
        out = shape(4, NZ, height, 128, dtype=BF)
        block = pl.BlockSpec((4, 1, height, 128), lambda k: (0, k, 0, 0))
        keep, send = call(
            kernel,
            name,
            (NZ,),
            [smem()] + [smem() if a.ndim == 1 else full(a.shape) for a in args],
            (out, out),
            (block, block),
            scratch,
            flops,
            32 * height * 128 * 2,
            co,
            *args,
        )
        return keep.reshape(4 * NZ, height, 128), send.reshape(4 * NZ, height, 128)

    dense_grad = lambda *r: grad_kernel(*r, band=band, w=w)
    flow = {}
    flow["down"] = sent(dense_grad, "down_grad", band, w, 2 * rows * width * ff, turned, dx2_low, act)
    df = grid.gate(df, [flow["down"]])
    flow["up"] = sent(dense_grad, "up_grad", band, w, 2 * rows * width * ff, turned, h2, df)
    far, near, core, z1, z2 = grid.far, grid.near, grid.core, grid.next_z, grid.far_z

    def plus(left, right):
        return (left.astype(F32) + right.astype(F32)).astype(BF)

    def quarters(kept, got):
        return [plus(kept[i * NZ : (i + 1) * NZ], got[i * NZ : (i + 1) * NZ]) for i in range(4)]

    def halves(kept, got):
        return plus(kept[:2], got[:2]), plus(kept[2:], got[2:])

    def ends(kept, got):
        return plus(kept[:1], got[:1]), plus(kept[1:], got[1:])

    (got,) = grid.begin([r4], (core, flow["down"][1]))
    dq = quarters(flow["down"][0], got)
    df = grid.gate(df, [flow["up"], dq])
    (f1d,) = grid.begin([dq, flow["up"]], (far, dq[3]))
    got = core(flow["up"][1])
    dx1, dx1_low, d_gain_two = call(
        lambda *r: up_back_kernel(*r, band=band, w=w),
        "up_back",
        (NZ,),
        [smem(), full((rows, ff)), wide, line, wide] + steps_of(band, w),
        (shape(rows, width), shape(rows, width, dtype=BF), one),
        (wide, wide, line),
        [pltpu.VMEM((rows, width), F32)],
        2 * rows * width * ff,
        1 << 24,
        co,
        df,
        x1,
        gain_two,
        dx2,
        *up,
    )
    uq = quarters(flow["up"][0], got)
    d_side = plus(dq[1], f1d)
    dx1_low = grid.gate(dx1_low, [f1d, uq])
    (f0d,) = grid.begin([f1d, uq, dx1], (far, dq[2]))
    dqkv = call(
        lambda *r: attend_back_kernel(*r, band=band, scale=scale),
        "attend_back",
        (NZ,),
        [smem(), wide, full((rows, 3 * width)), full((HEADS, micro, cap, cap))]
        + steps_of(band, 128, 0, 3),
        shape(rows, 3 * width, dtype=BF),
        full((rows, 3 * width)),
        [pltpu.VMEM((rows, width), F32), pltpu.VMEM((rows, width), BF)],
        2 * rows * width * width + 12 * rows * cap * width,
        1 << 22,
        co,
        dx1_low,
        qkv,
        probs,
        *attn,
    )
    d_line = plus(dq[0], f0d)
    dqkv = grid.gate(dqkv, [f0d, d_side])
    (f1u,) = grid.begin([f0d, dqkv], (far, uq[3]))
    flow["attn"] = sent_pairs(
        lambda *r: attention_grad_kernel(*r, band=band),
        "attention_grad",
        4 * band,
        8 * rows * width * width,
        turned * 2,
        h1,
        o,
        dqkv,
        dx1_low,
    )
    u_side = plus(uq[1], f1u)
    dqkv = grid.gate(dqkv, [f1u, flow["attn"]])
    f0u, nd = grid.begin([f1u, flow["attn"]], (far, uq[2]), (near, d_side))
    got = core(grid.gate(flow["attn"][1], f1u))
    dx0_low, d_gain_one, dx0_sum, dagg = call(
        lambda *r: leave_kernel(*r, band=band),
        "leave",
        (2 * NZ,),
        [smem(), wide, full((rows, 3 * width)), wide, line]
        + steps_of(3 * band, 128)
        + steps_of(band, 128, NZ, 1),
        (
            shape(rows, width, dtype=BF),
            one,
            shape(micro, width),
            shape(rows, width, dtype=BF),
        ),
        (wide, line, full((micro, width)), wide),
        [pltpu.VMEM((rows, width), F32)],
        8 * rows * width * width,
        1 << 23,
        co,
        dx1,
        dqkv,
        x0,
        gain_one,
        *attn,
        *low,
    )
    u_line = plus(uq[0], f0u)
    d_half = halves(d_line, nd)
    dagg = grid.gate(dagg, [f0u, nd])
    nu, z1d = grid.begin([f0u, nd, dagg], (near, u_side), (z1, d_half[1]))
    g_rows, s_rows = call(
        pool_back_kernel,
        "pool_back",
        (HEADS // 4,),
        [
            full((rows, n)),
            full((n, 128)),
            pl.BlockSpec((n, 256), lambda j: (0, j)),
            pl.BlockSpec((4, rows, n), lambda j: (j, 0, 0)),
            pl.BlockSpec((4, rows, 128), lambda j: (j, 0, 0)),
            pair,
        ],
        (shape(n, width), shape(HEADS // 4, 4, n)),
        (pl.BlockSpec((n, 256), lambda j: (0, j)), pl.BlockSpec((1, 4, n), lambda j: (j, 0, 0))),
        [],
        14 * HEADS * rows * n * 128,
        1 << 23,
        spread,
        var_of,
        tv,
        fold,
        pa,
        dagg,
    )
    aq = quarters(flow["attn"][0], got)
    u_half = halves(u_line, nu)
    d_end = ends(d_half[0], z1d)
    dx0_low = grid.gate(dx0_low, [g_rows, nu, z1d])
    f1a, z1u = grid.begin([nu, z1d, g_rows], (far, aq[3]), (z1, u_half[1]))
    flow["low"] = sent_pairs(
        lambda *r: low_grad_kernel(*r, band=band, tall=tall, top=src_at - (n - 16)),
        "low_grad",
        band + tall + head_rows,
        2 * rows * width * width,
        [*turned, pltpu.VMEM((n, width), BF)],
        groups[:, 0, 0],
        agg,
        dx0_low,
        g_rows,
        dx0_sum,
        jnp.concatenate([d_gain_one, d_gain_two], axis=0),
        d_head,
    )
    a_side = plus(aq[1], f1a)
    u_end = ends(u_half[0], z1u)
    lk, ls = flow["low"]
    f0a, z2d, z2u, got = grid.begin(
        [f1a, z1u, lk], (far, aq[2]), (z2, d_end[1]), (z2, u_end[1]), (core, ls)
    )
    lq = [plus(lk[: 2 * NZ], got[: 2 * NZ]), plus(lk[2 * NZ :], got[2 * NZ :])]
    fl = far(lq[1])
    down_sum = (d_end[0].astype(F32) + z2d.astype(F32))[0]
    up_sum = (u_end[0].astype(F32) + z2u.astype(F32))[0]
    a_line = plus(aq[0], f0a)
    l_side, l_line = plus(lq[0][NZ:], fl[NZ:]), plus(lq[0][:NZ], fl[:NZ])
    nl, na = grid.begin([f0a, z2d, z2u, fl], (near, l_side), (near, a_side))
    l_half = halves(l_line, nl)
    z1l = z1(l_half[1])
    a_half, l_end = halves(a_line, na), ends(l_half[0], z1l)
    s_sum = grid.hop(grid.gate(s_rows.reshape(HEADS, n), [f0a, z2d, z2u, fl]), ("c", 1), ("z", 1), ("z", 2))
    wq_parts = grid.gate(wq_parts, fl)
    wq, wk = call(
        lambda *r: square_kernel(*r, band=band),
        "squares",
        (NZ,),
        [smem()] + steps_of(2 * band, 128),
        (shape(width, width, dtype=BF),) * 2,
        (full((width, width)),) * 2,
        [],
        0,
        1 << 20,
        co,
        *twice(wq_parts),
    )
    z2l, z1a = grid.begin([na, z1l, s_sum, wq, wk], (z2, l_end[1]), (z1, a_half[1]))
    s_sum = grid.hop(grid.gate(s_sum, z2l), ("x", 1), ("y", 1))
    a_end = ends(a_half[0], z1a)
    (z2a,) = grid.begin([z1a], (z2, a_end[1]))
    low_sum, attn_sum = (
        (kept[0].astype(F32) + got.astype(F32))[0] for kept, got in ((l_end, z2l), (a_end, z2a))
    )
    u_heads = (jnp.arange(width)[:, None] // size == jnp.arange(HEADS)[None]).astype(F32)
    du = dot(table.astype(F32), s_sum, ((0,), (1,)), precision=HIGH)
    du_cols = dot(lax.dynamic_slice_in_dim(du, my_band * band, band), head_mask, NT, precision=HIGH)
    dqv_heads = dot(du, wk.astype(F32), TN, precision=HIGH) * scale
    dqv_all = jnp.sum(dqv_heads * u_heads.T, axis=0)
    dqv = lax.dynamic_slice_in_dim(dqv_all, my_strip * strip, strip)
    dq_own = jnp.sum(
        lax.dynamic_slice_in_dim(wq, my_strip * strip, strip, 0).astype(F32) * dqv_all[None], axis=1
    )
    table_own = lax.dynamic_slice_in_dim(table, my_band * band, band, 1)
    g_own = low_sum[band : band + tall]
    g_low = grid.gate(g_own.astype(BF), z1a)
    g_column = grid.collect(grid.collect(g_low, "c"), "y").reshape(n, strip)
    g_line = grid.collect(grid.collect(g_low, "x"), "z").reshape(STRIPS, tall, strip)
    g_line = jnp.transpose(g_line, (1, 0, 2)).reshape(tall, width)
    wa_sum = low_sum[:band]
    head_sum = low_sum[band + tall :].reshape(2, ho // STRIPS, strip)
    head_sum = jnp.transpose(head_sum, (1, 0, 2)).reshape(ho // STRIPS, band).T

    row_of = np.full((n,), base + SOURCES + 3)
    for row in range(base + SOURCES + 3):
        row_of[lane_of(row)] = row
    row_of = jnp.asarray(row_of)
    g_column = jnp.where((row_of < base)[:, None], g_column, 0.0).astype(BF)
    value_sum = dot(table_own, g_column, TN)
    key_sum = du_cols * qv_own.astype(F32)[None] * scale
    query_sum = query_own.astype(F32)[:, None] * dqv[None]
    s_own = lax.dynamic_slice_in_dim(s_sum, my_band * tall, tall, 1)
    wv_rows = lax.dynamic_slice_in_dim(wv, my_strip * strip, strip, 0)
    u_rows = lax.dynamic_slice_in_dim(u, my_strip * strip, strip, 0).astype(F32)
    d_rows = dot(g_line, wv_rows, NT) + dot(s_own, u_rows, ((0,), (1,)), precision=HIGH)
    own_row = lax.dynamic_slice_in_dim(row_of, my_band * tall, tall)[:, None]
    table_sum = jnp.where(own_row < base, d_rows, g_own)
    table_sum = jnp.where(own_row == base + SOURCES, dq_own[None], table_sum)[:table_band]
    square_sums = (query_sum, key_sum, value_sum, wa_sum, attn_sum)
    sumsq = sum(jnp.sum(s * s) for s in (*square_sums, up_sum, down_sum, head_sum, table_sum))
    both = grid.rounds(jnp.stack([loss_part[0, 0], sumsq]), AXES)
    loss = both[0] / count
    grad_norm = jnp.sqrt(both[1])
    factor = jnp.minimum(1.0, CLIP_AT / grad_norm)
    steps = step_count[0].astype(F32)
    square_sum = jnp.concatenate([s.reshape(-1, band, strip) for s in square_sums], axis=0)
    dense_sum = jnp.stack([up_sum, down_sum])
    sq = adam_update(square_master, square_first, square_second, square_sum, factor, steps, LEARN_RATE)
    de = adam_update(dense_master, dense_first, dense_second, dense_sum, factor, steps, LEARN_RATE)
    hd = adam_update(head_master, head_first, head_second, head_sum, factor, steps, LEARN_RATE)
    tb = adam_update(table_master, table_first, table_second, table_sum, factor, steps, TABLE_RATE)
    return (loss, grad_norm, *sq, *de, *hd, *tb)


def solution(mesh):
    grid = Grid(mesh)
    var, patch = ("y", "c"), ("z", "x")
    item = P(None, var, patch)
    weight = P(None, var, patch)
    flat = P(var, patch)
    in_specs = (
        P(None, None, patch, None, var),
        item,
        item,
        item,
        item,
        item,
        P(),
        *(weight,) * 6,
        *(flat,) * 6,
    )
    out_specs = (P(), P(), *(weight,) * 8, *(flat,) * 8)

    def step(*args):
        return (fast_body if grid.fast else body)(grid, *args)

    return jax.shard_map(step, mesh=grid.mesh, in_specs=in_specs, out_specs=out_specs, check_vma=False)
```

```python
import math

import jax
import jax.numpy as jnp
import numpy as np
from jax import lax
from jax.experimental import pallas as pl
from jax.experimental.pallas import tpu as pltpu
from jax.sharding import Mesh
from jax.sharding import PartitionSpec as P

HEADS = 16
V = 48
PATCH_PIXELS = 4
SOURCES = 5
LATS = 64
PAD = 8

HIGH = lax.Precision.HIGHEST
CLIP_AT = 0.01
LEARN_RATE = 0.01
TABLE_RATE = 0.3
WEIGHT_DECAY = 0.1
FIRST_DECAY = 0.5
SECOND_DECAY = 0.5
EPSILON = 1e-08
NORM_EPSILON = 1e-05
AXES = ("y", "c", "z", "x")
BF = jnp.bfloat16
F32 = jnp.float32


class Grid:
    def __init__(self, mesh):
        nv, npatch = mesh.shape["var"], mesh.shape["patch"]
        self.sizes = {"y": nv // 2, "c": 2, "z": npatch // 2, "x": 2}
        self.mesh = Mesh(mesh.devices.reshape(tuple(self.sizes.values())), AXES)
        self.nv, self.np = nv, npatch
        self.fast = self.sizes["y"] == 2 and self.sizes["z"] == 4

    def flat(self, move):
        s = [self.sizes[a] for a in AXES]
        pairs = []
        for y in range(s[0]):
            for c in range(s[1]):
                for z in range(s[2]):
                    for x in range(s[3]):
                        ty, tc, tz, tx = move(y, c, z, x)
                        src = ((y * s[1] + c) * s[2] + z) * s[3] + x
                        dst = ((ty * s[1] + tc) * s[2] + tz) * s[3] + tx
                        pairs.append((src, dst))
        return pairs

    def permute(self, value, move):
        return lax.ppermute(value, AXES, self.flat(move))

    def swap(self, value, axis, bit=1):
        return lax.ppermute(value, axis, [(i, i ^ bit) for i in range(self.sizes[axis])])

    def total(self, value, axes=AXES):
        for axis in axes:
            bit = 1
            while bit < self.sizes[axis]:
                value = jax.tree.map(lambda v: v + self.swap(v, axis, bit), value)
                bit *= 2
        return value

    def spread(self, value, axes):
        count = math.prod(self.sizes[a] for a in axes)
        held = jnp.zeros((count,) + value.shape, value.dtype)
        held = lax.dynamic_update_index_in_dim(held, value, lax.axis_index(axes), 0)
        return self.total(held, axes)

    def along(self, first):
        def move(y, c, z, x):
            if (c == 0) == first:
                return (y ^ 1, c, z, x)
            return (y, c, z, x ^ 1)

        return move

    def gather(self, piece):
        return lax.all_gather(piece, AXES).reshape(self.nv, self.np, *piece.shape)

    def scatter(self, parts):
        nv, npatch, rows, w = parts.shape
        flat = parts.reshape(nv * npatch * rows, w)
        return lax.psum_scatter(flat, AXES, scatter_dimension=0, tiled=True).astype(F32)

    def gate(self, values, before):
        empty = isinstance(before, list) and not before
        return values if empty else lax.optimization_barrier((values, before))[0]

    def hop(self, value, *steps):
        for axis, bit in steps:
            value = value + self.swap(value, axis, bit)
        return value

    def rounds(self, value, axes):
        if "c" in axes:
            value = value + self.swap(value, "c")
        if "y" in axes:
            both = self.permute(value, lambda y, c, z, x: (y ^ 1, c, z, x ^ 1))
            value = (value + self.swap(value, "x")) + (self.swap(value, "y") + both)
        elif "x" in axes:
            value = value + self.swap(value, "x")
        if "z" in axes:
            third = self.swap(value, "z", 3)
            value = (value + self.swap(value, "z", 1)) + (self.swap(value, "z", 2) + third)
        return value

    def collect(self, value, axis):
        count = self.sizes[axis]
        here = lax.axis_index(axis)
        got = [value] + [self.swap(value, axis, flip) for flip in range(1, count)]
        out = []
        for place in range(count):
            piece = got[count - 1]
            for flip in range(count - 1):
                piece = jnp.where((here ^ flip) == place, got[flip], piece)
            out.append(piece)
        return jnp.stack(out)

    def begin(self, before, *moves):
        operands = self.gate([v for _, v in moves], before)
        return [fn(v) for (fn, _), v in zip(moves, operands)]

    def far_z(self, piece):
        return self.swap(piece, "z", 2)

    def next_z(self, pair):
        return self.swap(pair, "z", 1)

    def near(self, line):
        return self.permute(line, self.along(False))

    def far(self, both):
        return self.permute(both, self.along(True))

    def core(self, value):
        return self.swap(value, "c")


def whole(chunks):
    nv, npatch, rows, w = chunks.shape
    return jnp.transpose(chunks, (0, 2, 1, 3)).reshape(nv * rows, npatch * w)


def chunked(value, nv, npatch):
    r, c = value.shape
    return jnp.transpose(value.reshape(nv, r // nv, npatch, c // npatch), (0, 2, 1, 3))


def latitude_table():
    levels = jnp.arange(2 * LATS).astype(F32)
    cosine = jnp.cos(((levels + 0.5) / (2 * LATS) - 0.5) * math.pi)
    scaled = cosine / jnp.mean(cosine)
    index = 2 * jnp.arange(LATS)[:, None] + jnp.arange(PATCH_PIXELS)[None, :] // 2
    return scaled[index]


def layer_norm(value, gain):
    center = value - jnp.mean(value, axis=-1, keepdims=True)
    spread = jnp.mean(center * center, axis=-1, keepdims=True)
    return center * lax.rsqrt(spread + NORM_EPSILON) * gain


def exact_gelu(value):
    return jax.nn.gelu(value, approximate=False)


def adam_update(master, first, second, grad, factor, steps, rate):
    clipped = grad * factor
    new_first = FIRST_DECAY * first + (1.0 - FIRST_DECAY) * clipped
    new_second = SECOND_DECAY * second + (1.0 - SECOND_DECAY) * clipped * clipped
    first_hat = new_first / (1.0 - jnp.power(FIRST_DECAY, steps))
    second_hat = new_second / (1.0 - jnp.power(SECOND_DECAY, steps))
    new_master = master - rate * (
        first_hat / (jnp.sqrt(second_hat) + EPSILON) + WEIGHT_DECAY * master
    )
    return (new_master, new_first, new_second, new_master.astype(BF))


def dot(a, b, dims, batch=((), ()), precision=None):
    return lax.dot_general(
        a, b, (dims, batch), precision=precision, preferred_element_type=F32
    )


NN = ((1,), (0,))
NT = ((1,), (1,))
TN = ((0,), (0,))


def body(
    grid,
    pixels,
    targets,
    masks,
    lengths,
    groups,
    latitudes,
    step_count,
    square_master,
    square_first,
    square_second,
    dense_master,
    dense_first,
    dense_second,
    head_master,
    head_first,
    head_second,
    table_master,
    table_first,
    table_second,
):
    nv, npatch = grid.nv, grid.np
    micro, items, _, cap, own_pixels = pixels.shape
    rows = micro * cap
    width = square_master.shape[1] * nv
    size = width // HEADS
    scale = size ** (-0.5)
    band, strip = square_master.shape[1:]
    ff_strip = dense_master.shape[2]
    ho = head_master.shape[1] * npatch
    base = 5 * V + cap
    table_band = table_master.shape[0]
    table_pad = -table_band % PAD
    my_band = lax.axis_index(("y", "c"))
    my_strip = lax.axis_index(("z", "x"))

    square_low = square_master.astype(BF)
    dense_low = dense_master.astype(BF)
    head_low = head_master.astype(BF)
    table_low = table_master.astype(BF)
    first = jnp.concatenate(
        [
            jnp.pad(table_low, ((0, table_pad), (0, 0))),
            square_low[2],
            square_low[3],
        ],
        axis=0,
    )
    first = grid.gather(first)
    table = whole(first[:, :, :table_band])
    start = table_band + table_pad
    wv = whole(first[:, :, start : start + band])
    wa = whole(first[:, :, start + band : start + 2 * band])
    second = grid.gather(square_low[4:8].reshape(4 * band, strip))
    wqkv = jnp.concatenate(
        [whole(second[:, :, k * band : (k + 1) * band]) for k in range(3)], axis=1
    )
    wo = whole(second[:, :, 3 * band :])
    w1 = whole(grid.gather(dense_low[0]))
    w2 = whole(grid.gather(dense_low[1]))
    head = whole(grid.gather(head_low))

    slots = jnp.arange(cap)
    lat_table = latitude_table()
    valid = masks[:, 0, 0].astype(F32) * (slots[None] < lengths[:, 0, 0][:, None]).astype(F32)[..., None]
    lat_onehot = (latitudes[:, 0, 0][..., None] == jnp.arange(LATS)).astype(F32)
    wpix = jnp.einsum("mcl,lk->mck", lat_onehot, lat_table, precision=HIGH) * valid
    weighted = jnp.tile(wpix.reshape(rows, PATCH_PIXELS), (1, V))
    count = grid.total(jnp.sum(valid))

    parts = pixels[:, :, 0]
    mine = lax.all_to_all(parts, ("y", "c"), split_axis=1, concat_axis=3, tiled=True)[:, 0]
    pix = jnp.transpose(mine.reshape(rows, V, PATCH_PIXELS), (0, 2, 1)).astype(F32)

    query = table[base + SOURCES]
    query_own = lax.dynamic_slice_in_dim(query, my_band * band, band)
    qv = dot(query_own[None], square_low[0], NN)[0]
    qv_own = grid.total(qv, ("y", "c")).astype(BF)
    col_head = (my_strip * strip + jnp.arange(strip)) // size
    head_mask = (col_head[:, None] == jnp.arange(HEADS)[None]).astype(F32)
    u_part = dot(square_low[1].astype(F32) * qv_own.astype(F32)[None], head_mask, NN, precision=HIGH)
    u_band = (grid.total(u_part, ("z", "x")) * scale).astype(BF)
    u = grid.spread(u_band, ("y", "c")).reshape(width, HEADS)
    rows_t = jnp.concatenate(
        [
            jnp.transpose(table[: PATCH_PIXELS * V].reshape(V, PATCH_PIXELS, width), (1, 0, 2)).reshape(-1, width),
            table[PATCH_PIXELS * V : base],
        ],
        axis=0,
    )
    tv = dot(rows_t, wv, NN)
    tu = dot(rows_t, u, NN)
    nk = PATCH_PIXELS * V
    n5 = nk + V
    scores = (
        jnp.einsum("ckv,kvh->chv", pix, tu[:nk].reshape(PATCH_PIXELS, V, HEADS), precision=HIGH)
        + tu[nk:n5].T[None]
        + jnp.tile(tu[n5:], (micro, 1))[:, :, None]
    )
    pa = jax.nn.softmax(scores, axis=-1)
    pal = pa.astype(BF).astype(F32)
    mass = jnp.sum(pal, axis=-1)
    fold = jnp.concatenate(
        [(pal[:, :, None] * pix[:, None]).reshape(rows, HEADS, nk), pal], axis=2
    )
    tv_heads = tv.reshape(-1, HEADS, size)
    pos_v = jnp.tile(tv_heads[n5:], (micro, 1, 1))
    agg = (
        jnp.einsum("chn,nhe->che", fold, tv_heads[:n5], precision=HIGH)
        + mass[:, :, None] * pos_v
    )
    gathered = agg.reshape(rows, width).astype(BF)

    gain_one = table[base + SOURCES + 1].astype(F32)
    gain_two = table[base + SOURCES + 2].astype(F32)
    onehot = (groups[:, 0, 0][:, None] == jnp.arange(SOURCES)).astype(F32)
    src = jnp.dot(onehot, table[base : base + SOURCES].astype(F32), precision=HIGH)
    x0 = dot(gathered, wa, NN) + jnp.repeat(src, cap, axis=0)
    h1 = layer_norm(x0, gain_one).astype(BF)
    qkv = dot(h1, wqkv, NN).astype(BF)
    q, k, vv = (
        qkv[:, i * width : (i + 1) * width].reshape(micro, cap, HEADS, size) for i in range(3)
    )
    keymask = slots[None] < lengths[:, 0, 0][:, None]
    raw = jnp.einsum("mqhe,mkhe->mhqk", q, k, preferred_element_type=F32) * scale
    probs = jax.nn.softmax(jnp.where(keymask[:, None, None], raw, -1e30), axis=-1)
    probs_low = probs.astype(BF)
    o = jnp.einsum("mhqk,mkhe->mqhe", probs_low, vv, preferred_element_type=F32)
    o = o.reshape(rows, width).astype(BF)
    x1 = x0 + dot(o, wo, NN)
    h2 = layer_norm(x1, gain_two).astype(BF)
    f = dot(h2, w1, NN)
    act = exact_gelu(f).astype(BF)
    x2 = x1 + dot(act, w2, NT)
    x2_low = x2.astype(BF)
    pred = dot(x2_low, head, NN)
    diff = pred - targets[:, 0, 0].astype(F32).reshape(rows, ho)
    loss_local = jnp.sum(weighted * diff * diff)
    dpred = (2.0 * weighted * diff / count).astype(BF)

    d_head = dot(x2_low, dpred, TN)
    dx2 = dot(dpred, head, NT)
    dx2_low = dx2.astype(BF)
    d_down = dot(dx2_low, act, TN)
    dact = dot(dx2_low, w2, NN)
    _, gelu_back = jax.vjp(exact_gelu, f)
    df = gelu_back(dact)[0].astype(BF)
    d_up = dot(h2, df, TN)
    dh2 = dot(df, w1, NT)
    _, norm_back = jax.vjp(layer_norm, x1, gain_two)
    dx1n, d_gain_two = norm_back(dh2)
    dx1 = dx2 + dx1n
    dx1_low = dx1.astype(BF)
    d_wo = dot(o, dx1_low, TN)
    do = dot(dx1_low, wo, NT).astype(BF).reshape(micro, cap, HEADS, size)
    dprobs = jnp.einsum("mqhe,mkhe->mhqk", do, vv, preferred_element_type=F32)
    dvv = jnp.einsum("mhqk,mqhe->mkhe", probs_low, do, preferred_element_type=F32)
    ds = (probs * (dprobs - jnp.sum(probs * dprobs, axis=-1, keepdims=True))).astype(BF)
    dq = jnp.einsum("mhqk,mkhe->mqhe", ds, k, preferred_element_type=F32) * scale
    dk = jnp.einsum("mhqk,mqhe->mkhe", ds, q, preferred_element_type=F32) * scale
    dqkv = jnp.concatenate([t.reshape(rows, width) for t in (dq, dk, dvv)], axis=1).astype(BF)
    d_wqkv = dot(h1, dqkv, TN)
    dh1 = dot(dqkv, wqkv, NT)
    _, norm_back = jax.vjp(layer_norm, x0, gain_one)
    dx0n, d_gain_one = norm_back(dh1)
    dx0 = dx1 + dx0n
    d_src = jnp.dot(onehot.T, jnp.sum(dx0.reshape(micro, cap, width), axis=1), precision=HIGH)
    dx0_low = dx0.astype(BF)
    d_wa = dot(gathered, dx0_low, TN)
    dagg = dot(dx0_low, wa, NT).astype(BF).astype(F32).reshape(rows, HEADS, size)

    dfold = jnp.einsum("che,nhe->chn", dagg, tv_heads[:n5], precision=HIGH)
    dpal = (
        jnp.sum(dfold[:, :, :nk].reshape(rows, HEADS, PATCH_PIXELS, V) * pix[:, None], axis=2)
        + dfold[:, :, nk:]
        + jnp.sum(dagg * pos_v, axis=-1)[:, :, None]
    )
    dsv = (pa * (dpal - jnp.sum(pa * dpal, axis=-1, keepdims=True))).astype(BF).astype(F32)
    g_rows = jnp.einsum("chn,che->nhe", fold, dagg, precision=HIGH).reshape(n5, width)
    g_pos = jnp.sum((mass[:, :, None] * dagg).reshape(micro, cap, width), axis=0)
    s_rows = jnp.concatenate(
        [
            jnp.einsum("ckv,chv->kvh", pix, dsv, precision=HIGH).reshape(nk, HEADS),
            jnp.sum(dsv, axis=0).T,
            jnp.sum(jnp.sum(dsv, axis=-1).reshape(micro, cap, HEADS), axis=0),
        ],
        axis=0,
    )
    g_table = jnp.concatenate(
        [
            jnp.transpose(g_rows[:nk].reshape(PATCH_PIXELS, V, width), (1, 0, 2)).reshape(nk, width),
            g_rows[nk:],
            g_pos,
            d_src,
            jnp.zeros((1, width), F32),
            d_gain_one[None],
            d_gain_two[None],
        ],
        axis=0,
    )
    s_table = jnp.concatenate(
        [
            jnp.transpose(s_rows[:nk].reshape(PATCH_PIXELS, V, HEADS), (1, 0, 2)).reshape(nk, HEADS),
            s_rows[nk:],
        ],
        axis=0,
    )

    def to_owner(value):
        return grid.scatter(chunked(value.astype(BF), nv, npatch))

    down_sum = to_owner(d_down)
    up_sum = to_owner(d_up)
    s_sum = grid.total(s_table)
    low_part = jnp.concatenate(
        [
            jnp.pad(chunked(g_table.astype(BF), nv, npatch), ((0, 0), (0, 0), (0, table_pad), (0, 0))),
            chunked(d_wa.astype(BF), nv, npatch),
        ],
        axis=2,
    )
    low_sum = grid.scatter(low_part)
    g_own = low_sum[:table_band]
    wa_sum = low_sum[table_band + table_pad :]
    attn_sum = grid.scatter(
        jnp.concatenate(
            [chunked(d_wqkv[:, i * width : (i + 1) * width].astype(BF), nv, npatch) for i in range(3)]
            + [chunked(d_wo.astype(BF), nv, npatch)],
            axis=2,
        )
    )
    head_sum = to_owner(d_head)

    g_low = g_own.astype(BF)
    g_column = grid.spread(g_low, ("y", "c")).reshape(nv * table_band, strip)[:base]
    g_line = jnp.transpose(grid.spread(g_low, ("z", "x")), (1, 0, 2)).reshape(table_band, width)
    table_own_band = lax.dynamic_slice_in_dim(table, my_band * band, band, 1)
    value_sum = dot(table_own_band[:base], g_column, TN)
    du_own = dot(table_own_band[:base].astype(F32), s_sum, TN, precision=HIGH)
    du_cols = dot(du_own, head_mask, NT, precision=HIGH)
    key_sum = du_cols * qv_own.astype(F32)[None] * scale
    dqv = grid.total(jnp.sum(square_low[1].astype(F32) * du_cols, axis=0) * scale, ("y", "c"))
    query_sum = query_own.astype(F32)[:, None] * dqv[None]
    dquery = jnp.sum(square_low[0].astype(F32) * dqv[None], axis=1)
    dquery = lax.dynamic_update_slice_in_dim(jnp.zeros((width,), F32), dquery, my_band * band, 0)
    dquery = grid.total(dquery)
    table_row = my_band * table_band + jnp.arange(table_band)
    s_pad = jnp.pad(s_sum, ((0, nv * table_band - base), (0, 0)))
    s_own = lax.dynamic_slice_in_dim(s_pad, my_band * table_band, table_band, 0)
    wv_rows = lax.dynamic_slice_in_dim(wv, my_strip * strip, strip, 0)
    u_rows = lax.dynamic_slice_in_dim(u, my_strip * strip, strip, 0)
    d_rows = dot(g_line, wv_rows, NT) + dot(s_own, u_rows.astype(F32), NT, precision=HIGH)
    dq_own = lax.dynamic_slice_in_dim(dquery, my_strip * strip, strip, 0)
    table_sum = jnp.where((table_row < base)[:, None], d_rows, g_own)
    table_sum = jnp.where((table_row == base + SOURCES)[:, None], dq_own[None], table_sum)
    square_sum = jnp.concatenate(
        [query_sum[None], key_sum[None], value_sum[None], wa_sum[None], attn_sum.reshape(4, band, strip)],
        axis=0,
    )
    dense_sum = jnp.stack([up_sum, down_sum])
    shards = (square_sum, dense_sum, head_sum, table_sum)
    sumsq = sum(jnp.sum(s * s) for s in shards)
    both = grid.total(jnp.stack([loss_local, sumsq]))
    loss = both[0] / count
    norm = jnp.sqrt(both[1])
    factor = jnp.minimum(1.0, CLIP_AT / norm)
    steps = step_count[0].astype(F32)
    sq = adam_update(square_master, square_first, square_second, shards[0], factor, steps, LEARN_RATE)
    de = adam_update(dense_master, dense_first, dense_second, shards[1], factor, steps, LEARN_RATE)
    hd = adam_update(head_master, head_first, head_second, shards[2], factor, steps, LEARN_RATE)
    tb = adam_update(table_master, table_first, table_second, shards[3], factor, steps, TABLE_RATE)
    return (loss, norm, *sq, *de, *hd, *tb)


NZ = 4
BANDS = 4
STRIPS = 8
NT_DIMS = (((1,), (1,)), ((), ()))
NN_DIMS = (((1,), (0,)), ((), ()))
TN_DIMS = (((0,), (0,)), ((), ()))
VMEM_LIMIT = 56 * 1024 * 1024


def mm(a, b):
    return lax.dot_general(a, b, NN_DIMS, preferred_element_type=F32)


def mm_nt(a, b):
    return lax.dot_general(a, b, NT_DIMS, preferred_element_type=F32)


def mm_tn(a, b):
    return lax.dot_general(a, b, TN_DIMS, preferred_element_type=F32)


def zflip(k):
    return (k % 2) * 2 + k // 2


def span(index, extent):
    return pl.ds(pl.multiple_of(index * extent, extent), extent)


def spots(core):
    out = []
    for owner in (core, 1 - core):
        for a in range(2):
            for b in range(2):
                out.append((a, b, owner) if owner == 0 else (b, a, owner))
    return out


def by_core(co, fn):
    for core in range(2):

        @pl.when(co[1] == core)
        def _(core=core):
            fn(core)


def forward_step(co, k, x_ref, chunks, row, band, w, put):
    back = co[2] ^ zflip(k)

    def run(core):
        places = spots(core)
        for fx in range(2):
            total = None
            for index, (fy, px, owner) in enumerate(places):
                if px != fx:
                    continue
                r = (co[0] ^ fy) * 2 + owner
                part = mm(x_ref[:, span(r, band)], chunks[index][0, row : row + band])
                total = part if total is None else total + part
            put(back * 2 + (co[3] ^ fx), total)

    by_core(co, run)


def backward_step(co, k, dy_ref, chunks, row, band, w, acc_ref, fresh):
    back = co[2] ^ zflip(k)

    def run(core):
        places = spots(core)
        for owner in range(2):
            for fy in range(2):
                total = None
                for index, (py, fx, who) in enumerate(places):
                    if (py, who) != (fy, owner):
                        continue
                    p = back * 2 + (co[3] ^ fx)
                    part = mm_nt(dy_ref[:, span(p, w)], chunks[index][0, row : row + band])
                    total = part if total is None else total + part
                r = (co[0] ^ fy) * 2 + owner

                @pl.when(fresh)
                def _():
                    acc_ref[:, span(r, band)] = total

                @pl.when(jnp.logical_not(fresh))
                def _():
                    acc_ref[:, span(r, band)] += total

    by_core(co, run)


def by_place(co, fn):
    for core in range(2):
        for x in range(2):

            @pl.when((co[1] == core) & (co[3] == x))
            def _(core=core, x=x):
                fn(core, x)


def pair_of(chunks, core, x, flip_y, owner, rows):
    found = [None, None]
    for index, (fy, fx, who) in enumerate(spots(core)):
        if (fy, who) == (flip_y, owner):
            found[fx ^ x] = chunks[index][0, rows]
    return jnp.concatenate(found, axis=1)


def forward_pair(co, k, x_ref, chunks, row, band, put):
    back = co[2] ^ zflip(k)

    def run(core, x):
        total = None
        for owner in range(2):
            for fy in range(2):
                r = (co[0] ^ fy) * 2 + owner
                w = pair_of(chunks, core, x, fy, owner, slice(row, row + band))
                part = mm(x_ref[:, span(r, band)], w)
                total = part if total is None else total + part
        put(back, total)

    by_place(co, run)


def backward_pair(co, k, dy_ref, chunks, parts, band, acc_ref, fresh):
    back = co[2] ^ zflip(k)
    width = dy_ref.shape[1] // parts

    def run(core, x):
        for owner in range(2):
            for fy in range(2):
                total = None
                for part in range(parts):
                    w = pair_of(chunks, core, x, fy, owner, slice(part * band, (part + 1) * band))
                    col = pl.multiple_of(part * width + back * 256, 256)
                    got = mm_nt(dy_ref[:, pl.ds(col, 256)], w)
                    total = got if total is None else total + got
                r = (co[0] ^ fy) * 2 + owner

                @pl.when(fresh)
                def _():
                    acc_ref[:, span(r, band)] = total

                @pl.when(jnp.logical_not(fresh))
                def _():
                    acc_ref[:, span(r, band)] += total

    by_place(co, run)


def smem():
    return pl.BlockSpec(memory_space=pltpu.SMEM)


def full(shape):
    zeros = (0,) * len(shape)
    return pl.BlockSpec(shape, lambda i: zeros)


def steps_of(rows, w, first=0, block=0):
    def at(b):
        return pl.BlockSpec(
            (1, rows, w), lambda i: (b * NZ + jnp.clip(i - first, 0, NZ - 1), block, 0)
        )

    return [at(0), at(1)] * 4


def twice(arrays):
    return [v for v in arrays for _ in range(2)]


def call(kernel, name, grid, in_specs, outs, out_specs, scratch, flops, moved, *args):
    return pl.pallas_call(
        kernel,
        name=name,
        grid=grid,
        in_specs=in_specs,
        out_shape=outs,
        out_specs=out_specs,
        scratch_shapes=scratch,
        compiler_params=pltpu.CompilerParams(
            vmem_limit_bytes=VMEM_LIMIT
        ),
        cost_estimate=pl.CostEstimate(flops=flops, bytes_accessed=moved, transcendentals=0),
    )(*args)


def shape(*dims, dtype=F32):
    return jax.ShapeDtypeStruct(dims, dtype)


def norm(value, gain):
    center = value - jnp.mean(value, axis=-1, keepdims=True)
    spread = jnp.mean(center * center, axis=-1, keepdims=True)
    return center * lax.rsqrt(spread + NORM_EPSILON) * gain


def norm_grad(value, gain, grad):
    center = value - jnp.mean(value, axis=-1, keepdims=True)
    spread = jnp.mean(center * center, axis=-1, keepdims=True)
    inverse = lax.rsqrt(spread + NORM_EPSILON)
    unit = center * inverse
    inner = grad * gain
    out = inverse * (
        inner
        - jnp.mean(inner, axis=-1, keepdims=True)
        - unit * jnp.mean(inner * unit, axis=-1, keepdims=True)
    )
    return out, jnp.sum(grad * unit, axis=0, keepdims=True)


def half_masks(rows):
    lane = lax.broadcasted_iota(jnp.int32, (rows, 128), 1)
    return [(lane < 64).astype(BF), (lane >= 64).astype(BF)]


def assemble_kernel(co, *refs, band, offset, tall, extra):
    chunks, (table_ref, more_ref, value_ref) = refs[:8], refs[8:]
    k = pl.program_id(0)
    back = co[2] ^ zflip(k)

    def run(core):
        for index, (fy, fx, owner) in enumerate(spots(core)):
            r = (co[0] ^ fy) * 2 + owner
            p = back * 2 + (co[3] ^ fx)
            table_ref[span(r, tall), span(p, 128)] = chunks[index][0, offset : offset + tall]
            more = chunks[index][0, offset + tall : offset + tall + extra].astype(F32)
            half = extra // 2
            for part in range(2):
                col = pl.multiple_of(r * band + part * 128, 128)
                more_ref[span(p, half), pl.ds(col, 128)] = more[part * half : (part + 1) * half]
            value_ref[span(r, band), span(p, 128)] = chunks[index][0, :band]

    by_core(co, run)


def square_kernel(co, *refs, band):
    chunks, outs = refs[:8], refs[8:]
    k = pl.program_id(0)

    def run(core):
        for index, (fy, fx, owner) in enumerate(spots(core)):
            r = (co[0] ^ fy) * 2 + owner
            p = (co[2] ^ zflip(k)) * 2 + (co[3] ^ fx)
            for part, out_ref in enumerate(outs):
                out_ref[span(r, band), span(p, 128)] = chunks[index][0, part * band : (part + 1) * band]

    by_core(co, run)


def product_kernel(co, x_ref, *refs, band):
    chunks, out_ref = refs[:8], refs[8]

    def put(p, total):
        out_ref[:, span(p, 256)] = total.astype(out_ref.dtype)

    forward_pair(co, pl.program_id(0), x_ref, chunks, 0, band, put)


def pool_kernel(x_ref, e_ref, tu_ref, tv_ref, agg_ref, a_ref, pa_ref):
    j = pl.program_id(0)
    x, e = x_ref[...], e_ref[...]
    wide_x, wide_e = x.astype(F32), e.astype(F32)
    rows, n = x.shape
    masks = half_masks(n)
    lane = lax.broadcasted_iota(jnp.int32, (n, 128), 1)
    keep = lax.broadcasted_iota(jnp.int32, (rows, 128), 1) < V
    for pair in range(2):
        total = None
        for half in range(2):
            head = 2 * pair + half
            column = jnp.sum(jnp.where(lane == 4 * j + head, tu_ref[...], 0.0), axis=1, keepdims=True)
            m = wide_e * column
            high = m.astype(BF)
            rest = (m - high.astype(F32)).astype(BF)
            s = mm(x, high) + mm(x, rest)
            s = jnp.where(keep, s, -1e30)
            s = jnp.exp(s - jnp.max(s, axis=-1, keepdims=True))
            pa = s * (1.0 / jnp.sum(s, axis=-1, keepdims=True))
            wide = mm_nt(pa.astype(BF), e)
            a = (wide_x * wide).astype(BF)
            pa_ref[head] = pa
            a_ref[head] = a
            part = mm(a, tv_ref[:, pair * 128 : (pair + 1) * 128] * masks[half])
            total = part if total is None else total + part
        agg_ref[:, pair * 128 : (pair + 1) * 128] = total.astype(BF)


def enter_kernel(co, agg_ref, src_ref, gain_ref, *refs, band):
    chunks, (x0_ref, h1_ref) = refs[:8], refs[8:]
    k = pl.program_id(0)

    def put(p, total):
        x0_ref[:, span(p, 256)] = total

    forward_pair(co, k, agg_ref, chunks, 0, band, put)

    @pl.when(k == NZ - 1)
    def _():
        cap = x0_ref.shape[0] // src_ref.shape[0]
        for m in range(src_ref.shape[0]):
            x0_ref[m * cap : (m + 1) * cap] += src_ref[m : m + 1]
        h1_ref[...] = norm(x0_ref[...], gain_ref[...]).astype(BF)


def attend_kernel(co, lens, x0_ref, h1_ref, gain_ref, *refs, band, scale):
    qkv_chunks, o_chunks = refs[:8], refs[8:16]
    qkv_ref, p_ref, o_ref, x1_ref, h2_ref = refs[16:]
    i = pl.program_id(0)
    micro = lens.shape[0]
    width = x0_ref.shape[1]
    cap = x0_ref.shape[0] // micro

    @pl.when(i < NZ)
    def _():
        for part in range(3):

            def put(p, total, part=part):
                col = pl.multiple_of(part * width + p * 256, 256)
                qkv_ref[:, pl.ds(col, 256)] = total.astype(BF)

            forward_pair(co, i, h1_ref, qkv_chunks, part * band, band, put)

    @pl.when(i == NZ - 1)
    def _():
        masks = half_masks(cap)
        key = lax.broadcasted_iota(jnp.int32, (cap, cap), 1)

        @pl.loop(0, width // 128, unroll=4)
        def _(j):
            for m in range(micro):
                rows = slice(m * cap, (m + 1) * cap)
                q = qkv_ref[rows, span(j, 128)]
                kk = qkv_ref[rows, pl.ds(pl.multiple_of(width + j * 128, 128), 128)]
                vv = qkv_ref[rows, pl.ds(pl.multiple_of(2 * width + j * 128, 128), 128)]
                total = None
                for half in range(2):
                    s = mm_nt(q * masks[half], kk) * scale
                    s = jnp.where(key < lens[m], s, -1e30)
                    s = jnp.exp(s - jnp.max(s, axis=-1, keepdims=True))
                    p = s * (1.0 / jnp.sum(s, axis=-1, keepdims=True))
                    p_ref[2 * j + half, m] = p
                    part = mm(p.astype(BF), vv * masks[half])
                    total = part if total is None else total + part
                o_ref[rows, span(j, 128)] = total.astype(BF)

    @pl.when(i >= NZ)
    def _():
        def put(p, total):
            x1_ref[:, span(p, 256)] = x0_ref[:, span(p, 256)] + total

        forward_pair(co, i - NZ, o_ref, o_chunks, 0, band, put)

    @pl.when(i == 2 * NZ - 1)
    def _():
        h2_ref[...] = norm(x1_ref[...], gain_ref[...]).astype(BF)


def up_kernel(co, h2_ref, *refs, band, w):
    chunks, (act_ref, slope_ref) = refs[:8], refs[8:]

    def put(p, f):
        bell = jnp.exp(-0.5 * f * f)
        t = 1.0 / (1.0 + (0.3275911 * 0.5**0.5) * jnp.abs(f))
        tail = t * (1.061405429 * 0.5)
        for term in (-1.453152027, 1.421413741, -0.284496736, 0.254829592):
            tail = t * (0.5 * term + tail)
        tail = tail * bell
        share = jnp.where(f < 0.0, tail, 1.0 - tail)
        act_ref[:, span(p, w)] = (f * share).astype(BF)
        slope_ref[:, span(p, w)] = (share + f * bell * ((2.0 * math.pi) ** -0.5)).astype(BF)

    forward_step(co, pl.program_id(0), h2_ref, chunks, 0, band, w, put)


def down_kernel(co, count, x1_ref, act_ref, slope_ref, head_ref, target_ref, weight_ref, *refs, band, w):
    chunks = refs[:8]
    loss_ref, dx2_ref, dx2_low_ref, dhead_ref, df_ref = refs[8:13]
    acc_ref = refs[13]
    i = pl.program_id(0)

    @pl.when(i < NZ)
    def _():
        backward_step(co, i, act_ref, chunks, 0, band, w, acc_ref, i == 0)

    @pl.when(i == NZ - 1)
    def _():
        x2 = (x1_ref[...] + acc_ref[...]).astype(BF)
        head = head_ref[...].astype(BF)
        diff = mm_nt(x2, head) - target_ref[...].astype(F32)
        weighted = weight_ref[...] * diff
        loss_ref[...] = jnp.broadcast_to(jnp.sum(weighted * diff), loss_ref.shape)
        dpred = (2.0 * weighted / count[0]).astype(BF)
        dhead_ref[...] = mm_tn(dpred, x2)
        dx2 = mm(dpred, head)
        dx2_ref[...] = dx2
        dx2_low_ref[...] = dx2.astype(BF)

    @pl.when(i >= NZ)
    def _():
        def put(p, dact):
            df_ref[:, span(p, w)] = (dact * slope_ref[:, span(p, w)].astype(F32)).astype(BF)

        forward_step(co, i - NZ, dx2_low_ref, chunks, 0, band, w, put)


def owner_place(co, i, owner):
    a, b, k = i // (2 * NZ), (i // NZ) % 2, i % NZ
    fy = jnp.where(owner == 0, a, b)
    fx = jnp.where(owner == 0, b, a)
    return (co[0] ^ fy) * 2 + owner, (co[2] ^ zflip(k)) * 2 + (co[3] ^ fx)


def targets(co, keep_ref, send_ref):
    return [
        (out, owner, j)
        for out, owner in ((keep_ref, co[1]), (send_ref, 1 - co[1]))
        for j in range(NZ)
    ]


def grad_kernel(co, x_ref, dy_ref, keep_ref, send_ref, xt_ref, *, band, w):
    i = pl.program_id(0)

    @pl.when(i == 0)
    def _():
        xt_ref[...] = x_ref[...].T

    for out_ref, owner, j in targets(co, keep_ref, send_ref):
        r, p = owner_place(co, i * NZ + j, owner)
        out_ref[j] = mm(xt_ref[span(r, band)], dy_ref[:, span(p, w)]).astype(BF)


def pair_places(co, k, keep_ref, send_ref):
    out = []
    for out_ref, owner in ((keep_ref, co[1]), (send_ref, 1 - co[1])):
        for fy in range(2):
            at = []
            for half in range(2):
                fx = co[3] ^ half
                at.append(jnp.where(owner == 0, fy * 2 + fx, fx * 2 + fy))
            out.append((out_ref, (co[0] ^ fy) * 2 + owner, co[2] ^ zflip(k), at))
    return out


def attention_grad_kernel(co, h1_ref, o_ref, dqkv_ref, dx1_ref, keep_ref, send_ref, ht_ref, ot_ref, *, band):
    k = pl.program_id(0)
    width = h1_ref.shape[1]

    @pl.when(k == 0)
    def _():
        ht_ref[...] = h1_ref[...].T
        ot_ref[...] = o_ref[...].T

    for out_ref, r, back, at in pair_places(co, k, keep_ref, send_ref):
        for part in range(4):
            if part < 3:
                col = pl.multiple_of(part * width + back * 256, 256)
                got = mm(ht_ref[span(r, band)], dqkv_ref[:, pl.ds(col, 256)])
            else:
                got = mm(ot_ref[span(r, band)], dx1_ref[:, span(back, 256)])
            for half in range(2):
                out_ref[at[half], 0, part * band : (part + 1) * band] = got[
                    :, half * 128 : (half + 1) * 128
                ].astype(BF)


def low_grad_kernel(
    co, groups, agg_ref, dx0_ref, g_ref, sum_ref, gain_ref, head_ref, keep_ref, send_ref, at_ref, gl_ref, *, band, tall, top
):
    k = pl.program_id(0)
    n = g_ref.shape[0]
    piece = head_ref.shape[0] // STRIPS

    @pl.when(k == 0)
    def _():
        at_ref[...] = agg_ref[...].T
        gl_ref[: n - 16] = g_ref[: n - 16].astype(BF)
        last = g_ref[n - 16 :]
        row = lax.broadcasted_iota(jnp.int32, last.shape, 0)
        for m in range(sum_ref.shape[0]):
            last += jnp.where(row == top + groups[m], sum_ref[m : m + 1], 0.0)
        for m in range(2):
            last += jnp.where(row == top + SOURCES + 1 + m, gain_ref[m : m + 1], 0.0)
        gl_ref[n - 16 :] = last.astype(BF)

    for out_ref, r, back, at in pair_places(co, k, keep_ref, send_ref):
        got = mm(at_ref[span(r, band)], dx0_ref[:, span(back, 256)])
        for half in range(2):
            p = back * 2 + half
            out_ref[at[half], 0, :band] = got[:, half * 128 : (half + 1) * 128].astype(BF)
            out_ref[at[half], 0, band : band + tall] = gl_ref[span(r, tall), span(p, 128)]
            head = [
                head_ref[span(p, piece), pl.ds(pl.multiple_of(r * band + part * 128, 128), 128)]
                for part in range(2)
            ]
            out_ref[at[half], 0, band + tall :] = jnp.concatenate(head, axis=0).astype(BF)


def up_back_kernel(co, df_ref, x1_ref, gain_ref, dx2_ref, *refs, band, w):
    chunks, (dx1_ref, dx1_low_ref, dgain_ref, acc_ref) = refs[:8], refs[8:]
    k = pl.program_id(0)
    backward_step(co, k, df_ref, chunks, 0, band, w, acc_ref, k == 0)

    @pl.when(k == NZ - 1)
    def _():
        out, dgain = norm_grad(x1_ref[...], gain_ref[...], acc_ref[...])
        dx1 = dx2_ref[...] + out
        dx1_ref[...] = dx1
        dx1_low_ref[...] = dx1.astype(BF)
        dgain_ref[...] = dgain


def attend_back_kernel(co, dx1_low_ref, qkv_ref, p_ref, *refs, band, scale):
    o_chunks = refs[:8]
    dqkv_ref, acc_ref, do_ref = refs[8:]
    i = pl.program_id(0)
    micro = p_ref.shape[1]
    width = dx1_low_ref.shape[1]
    cap = dx1_low_ref.shape[0] // micro

    @pl.when(i < NZ)
    def _():
        backward_pair(co, i, dx1_low_ref, o_chunks, 1, band, acc_ref, i == 0)

    @pl.when(i == NZ - 1)
    def _():
        do_ref[...] = acc_ref[...].astype(BF)
        masks = half_masks(cap)

        @pl.loop(0, width // 128, unroll=4)
        def _(j):
            for m in range(micro):
                rows = slice(m * cap, (m + 1) * cap)
                k_at = pl.ds(pl.multiple_of(width + j * 128, 128), 128)
                v_at = pl.ds(pl.multiple_of(2 * width + j * 128, 128), 128)
                q, kk, vv = qkv_ref[rows, span(j, 128)], qkv_ref[rows, k_at], qkv_ref[rows, v_at]
                do = do_ref[rows, span(j, 128)]
                dq = dk = dv = None
                for half in range(2):
                    p = p_ref[2 * j + half, m]
                    do_half = do * masks[half]
                    dp = mm_nt(do_half, vv)
                    moved = p * dp
                    ds = (moved - p * jnp.sum(moved, axis=-1, keepdims=True)).astype(BF)
                    parts = (
                        mm(ds, kk * masks[half]),
                        mm_tn(ds, q * masks[half]),
                        mm_tn(p.astype(BF), do_half),
                    )
                    if dq is None:
                        dq, dk, dv = parts
                    else:
                        dq, dk, dv = dq + parts[0], dk + parts[1], dv + parts[2]
                dqkv_ref[rows, span(j, 128)] = (dq * scale).astype(BF)
                dqkv_ref[rows, k_at] = (dk * scale).astype(BF)
                dqkv_ref[rows, v_at] = dv.astype(BF)


def leave_kernel(co, dx1_ref, dqkv_ref, x0_ref, gain_ref, *refs, band):
    qkv_chunks, a_chunks = refs[:8], refs[8:16]
    dx0_low_ref, dgain_ref, dsum_ref, dagg_ref, acc_ref = refs[16:]
    i = pl.program_id(0)
    micro = dsum_ref.shape[0]
    width = x0_ref.shape[1]
    cap = x0_ref.shape[0] // micro

    @pl.when(i < NZ)
    def _():
        backward_pair(co, i, dqkv_ref, qkv_chunks, 3, band, acc_ref, i == 0)

    @pl.when(i == NZ - 1)
    def _():
        out, dgain = norm_grad(x0_ref[...], gain_ref[...], acc_ref[...])
        dx0 = dx1_ref[...] + out
        dx0_low_ref[...] = dx0.astype(BF)
        dgain_ref[...] = dgain
        for m in range(micro):
            dsum_ref[m : m + 1] = jnp.sum(dx0[m * cap : (m + 1) * cap], axis=0, keepdims=True)

    @pl.when(i >= NZ)
    def _():
        backward_pair(co, i - NZ, dx0_low_ref, a_chunks, 1, band, acc_ref, i == NZ)

    @pl.when(i == 2 * NZ - 1)
    def _():
        dagg_ref[...] = acc_ref[...].astype(BF)


def pool_back_kernel(x_ref, e_ref, tv_ref, a_ref, pa_ref, dagg_ref, g_ref, s_ref):
    x, e = x_ref[...].astype(F32), e_ref[...]
    masks = half_masks(x.shape[0])
    for pair in range(2):
        at = slice(pair * 128, (pair + 1) * 128)
        total = None
        for half in range(2):
            head = 2 * pair + half
            part = dagg_ref[:, at] * masks[half]
            dpal = mm((mm_nt(part, tv_ref[:, at]) * x).astype(BF), e)
            pa = pa_ref[head]
            inner = pa * dpal
            ds = (inner - pa * jnp.sum(inner, axis=-1, keepdims=True)).astype(BF)
            s_ref[0, head : head + 1] = jnp.sum(mm_nt(ds, e) * x, axis=0, keepdims=True)
            got = mm_tn(a_ref[head], part)
            total = got if total is None else total + got
        g_ref[:, at] = total


def table_layout(cap, band, tall):
    n = BANDS * tall
    nk = PATCH_PIXELS * V
    select = np.zeros((nk, n), np.float32)
    fixed = np.zeros((cap, n), np.float32)
    var_of = np.zeros((n, 128), np.float32)
    for row in range(5 * V + cap):
        lane = (row // band) * tall + row % band
        if row < nk:
            select[row, lane] = 1.0
            var_of[lane, row // PATCH_PIXELS] = 1.0
        elif row < 5 * V:
            fixed[:, lane] = 1.0
            var_of[lane, row - nk] = 1.0
        else:
            fixed[row - 5 * V, lane] = 1.0
            var_of[lane, :V] = 1.0
    return select, fixed, var_of


def fast_body(
    grid,
    pixels,
    targets,
    masks,
    lengths,
    groups,
    latitudes,
    step_count,
    square_master,
    square_first,
    square_second,
    dense_master,
    dense_first,
    dense_second,
    head_master,
    head_first,
    head_second,
    table_master,
    table_first,
    table_second,
):
    micro, items, _, cap, own_pixels = pixels.shape
    rows = micro * cap
    band, strip = square_master.shape[1:]
    width = band * BANDS
    size = width // HEADS
    scale = size ** (-0.5)
    w = dense_master.shape[2]
    ff = w * STRIPS
    ho = head_master.shape[1] * STRIPS
    base = 5 * V + cap
    table_band = table_master.shape[0]
    tall = table_band + -table_band % 16
    n = BANDS * tall
    head_rows = head_master.size // strip
    y, c, z, x = (lax.axis_index(a) for a in AXES)
    co = jnp.stack([y, c, z, x]).astype(jnp.int32)
    my_band = y * 2 + c
    my_strip = z * 2 + x
    select, fixed, var_of = table_layout(cap, table_band, tall)

    def lane_of(row):
        return (row // table_band) * tall + row % table_band

    square_low = square_master.astype(BF)
    dense_low = dense_master.astype(BF)
    low_rows = 2 * band + tall + head_rows
    low = jnp.concatenate(
        [
            square_low[2],
            square_low[3],
            jnp.pad(table_master.astype(BF), ((0, tall - table_band), (0, 0))),
            jnp.transpose(
                head_master.astype(BF).T.reshape(ho // STRIPS, 2, strip), (1, 0, 2)
            ).reshape(head_rows, strip),
        ],
        axis=0,
    )
    attn = square_low[4:8].reshape(4 * band, strip)
    slots = jnp.arange(cap)
    lens = lengths[:, 0, 0]
    valid = masks[:, 0, 0].astype(F32) * (slots[None] < lens[:, None]).astype(F32)[..., None]
    lat_onehot = (latitudes[:, 0, 0][..., None] == jnp.arange(LATS)).astype(F32)
    wpix = jnp.einsum("mcl,lk->mck", lat_onehot, latitude_table(), precision=HIGH) * valid
    weighted = jnp.tile(wpix.reshape(rows, PATCH_PIXELS), (1, V))
    var_of = jnp.asarray(var_of, BF)
    query_row = base + SOURCES
    col_head = (my_strip * strip + jnp.arange(strip)) // size
    head_mask = (col_head[:, None] == jnp.arange(HEADS)[None]).astype(F32)
    wide, line, one = full((rows, width)), full((1, width)), shape(1, width)
    pair = pl.BlockSpec((rows, 256), lambda j: (0, j))
    src_at = lane_of(base)
    row = jnp.where(my_band == query_row // table_band, 1.0, 0.0) * table_master[query_row % table_band]
    first_pack = lax.dynamic_update_slice_in_dim(
        jnp.zeros((width,), F32), row.astype(BF).astype(F32), my_strip * strip, 0
    )
    first_pack = jnp.concatenate([first_pack, jnp.broadcast_to(jnp.sum(valid), (128,))])

    bundles = [low, attn, dense_low[0], dense_low[1], square_low[:2].reshape(2 * band, strip)]
    stack, join = lambda i, v: jnp.stack([bundles[i], v]), lambda a, b: jnp.concatenate([a, b], axis=0)
    z2, z1, near, far, core = grid.far_z, grid.next_z, grid.near, grid.far, grid.core
    (a0,) = grid.begin([], (z2, bundles[0]))
    first_pack = grid.hop(grid.gate(first_pack, [a0]), ("z", 1), ("z", 2))
    p0 = stack(0, a0)
    b0, a1 = got = grid.begin([a0, first_pack], (z1, p0), (z2, bundles[1]))
    l0, p1 = join(p0, b0), stack(1, a1)
    pack = grid.hop(first_pack, ("x", 1))
    pack = grid.hop(pack, ("y", 1), ("c", 1))
    query, count = pack[:width].astype(BF), pack[width]
    query_own = lax.dynamic_slice_in_dim(query, my_band * band, band)
    spread = jnp.tile(jnp.asarray(fixed), (micro, 1))
    for fy in range(2):
        for fc in range(2):
            other = (y ^ fy) * 2 + (c ^ fc)
            piece = lax.dynamic_index_in_dim(pixels[:, :, 0], other, 1, False)
            if fy or fc:
                piece = grid.permute(piece, lambda a, b, d, e, fy=fy, fc=fc: (a ^ fy, b ^ fc, d, e))
            pick = lax.dynamic_slice_in_dim(
                jnp.asarray(select, BF), other * own_pixels, own_pixels, 0
            )
            spread = spread + mm(piece.reshape(rows, own_pixels), pick)
    spread = spread.astype(BF)
    qv = dot(query_own[None], square_low[0], NN)[0]
    qv_own = grid.hop(qv, ("y", 1), ("c", 1)).astype(BF)
    u_part = dot(square_low[1].astype(F32) * qv_own.astype(F32)[None], head_mask, NN, precision=HIGH)
    u_part = lax.dynamic_update_slice_in_dim(jnp.zeros((width, HEADS), F32), u_part, my_band * band, 0)
    u_part = grid.hop(u_part, ("x", 1))
    n0, b1 = got = grid.begin([got, qv_own, spread], (near, l0), (z1, p1))
    f0, l1 = join(l0, n0), join(p1, b1)
    u_part = grid.hop(u_part, ("y", 1), ("c", 1), ("z", 1))
    r0, n1, a2 = got = grid.begin([got, u_part], (far, f0), (near, l1), (z2, bundles[2]))
    f1, p2 = join(l1, n1), stack(2, a2)
    (b2,) = grid.begin([], (z1, p2))
    l2 = join(p2, b2)
    c0, d0, r1, a3 = got = grid.begin(
        [got, b2, u_part], (core, f0), (core, r0), (far, f1), (z2, bundles[3])
    )
    p3 = stack(3, a3)
    u_part = grid.hop(u_part, ("z", 2))
    low = twice([f0, r0, c0, d0])
    n2, c1, d1, b3 = got = grid.begin(
        [got, u_part], (near, l2), (core, f1), (core, r1), (z1, p3)
    )
    f2, l3 = join(l2, n2), join(p3, b3)
    u = (u_part * scale).astype(BF)
    table, head, wv = call(
        lambda *r: assemble_kernel(*r, band=band, offset=2 * band, tall=tall, extra=head_rows),
        "assemble",
        (NZ,),
        [smem()] + steps_of(low_rows, 128),
        (
            shape(n, width, dtype=BF),
            shape(ho, width),
            shape(width, width, dtype=BF),
        ),
        (full((n, width)), full((ho, width)), full((width, width))),
        [],
        0,
        1 << 23,
        co,
        *low,
    )
    tv = call(
        lambda *r: product_kernel(*r, band=band),
        "table_values",
        (NZ,),
        [smem(), full((n, width))] + steps_of(band, 128),
        shape(n, width, dtype=BF),
        full((n, width)),
        [],
        2 * n * width * width,
        1 << 22,
        co,
        table,
        *low,
    )
    tu = jnp.pad(dot(table, u, NN), ((0, 0), (0, 128 - HEADS)))
    attn = twice([f1, r1, c1, d1])
    r2, n3, a4 = got = grid.begin([got, u, tv], (far, f2), (near, l3), (z2, bundles[4]))
    f3, p4 = join(l3, n3), stack(4, a4)
    aims = targets[:, 0, 0].reshape(rows, ho)
    tu, weighted, aims = grid.gate((tu, weighted, aims), [n2])
    tu = grid.gate(tu, [weighted, aims])
    agg, fold, pa = call(
        pool_kernel,
        "pool",
        (HEADS // 4,),
        [full((rows, n)), full((n, 128)), full((n, 128)), pl.BlockSpec((n, 256), lambda j: (0, j))],
        (shape(rows, width, dtype=BF), shape(HEADS, rows, n, dtype=BF), shape(HEADS, rows, 128)),
        (
            pair,
            pl.BlockSpec((4, rows, n), lambda j: (j, 0, 0)),
            pl.BlockSpec((4, rows, 128), lambda j: (j, 0, 0)),
        ),
        [],
        12 * HEADS * rows * n * 128,
        1 << 23,
        spread,
        var_of,
        tu,
        tv,
    )

    gain_one = table[lane_of(base + SOURCES + 1)].astype(F32)[None]
    gain_two = table[lane_of(base + SOURCES + 2)].astype(F32)[None]
    onehot = (groups[:, 0, 0][:, None] == jnp.arange(SOURCES)).astype(F32)
    src = dot(onehot, table[src_at : src_at + SOURCES].astype(F32), NN, precision=HIGH)
    x0, h1 = call(
        lambda *r: enter_kernel(*r, band=band),
        "enter",
        (NZ,),
        [smem(), wide, full((micro, width)), line] + steps_of(band, 128, 0, 1),
        (shape(rows, width), shape(rows, width, dtype=BF)),
        (wide, wide),
        [],
        2 * rows * width * width,
        1 << 22,
        co,
        agg,
        src,
        gain_one,
        *low,
    )
    c2, d2, r3, b4 = got = grid.begin([got, h1], (core, f2), (core, r2), (far, f3), (z1, p4))
    l4 = join(p4, b4)
    up = twice([f2, r2, c2, d2])
    qkv, probs, o, x1, h2 = call(
        lambda *r: attend_kernel(*r, band=band, scale=scale),
        "attend",
        (2 * NZ,),
        [smem(), smem(), wide, wide, line]
        + steps_of(3 * band, 128)
        + steps_of(band, 128, NZ, 3),
        (
            shape(rows, 3 * width, dtype=BF),
            shape(HEADS, micro, cap, cap),
            shape(rows, width, dtype=BF),
            shape(rows, width),
            shape(rows, width, dtype=BF),
        ),
        (full((rows, 3 * width)), full((HEADS, micro, cap, cap)), wide, wide, wide),
        [],
        8 * rows * width * width + 8 * rows * cap * width,
        1 << 24,
        co,
        lens,
        x0,
        h1,
        gain_two,
        *attn,
        *attn,
    )
    c3, d3, n4 = got = grid.begin([got, h2], (core, f3), (core, r3), (near, l4))
    f4 = join(l4, n4)
    down = twice([f3, r3, c3, d3])
    act, slope = call(
        lambda *r: up_kernel(*r, band=band, w=w),
        "up",
        (NZ,),
        [smem(), wide] + steps_of(band, w),
        (shape(rows, ff, dtype=BF), shape(rows, ff, dtype=BF)),
        (full((rows, ff)), full((rows, ff))),
        [],
        2 * rows * width * ff,
        1 << 24,
        co,
        h2,
        *up,
    )
    act = grid.gate(act, [n4])
    (r4,) = grid.begin([act], (far, f4))
    wq_parts = [f4, r4, *grid.begin([], (core, f4), (core, r4))]
    loss_part, dx2, dx2_low, d_head, df = call(
        lambda *r: down_kernel(*r, band=band, w=w),
        "down",
        (2 * NZ,),
        [smem(), smem(), wide, full((rows, ff)), full((rows, ff)), full((ho, width)), full((rows, ho)), full((rows, ho))]
        + [pl.BlockSpec((1, band, w), lambda i, b=b: (b * NZ + i % NZ, 0, 0)) for b in range(2)] * 4,
        (
            shape(8, 128),
            shape(rows, width),
            shape(rows, width, dtype=BF),
            shape(ho, width),
            shape(rows, ff, dtype=BF),
        ),
        (full((8, 128)), wide, wide, full((ho, width)), full((rows, ff))),
        [pltpu.VMEM((rows, width), F32)],
        4 * rows * width * ff,
        1 << 25,
        co,
        count[None],
        x1,
        act,
        slope,
        head,
        aims,
        weighted,
        *down,
    )

    place = lambda height, wid: pl.BlockSpec((NZ, height, wid), lambda i: (i, 0, 0))

    turned = [pltpu.VMEM((width, rows), BF)]

    def sent(kernel, name, height, wid, flops, scratch, *args):
        out = shape(4 * NZ, height, wid, dtype=BF)
        return call(
            kernel,
            name,
            (NZ,),
            [smem()] + [full(a.shape) for a in args],
            (out, out),
            (place(height, wid),) * 2,
            scratch,
            flops,
            32 * height * wid * 2 + 4 * 1024 * 1024,
            co,
            *args,
        )

    def sent_pairs(kernel, name, height, flops, scratch, *args):
        out = shape(4, NZ, height, 128, dtype=BF)
        block = pl.BlockSpec((4, 1, height, 128), lambda k: (0, k, 0, 0))
        keep, send = call(
            kernel,
            name,
            (NZ,),
            [smem()] + [smem() if a.ndim == 1 else full(a.shape) for a in args],
            (out, out),
            (block, block),
            scratch,
            flops,
            32 * height * 128 * 2,
            co,
            *args,
        )
        return keep.reshape(4 * NZ, height, 128), send.reshape(4 * NZ, height, 128)

    dense_grad = lambda *r: grad_kernel(*r, band=band, w=w)
    flow = {}
    flow["down"] = sent(dense_grad, "down_grad", band, w, 2 * rows * width * ff, turned, dx2_low, act)
    df = grid.gate(df, [flow["down"]])
    flow["up"] = sent(dense_grad, "up_grad", band, w, 2 * rows * width * ff, turned, h2, df)
    far, near, core, z1, z2 = grid.far, grid.near, grid.core, grid.next_z, grid.far_z

    def plus(left, right):
        return (left.astype(F32) + right.astype(F32)).astype(BF)

    def quarters(kept, got):
        return [plus(kept[i * NZ : (i + 1) * NZ], got[i * NZ : (i + 1) * NZ]) for i in range(4)]

    def halves(kept, got):
        return plus(kept[:2], got[:2]), plus(kept[2:], got[2:])

    def ends(kept, got):
        return plus(kept[:1], got[:1]), plus(kept[1:], got[1:])

    (got,) = grid.begin([r4], (core, flow["down"][1]))
    dq = quarters(flow["down"][0], got)
    df = grid.gate(df, [flow["up"], dq])
    (f1d,) = grid.begin([dq, flow["up"]], (far, dq[3]))
    got = core(flow["up"][1])
    dx1, dx1_low, d_gain_two = call(
        lambda *r: up_back_kernel(*r, band=band, w=w),
        "up_back",
        (NZ,),
        [smem(), full((rows, ff)), wide, line, wide] + steps_of(band, w),
        (shape(rows, width), shape(rows, width, dtype=BF), one),
        (wide, wide, line),
        [pltpu.VMEM((rows, width), F32)],
        2 * rows * width * ff,
        1 << 24,
        co,
        df,
        x1,
        gain_two,
        dx2,
        *up,
    )
    uq = quarters(flow["up"][0], got)
    d_side = plus(dq[1], f1d)
    dx1_low = grid.gate(dx1_low, [f1d, uq])
    (f0d,) = grid.begin([f1d, uq, dx1], (far, dq[2]))
    dqkv = call(
        lambda *r: attend_back_kernel(*r, band=band, scale=scale),
        "attend_back",
        (NZ,),
        [smem(), wide, full((rows, 3 * width)), full((HEADS, micro, cap, cap))]
        + steps_of(band, 128, 0, 3),
        shape(rows, 3 * width, dtype=BF),
        full((rows, 3 * width)),
        [pltpu.VMEM((rows, width), F32), pltpu.VMEM((rows, width), BF)],
        2 * rows * width * width + 12 * rows * cap * width,
        1 << 22,
        co,
        dx1_low,
        qkv,
        probs,
        *attn,
    )
    d_line = plus(dq[0], f0d)
    dqkv = grid.gate(dqkv, [f0d, d_side])
    (f1u,) = grid.begin([f0d, dqkv], (far, uq[3]))
    flow["attn"] = sent_pairs(
        lambda *r: attention_grad_kernel(*r, band=band),
        "attention_grad",
        4 * band,
        8 * rows * width * width,
        turned * 2,
        h1,
        o,
        dqkv,
        dx1_low,
    )
    u_side = plus(uq[1], f1u)
    dqkv = grid.gate(dqkv, [f1u, flow["attn"]])
    f0u, nd = grid.begin([f1u, flow["attn"]], (far, uq[2]), (near, d_side))
    got = core(grid.gate(flow["attn"][1], f1u))
    dx0_low, d_gain_one, dx0_sum, dagg = call(
        lambda *r: leave_kernel(*r, band=band),
        "leave",
        (2 * NZ,),
        [smem(), wide, full((rows, 3 * width)), wide, line]
        + steps_of(3 * band, 128)
        + steps_of(band, 128, NZ, 1),
        (
            shape(rows, width, dtype=BF),
            one,
            shape(micro, width),
            shape(rows, width, dtype=BF),
        ),
        (wide, line, full((micro, width)), wide),
        [pltpu.VMEM((rows, width), F32)],
        8 * rows * width * width,
        1 << 23,
        co,
        dx1,
        dqkv,
        x0,
        gain_one,
        *attn,
        *low,
    )
    u_line = plus(uq[0], f0u)
    d_half = halves(d_line, nd)
    dagg = grid.gate(dagg, [f0u, nd])
    nu, z1d = grid.begin([f0u, nd, dagg], (near, u_side), (z1, d_half[1]))
    g_rows, s_rows = call(
        pool_back_kernel,
        "pool_back",
        (HEADS // 4,),
        [
            full((rows, n)),
            full((n, 128)),
            pl.BlockSpec((n, 256), lambda j: (0, j)),
            pl.BlockSpec((4, rows, n), lambda j: (j, 0, 0)),
            pl.BlockSpec((4, rows, 128), lambda j: (j, 0, 0)),
            pair,
        ],
        (shape(n, width), shape(HEADS // 4, 4, n)),
        (pl.BlockSpec((n, 256), lambda j: (0, j)), pl.BlockSpec((1, 4, n), lambda j: (j, 0, 0))),
        [],
        14 * HEADS * rows * n * 128,
        1 << 23,
        spread,
        var_of,
        tv,
        fold,
        pa,
        dagg,
    )
    aq = quarters(flow["attn"][0], got)
    u_half = halves(u_line, nu)
    d_end = ends(d_half[0], z1d)
    dx0_low = grid.gate(dx0_low, [g_rows, nu, z1d])
    f1a, z1u = grid.begin([nu, z1d, g_rows], (far, aq[3]), (z1, u_half[1]))
    flow["low"] = sent_pairs(
        lambda *r: low_grad_kernel(*r, band=band, tall=tall, top=src_at - (n - 16)),
        "low_grad",
        band + tall + head_rows,
        2 * rows * width * width,
        [*turned, pltpu.VMEM((n, width), BF)],
        groups[:, 0, 0],
        agg,
        dx0_low,
        g_rows,
        dx0_sum,
        jnp.concatenate([d_gain_one, d_gain_two], axis=0),
        d_head,
    )
    a_side = plus(aq[1], f1a)
    u_end = ends(u_half[0], z1u)
    lk, ls = flow["low"]
    f0a, z2d, z2u, got = grid.begin(
        [f1a, z1u, lk], (far, aq[2]), (z2, d_end[1]), (z2, u_end[1]), (core, ls)
    )
    lq = [plus(lk[: 2 * NZ], got[: 2 * NZ]), plus(lk[2 * NZ :], got[2 * NZ :])]
    fl = far(lq[1])
    down_sum = (d_end[0].astype(F32) + z2d.astype(F32))[0]
    up_sum = (u_end[0].astype(F32) + z2u.astype(F32))[0]
    a_line = plus(aq[0], f0a)
    l_side, l_line = plus(lq[0][NZ:], fl[NZ:]), plus(lq[0][:NZ], fl[:NZ])
    nl, na = grid.begin([f0a, z2d, z2u, fl], (near, l_side), (near, a_side))
    l_half = halves(l_line, nl)
    z1l = z1(l_half[1])
    a_half, l_end = halves(a_line, na), ends(l_half[0], z1l)
    s_sum = grid.hop(grid.gate(s_rows.reshape(HEADS, n), [f0a, z2d, z2u, fl]), ("c", 1), ("z", 1), ("z", 2))
    wq_parts = grid.gate(wq_parts, fl)
    wq, wk = call(
        lambda *r: square_kernel(*r, band=band),
        "squares",
        (NZ,),
        [smem()] + steps_of(2 * band, 128),
        (shape(width, width, dtype=BF),) * 2,
        (full((width, width)),) * 2,
        [],
        0,
        1 << 20,
        co,
        *twice(wq_parts),
    )
    z2l, z1a = grid.begin([na, z1l, s_sum, wq, wk], (z2, l_end[1]), (z1, a_half[1]))
    s_sum = grid.rounds(grid.gate(s_sum, z2l), "yx")
    a_end = ends(a_half[0], z1a)
    (z2a,) = grid.begin([z1a], (z2, a_end[1]))
    low_sum, attn_sum = (
        (kept[0].astype(F32) + got.astype(F32))[0] for kept, got in ((l_end, z2l), (a_end, z2a))
    )
    u_heads = (jnp.arange(width)[:, None] // size == jnp.arange(HEADS)[None]).astype(F32)
    du = dot(table.astype(F32), s_sum, ((0,), (1,)), precision=HIGH)
    du_cols = dot(lax.dynamic_slice_in_dim(du, my_band * band, band), head_mask, NT, precision=HIGH)
    dqv_heads = dot(du, wk.astype(F32), TN, precision=HIGH) * scale
    dqv_all = jnp.sum(dqv_heads * u_heads.T, axis=0)
    dqv = lax.dynamic_slice_in_dim(dqv_all, my_strip * strip, strip)
    dq_own = jnp.sum(
        lax.dynamic_slice_in_dim(wq, my_strip * strip, strip, 0).astype(F32) * dqv_all[None], axis=1
    )
    table_own = lax.dynamic_slice_in_dim(table, my_band * band, band, 1)
    g_own = low_sum[band : band + tall]
    g_low = grid.gate(g_own.astype(BF), z1a)
    g_column = grid.collect(grid.collect(g_low, "c"), "y").reshape(n, strip)
    g_line = grid.collect(grid.collect(g_low, "x"), "z").reshape(STRIPS, tall, strip)
    g_line = jnp.transpose(g_line, (1, 0, 2)).reshape(tall, width)
    wa_sum = low_sum[:band]
    head_sum = low_sum[band + tall :].reshape(2, ho // STRIPS, strip)
    head_sum = jnp.transpose(head_sum, (1, 0, 2)).reshape(ho // STRIPS, band).T

    row_of = np.full((n,), base + SOURCES + 3)
    for row in range(base + SOURCES + 3):
        row_of[lane_of(row)] = row
    row_of = jnp.asarray(row_of)
    g_column = jnp.where((row_of < base)[:, None], g_column, 0.0).astype(BF)
    value_sum = dot(table_own, g_column, TN)
    key_sum = du_cols * qv_own.astype(F32)[None] * scale
    query_sum = query_own.astype(F32)[:, None] * dqv[None]
    s_own = lax.dynamic_slice_in_dim(s_sum, my_band * tall, tall, 1)
    wv_rows = lax.dynamic_slice_in_dim(wv, my_strip * strip, strip, 0)
    u_rows = lax.dynamic_slice_in_dim(u, my_strip * strip, strip, 0).astype(F32)
    d_rows = dot(g_line, wv_rows, NT) + dot(s_own, u_rows, ((0,), (1,)), precision=HIGH)
    own_row = lax.dynamic_slice_in_dim(row_of, my_band * tall, tall)[:, None]
    table_sum = jnp.where(own_row < base, d_rows, g_own)
    table_sum = jnp.where(own_row == base + SOURCES, dq_own[None], table_sum)[:table_band]
    square_sums = (query_sum, key_sum, value_sum, wa_sum, attn_sum)
    sumsq = sum(jnp.sum(s * s) for s in (*square_sums, up_sum, down_sum, head_sum, table_sum))
    both = grid.rounds(jnp.stack([loss_part[0, 0], sumsq]), AXES)
    loss = both[0] / count
    grad_norm = jnp.sqrt(both[1])
    factor = jnp.minimum(1.0, CLIP_AT / grad_norm)
    steps = step_count[0].astype(F32)
    square_sum = jnp.concatenate([s.reshape(-1, band, strip) for s in square_sums], axis=0)
    dense_sum = jnp.stack([up_sum, down_sum])
    sq = adam_update(square_master, square_first, square_second, square_sum, factor, steps, LEARN_RATE)
    de = adam_update(dense_master, dense_first, dense_second, dense_sum, factor, steps, LEARN_RATE)
    hd = adam_update(head_master, head_first, head_second, head_sum, factor, steps, LEARN_RATE)
    tb = adam_update(table_master, table_first, table_second, table_sum, factor, steps, TABLE_RATE)
    return (loss, grad_norm, *sq, *de, *hd, *tb)


def solution(mesh):
    grid = Grid(mesh)
    var, patch = ("y", "c"), ("z", "x")
    item = P(None, var, patch)
    weight = P(None, var, patch)
    flat = P(var, patch)
    in_specs = (
        P(None, None, patch, None, var),
        item,
        item,
        item,
        item,
        item,
        P(),
        *(weight,) * 6,
        *(flat,) * 6,
    )
    out_specs = (P(), P(), *(weight,) * 8, *(flat,) * 8)

    def step(*args):
        return (fast_body if grid.fast else body)(grid, *args)

    return jax.shard_map(step, mesh=grid.mesh, in_specs=in_specs, out_specs=out_specs, check_vma=False)
```
